32 devices in a mesh: groups: 2 (over y), dp: 4 (over z), blk: 2 (over x), mp: 2 (over core).
Axes of the slice: x: 2, y: 2, z: 4, core: 2. Of those that a mesh axis runs over, the one named last changes fastest.
Arguments:
- train_inputs: bfloat16 [16, 128, 8192], P(('groups', 'dp', 'blk'), None, 'mp'), parts along dimension 0, may hold values from -6 to 6
- train_cotangents: bfloat16 [16, 128, 8192], P(('groups', 'dp', 'blk'), None, 'mp'), parts along dimension 0, may hold values from -6 to 6
- train_lengths: int32 [16], P(('groups', 'dp', 'blk')), parts along dimension 0, may hold values from 32 to 128, as said below
- test_inputs: bfloat16 [16, 128, 8192], P(('groups', 'dp', 'blk'), None, 'mp'), parts along dimension 0, may hold values from -6 to 6
- test_cotangents: bfloat16 [16, 128, 8192], P(('groups', 'dp', 'blk'), None, 'mp'), parts along dimension 0, may hold values from -6 to 6
- test_lengths: int32 [16], P(('groups', 'dp', 'blk')), parts along dimension 0, may hold values from 32 to 128, as said below
- proj_in: bfloat16 [8192, 128], P('mp', 'dp')
- proj_out: bfloat16 [8192, 64], P('mp', 'dp')
Outputs:
- scores: float32 [16, 8], P(('groups', 'dp', 'blk')), parts along dimension 0
The draws below stay inside these ranges and needn't reach their ends.
There are 2 independent parts, one for each index of `groups`. The reference program is written for one: setup_inputs(seed, part) draws one part's arguments, and reference() takes and returns one part's arrays. A program takes and returns all parts, laid end to end along the dimension named above; an argument that names none is the same for every part. Nothing has to cross between parts.
Inputs may be any that keep to these rules, and one draw needn't show every extreme that they name: `train_lengths`: live tokens come first in an example; the first example has all 128. `test_lengths`: live tokens come first in an example; the first example has all 128.
All inputs are finite; a program needn't handle non-finite values.
Results may differ from the reference program's by a relative error of at most 0.0003.
Values may be sent and summed in bfloat16 or wider, within the bound.
No kernel may reach another device: no remote copies, remote signals or barrier semaphores. Data moves between devices by JAX's collectives and lax.ppermute only.
A program may use at most 64 MiB of HBM per device.

```python
import jax
import jax.numpy as jnp
from jax import lax

D = 8192
KI = 128
KO = 64
SEQ = 128
NTR = 8
NTE = 8


def draw_train_lengths(key, part):
    key = jax.random.fold_in(key, 1)
    values = jax.random.randint(key, (NTR,), SEQ // 4, SEQ + 1)
    return values.at[0].set(SEQ).astype(jnp.int32)


def draw_test_lengths(key, part):
    key = jax.random.fold_in(key, 2)
    values = jax.random.randint(key, (NTE,), SEQ // 4, SEQ + 1)
    return values.at[0].set(SEQ).astype(jnp.int32)


def projection_matrix(key, columns, shared_weight):
    base_key, shared_key, scale_key = jax.random.split(key, 3)
    base = jax.random.normal(base_key, (D, columns), jnp.float32)
    shared = jax.random.normal(shared_key, (D, 1), jnp.float32)
    spread = jnp.exp(jax.random.uniform(scale_key, (1, columns), jnp.float32, 0.0, 2.3))
    return ((base + shared_weight * shared) * spread / D ** 0.5).astype(jnp.bfloat16)


def draw_proj_in(key, part):
    key = jax.random.fold_in(key, 3)
    return projection_matrix(key, KI, 0.6)


def draw_proj_out(key, part):
    key = jax.random.fold_in(key, 4)
    return projection_matrix(key, KO, 0.6)


def shard_levels(key, extent, pieces, least, top_value):
    factor_of = 1.0
    for position, parts in pieces:
        steps = jax.random.uniform(jax.random.fold_in(jax.random.fold_in(key, 6), position), (parts,), jnp.float32, least / len(pieces), top_value / len(pieces))
        factor_of = factor_of * jnp.repeat(jnp.exp(steps), extent[position] // parts).reshape((-1,) + (1,) * (len(extent) - 1 - position))
    return factor_of


def normal_values(key, dims, scale, limit, cuts=(), kind=jnp.bfloat16):
    result = scale * jax.random.normal(key, dims, jnp.float32)
    if cuts:
        result = result * shard_levels(key, dims, cuts, -0.22, 0.18)
    return jnp.clip(result, -limit, limit).astype(kind)


def setup_inputs(seed: int = 0, part: int = 0) -> dict:
    key_list = jax.random.split(jax.random.key(seed), 9)
    part_splits = jax.random.split(jax.random.fold_in(key_list[8], part), 9)
    return {
        "train_inputs": normal_values(part_splits[0], (NTR, SEQ, D), 1.0, 6.0, ((0, 8), (2, 2))),
        "train_cotangents": normal_values(part_splits[1], (NTR, SEQ, D), 1.0, 6.0, ((0, 8), (2, 2))),
        "train_lengths": draw_train_lengths(jax.random.fold_in(jax.random.fold_in(key_list[8], part), 71), part),
        "test_inputs": normal_values(part_splits[3], (NTE, SEQ, D), 1.0, 6.0, ((0, 8), (2, 2))),
        "test_cotangents": normal_values(part_splits[4], (NTE, SEQ, D), 1.0, 6.0, ((0, 8), (2, 2))),
        "test_lengths": draw_test_lengths(jax.random.fold_in(jax.random.fold_in(key_list[8], part), 71), part),
        "proj_in": draw_proj_in(jax.random.fold_in(key_list[8], 71), part),
        "proj_out": draw_proj_out(jax.random.fold_in(key_list[8], 71), part),
    }


def project(inputs, weights):
    examples, seq_len, width = inputs.shape
    flat = inputs.reshape(examples * seq_len, width)
    return jnp.dot(flat.astype(jnp.float32), weights.astype(jnp.float32), preferred_element_type=jnp.float32).reshape(examples, seq_len, weights.shape[1])

def live_mask(lengths, seq_len):
    positions = lax.broadcasted_iota(jnp.int32, (lengths.shape[0], seq_len), 1)
    return (positions < lengths[:, None]).astype(jnp.float32)

def factor_total(projected, lengths):
    examples, seq_len, rank_dim = projected.shape
    live = live_mask(lengths, seq_len).reshape(examples * seq_len, 1)
    flat = projected.reshape(examples * seq_len, rank_dim)
    return jnp.dot((flat * live).T, flat, precision=lax.Precision.HIGHEST)

def inverse_factor(total, tokens_live):
    factor = total / tokens_live
    factor_order = factor.shape[0]
    identity = jnp.eye(factor_order, dtype=jnp.float32)
    damped = factor + 0.1 * jnp.trace(factor) / factor_order * identity
    lower = jnp.linalg.cholesky(damped)
    return jax.scipy.linalg.cho_solve((lower, True), identity)

def example_grads(inputs_proj, outputs_proj, lengths):
    seq_len = inputs_proj.shape[1]
    weighting = live_mask(lengths, seq_len) / lengths.astype(jnp.float32)[:, None]
    return jnp.einsum('nsk,nsl->nkl', inputs_proj * weighting[:, :, None], outputs_proj, precision=lax.Precision.HIGHEST)

def precondition(gradients, inv_in, inv_out):
    left = jnp.einsum('kj,njl->nkl', inv_in, gradients, precision=lax.Precision.HIGHEST)
    return jnp.einsum('nkl,lm->nkm', left, inv_out, precision=lax.Precision.HIGHEST)

def reference(train_inputs, train_cotangents, train_lengths, test_inputs, test_cotangents, test_lengths, proj_in, proj_out):
    xp_train = project(train_inputs, proj_in)
    gp_train = project(train_cotangents, proj_out)
    xp_test = project(test_inputs, proj_in)
    gp_test = project(test_cotangents, proj_out)
    tokens_live = jnp.sum(train_lengths.astype(jnp.float32))
    inv_in = inverse_factor(factor_total(xp_train, train_lengths), tokens_live)
    inv_out = inverse_factor(factor_total(gp_train, train_lengths), tokens_live)
    grad_train = example_grads(xp_train, gp_train, train_lengths)
    grad_test = precondition(example_grads(xp_test, gp_test, test_lengths), inv_in, inv_out)
    train_flat = grad_train.reshape(grad_train.shape[0], -1)
    test_flat = grad_test.reshape(grad_test.shape[0], -1)
    return jnp.dot(train_flat, test_flat.T, precision=lax.Precision.HIGHEST)
```

```python
import functools

import jax
import jax.numpy as jnp
from jax import lax
from jax.experimental import pallas as pl
from jax.experimental.pallas import tpu as pltpu
from jax.sharding import PartitionSpec as P

HI = lax.Precision.HIGHEST
NT = (((1,), (1,)), ((), ()))
TN = (((0,), (0,)), ((), ()))
PARAMS = pltpu.CompilerParams(vmem_limit_bytes=40 * 1024 * 1024)
NEWTON_STEPS = 8


def vmem():
    return pl.BlockSpec(memory_space=pltpu.VMEM)


def smem():
    return pl.BlockSpec(memory_space=pltpu.SMEM)


def swap(x, axis, count, k):
    return lax.ppermute(x, axis, [(i, i ^ k) for i in range(count)])


def write_projections(x_refs, w_in, w_out, out_ref):
    tokens = x_refs[0].shape[0]
    ko = w_out.shape[0]
    for n, ref in enumerate((x_refs[0], x_refs[2])):
        out_ref[n * tokens : (n + 1) * tokens, :] = lax.dot_general(
            ref[...], w_in, NT, preferred_element_type=jnp.float32
        )
    for n, ref in enumerate((x_refs[1], x_refs[3])):
        out_ref[2 * tokens : 3 * tokens, n * ko : (n + 1) * ko] = lax.dot_general(
            ref[...], w_out, NT, preferred_element_type=jnp.float32
        )


def project_kernel(*refs):
    x_refs, (w_in, w_out, out_ref) = refs[:4], refs[4:]
    write_projections(x_refs, w_in[...], w_out[...], out_ref)


def project_pieces_kernel(n_dp, n_xy, *refs):
    x_refs, (own_in, own_out) = refs[:4], refs[4:6]
    first = refs[6 : 5 + n_dp]
    rest = refs[5 + n_dp : 4 + n_dp + n_xy]
    out_ref, w_in, w_out = refs[4 + n_dp + n_xy :]
    z = lax.axis_index("dp")
    q = lax.axis_index(("groups", "blk"))
    rin, rout = own_in.shape[0], own_out.shape[0]
    width = first[0].shape[1]
    w_in[pl.ds(pl.multiple_of(z * rin, rin), rin), :] = own_in[...]
    w_out[pl.ds(pl.multiple_of(z * rout, rout), rout), :] = own_out[...]
    for j in range(n_xy):
        cols = pl.ds(pl.multiple_of((q ^ j) * width, width), width)
        for k in range(1, n_dp):
            src = z ^ k
            if j == 0:
                piece = first[k - 1][...]
            else:
                piece = rest[j - 1][(k - 1) * (rin + rout) : k * (rin + rout), :]
            w_in[pl.ds(pl.multiple_of(src * rin, rin), rin), cols] = piece[:rin]
            w_out[pl.ds(pl.multiple_of(src * rout, rout), rout), cols] = piece[rin:]
    write_projections(x_refs, w_in[...], w_out[...], out_ref)


def moments_kernel(len_tr, len_te, mine, other, fac_ref, gte_ref, gtr_ref):
    tokens = mine.shape[0] // 3
    ki = mine.shape[1]
    ko = ki // 2
    total = mine[...] + other[...]
    rows = lax.broadcasted_iota(jnp.int32, (tokens, ki), 0)
    n_tr, n_te = len_tr[0], len_te[0]
    x_tr = jnp.where(rows < n_tr, total[:tokens], 0.0)
    x_te = jnp.where(rows < n_te, total[tokens : 2 * tokens], 0.0)
    g_both = total[2 * tokens :]
    g_tr = jnp.where(rows < n_tr, g_both, 0.0)[:, :ko]
    g_te = g_both[:, ko:]
    dot = functools.partial(
        lax.dot_general, dimension_numbers=TN, precision=HI,
        preferred_element_type=jnp.float32,
    )
    c_in = dot(x_tr, x_tr)
    c_out = dot(g_tr, g_tr)
    half = ki // 2
    fac_ref[:half, :] = c_in[:half, :]
    fac_ref[half:ki, :half] = c_in[half:, half:]
    fac_ref[half:ki, half:] = c_out
    fac_ref[ki:, :] = jnp.full((8, ki), n_tr.astype(jnp.float32))
    grad_tr = dot(x_tr, g_tr) / n_tr.astype(jnp.float32)
    grad_te = dot(x_te, g_te) / n_te.astype(jnp.float32)
    gtr_ref[...] = grad_tr
    gte_ref[0, :, :ko] = grad_te[:half]
    gte_ref[0, :, ko:] = grad_te[half:]


def damped(c):
    n = c.shape[0]
    i = lax.broadcasted_iota(jnp.int32, (n, n), 0)
    j = lax.broadcasted_iota(jnp.int32, (n, n), 1)
    eye = (i == j).astype(jnp.float32)
    trace = jnp.sum(c * eye, axis=(0, 1), keepdims=True)
    low = 0.1 * trace / n
    a = c + low * eye
    high = jnp.max(jnp.sum(jnp.abs(a), axis=1, keepdims=True), axis=0, keepdims=True)
    return a, eye, low, jnp.minimum(high, trace + low)


def mm(a, b):
    return jnp.dot(a, b, precision=HI, preferred_element_type=jnp.float32)


def inverses(matrices):
    state = []
    for c in matrices:
        a, eye, low, high = damped(c)
        scale = 2.0 / (low + high)
        r = (high - low) / (high + low)
        state.append((a, eye, scale * a, scale * eye, r))
    for step in range(NEWTON_STEPS):
        nxt = []
        for a, eye, m, x, r in state:
            s = 2.0 / (2.0 - r * r)
            n = m.shape[0]
            if step == 0:
                mx = s * (2.0 * m - mm(m, m))
                xx = s * (2.0 * x - x[:1, :1] * m)
            else:
                both = mm(jnp.concatenate([m, x], axis=0), m)
                mx = s * (2.0 * m - both[:n])
                xx = s * (2.0 * x - both[n:])
            nxt.append((a, eye, mx, xx, r * r / (2.0 - r * r)))
        state = nxt
    return [2.0 * x - mm(x, mm(a, x)) for a, eye, m, x, r in state]


def scores_kernel(n_dp, n_blk, *refs):
    facs, grads = refs[:n_dp], refs[n_dp : 2 * n_dp]
    gtr_ref, out_ref = refs[2 * n_dp :]
    total = functools.reduce(jnp.add, [f[...] for f in facs])
    ki = total.shape[1]
    half = ki // 2
    top = total[:half, :]
    c_in = jnp.concatenate(
        [top, jnp.concatenate([top[:, half:].T, total[half:ki, :half]], axis=1)], axis=0
    )
    c_out = total[half:ki, half:]
    count = total[ki : ki + 1, :1]
    inv_in, inv_out = inverses([c_in, c_out])
    side = mm(mm(inv_in, gtr_ref[...]), inv_out) * (count * count)
    packed = jnp.concatenate([side[:half], side[half:]], axis=1)
    z = lax.axis_index("dp")
    b = lax.axis_index("blk")
    lane = lax.broadcasted_iota(jnp.int32, out_ref.shape, 1)
    row = jnp.zeros(out_ref.shape, jnp.float32)
    for k in range(n_dp):
        for l in range(n_blk):
            value = jnp.sum(packed * grads[k][l], axis=(0, 1), keepdims=True)
            row = jnp.where(lane == (z ^ k) * n_blk + (b ^ l), value, row)
    out_ref[...] = row


def per_device(
    n_groups, n_dp, n_blk, train_inputs, train_cotangents, train_lengths,
    test_inputs, test_cotangents, test_lengths, proj_in, proj_out,
):
    _, tokens, width = train_inputs.shape
    xs = [a.reshape(tokens, width) for a in (
        train_inputs, train_cotangents, test_inputs, test_cotangents)]
    w_in, w_out = proj_in.T, proj_out.T
    rin, rout = w_in.shape[0], w_out.shape[0]
    ki, ko = rin * n_dp, rout * n_dp
    n_xy = n_groups * n_blk
    proj_shape = jax.ShapeDtypeStruct((3 * tokens, ki), jnp.float32)
    if rin % 16 == 0 and rout % 16 == 0:
        piece_w = width // n_xy
        q = lax.axis_index(("groups", "blk"))
        mine = lax.dynamic_slice(
            jnp.concatenate([w_in, w_out], axis=0), (0, q * piece_w), (rin + rout, piece_w))
        first = [swap(mine, "dp", n_dp, k) for k in range(1, n_dp)]
        block = jnp.concatenate(first, axis=0)
        rest = [swap(block, ("groups", "blk"), n_xy, j) for j in range(1, n_xy)]
        args = (*xs, w_in, w_out, *first, *rest)
        part = pl.pallas_call(
            functools.partial(project_pieces_kernel, n_dp, n_xy),
            out_shape=proj_shape,
            in_specs=[vmem()] * len(args),
            out_specs=vmem(),
            scratch_shapes=[
                pltpu.VMEM((ki, width), jnp.bfloat16),
                pltpu.VMEM((ko, width), jnp.bfloat16),
            ],
            compiler_params=PARAMS,
        )(*args)
    else:
        w_in = lax.all_gather(w_in, "dp", axis=0, tiled=True)
        w_out = lax.all_gather(w_out, "dp", axis=0, tiled=True)
        part = pl.pallas_call(
            project_kernel,
            out_shape=proj_shape,
            in_specs=[vmem()] * 6,
            out_specs=vmem(),
            compiler_params=PARAMS,
        )(*xs, w_in, w_out)
    other = swap(part, "mp", 2, 1)
    fac, gte, gtr = pl.pallas_call(
        moments_kernel,
        out_shape=(
            jax.ShapeDtypeStruct((ki + 8, ki), jnp.float32),
            jax.ShapeDtypeStruct((1, ki // 2, 2 * ko), jnp.float32),
            jax.ShapeDtypeStruct((ki, ko), jnp.float32),
        ),
        in_specs=[smem(), smem(), vmem(), vmem()],
        out_specs=(vmem(), vmem(), vmem()),
        compiler_params=PARAMS,
    )(train_lengths, test_lengths, part, other)
    fac = functools.reduce(
        jnp.add, [fac] + [swap(fac, "blk", n_blk, l) for l in range(1, n_blk)])
    facs = [fac] + [swap(fac, "dp", n_dp, k) for k in range(1, n_dp)]
    gte = jnp.concatenate(
        [gte] + [swap(gte, "blk", n_blk, l) for l in range(1, n_blk)], axis=0)
    gtes = [gte] + [swap(gte, "dp", n_dp, k) for k in range(1, n_dp)]
    return pl.pallas_call(
        functools.partial(scores_kernel, n_dp, n_blk),
        out_shape=jax.ShapeDtypeStruct((1, n_dp * n_blk), jnp.float32),
        in_specs=[vmem()] * (2 * n_dp + 1),
        out_specs=vmem(),
        compiler_params=PARAMS,
    )(*facs, *gtes, gtr)


def solution(mesh):
    feature = P(("groups", "dp", "blk"), None, "mp")
    length = P(("groups", "dp", "blk"))
    weight = P("mp", "dp")
    shape = mesh.shape
    return jax.shard_map(
        functools.partial(per_device, shape["groups"], shape["dp"], shape["blk"]),
        mesh=mesh,
        in_specs=(feature, feature, length, feature, feature, length, weight, weight),
        out_specs=P(("groups", "dp", "blk"), None),
        check_vma=False,
    )
```

```python
import functools

import jax
import jax.numpy as jnp
from jax import lax
from jax.experimental import pallas as pl
from jax.experimental.pallas import tpu as pltpu
from jax.sharding import PartitionSpec as P

HI = lax.Precision.HIGHEST
NT = (((1,), (1,)), ((), ()))
TN = (((0,), (0,)), ((), ()))
NEWTON_STEPS = 7
PLANE = ("groups", "blk")


def vmem():
    return pl.BlockSpec(memory_space=pltpu.VMEM)


def smem():
    return pl.BlockSpec(memory_space=pltpu.SMEM)


def call(kernel, out_shape, in_specs, args, flops=0, **kw):
    return pl.pallas_call(
        kernel,
        out_shape=out_shape,
        in_specs=in_specs,
        out_specs=jax.tree.map(lambda _: vmem(), out_shape),
        compiler_params=pltpu.CompilerParams(vmem_limit_bytes=32 * 1024 * 1024),
        cost_estimate=pl.CostEstimate(flops=flops, bytes_accessed=4 << 20, transcendentals=0),
        **kw,
    )(*args)


def swap(x, axis, count, k):
    return lax.ppermute(x, axis, [(i, i ^ k) for i in range(count)])


def bits(count):
    return [1 << s for s in reversed(range(count.bit_length() - 1))]


def load_kernel(*refs):
    srcs, dsts, sem = refs[:4], refs[4:8], refs[8]
    copies = []
    for i, (src, dst) in enumerate(zip(srcs, dsts)):
        rows = src.shape[0] // 2
        for h in range(2):
            part = pl.ds(h * rows, rows)
            copies.append(pltpu.make_async_copy(src.at[part], dst.at[part], sem.at[2 * i + h]))
    for c in copies:
        c.start()
    for c in copies:
        c.wait()


def store_products(x_parts, g_parts, acc_ref, out_ref):
    tokens = out_ref.shape[0] // 3
    ko = g_parts[0].shape[1]
    for n in range(2):
        rows = slice(n * tokens, (n + 1) * tokens)
        prior = 0.0 if acc_ref is None else acc_ref[rows, :]
        out_ref[rows, :] = prior + x_parts[n]
    rows = slice(2 * tokens, 3 * tokens)
    for n in range(2):
        cols = slice(n * ko, (n + 1) * ko)
        prior = 0.0 if acc_ref is None else acc_ref[rows, cols]
        out_ref[rows, cols] = prior + g_parts[n]


def nt(a, b):
    return lax.dot_general(a, b, NT, preferred_element_type=jnp.float32)


def project_kernel(*refs):
    x_refs, (w_in, w_out, out_ref) = refs[:4], refs[4:]
    xs = [nt(x_refs[n][...], w_in[...]) for n in (0, 2)]
    gs = [nt(x_refs[n][...], w_out[...]) for n in (1, 3)]
    store_products(xs, gs, None, out_ref)


def project_pieces_kernel(plan, shifts, with_acc, n_pieces, *refs):
    x_refs, (own_in, own_out) = refs[:4], refs[4:6]
    pieces = refs[6 : 6 + n_pieces]
    acc_ref = refs[6 + n_pieces] if with_acc else None
    out_ref, w_in, w_out = refs[6 + n_pieces + with_acc :]
    z = lax.axis_index("dp")
    q = lax.axis_index(PLANE)
    rin, rout = own_in.shape[0], own_out.shape[0]
    width = pieces[0].shape[1]
    xs, gs = [0.0, 0.0], [0.0, 0.0]
    for n, (dq, half, p, row) in enumerate(plan):
        start = pl.multiple_of(((q ^ dq) * 2 + half) * width, width)
        cols = pl.ds(start, width)
        here = slice(n * width, (n + 1) * width)
        w_in[pl.ds(pl.multiple_of(z * rin, rin), rin), here] = own_in[:, cols]
        w_out[pl.ds(pl.multiple_of(z * rout, rout), rout), here] = own_out[:, cols]
        for i, k in enumerate(shifts):
            at = row + i * (rin + rout)
            dst_in = pl.multiple_of((z ^ k) * rin, rin)
            dst_out = pl.multiple_of((z ^ k) * rout, rout)
            w_in[pl.ds(dst_in, rin), here] = pieces[p][at : at + rin, :]
            w_out[pl.ds(dst_out, rout), here] = pieces[p][at + rin : at + rin + rout, :]
        for m in range(2):
            xs[m] += nt(x_refs[2 * m][:, cols], w_in[:, here])
            gs[m] += nt(x_refs[2 * m + 1][:, cols], w_out[:, here])
    store_products(xs, gs, acc_ref, out_ref)


def moments_kernel(len_tr, len_te, mine, other, fac_ref, gte_ref, gtr_ref):
    tokens = mine.shape[0] // 3
    ki = mine.shape[1]
    ko = ki // 2
    total = mine[...] + other[...]
    rows = lax.broadcasted_iota(jnp.int32, (tokens, ki), 0)
    n_tr, n_te = len_tr[0], len_te[0]
    x_tr = jnp.where(rows < n_tr, total[:tokens], 0.0)
    x_te = jnp.where(rows < n_te, total[tokens : 2 * tokens], 0.0)
    g_both = total[2 * tokens :]
    g_tr = jnp.where(rows < n_tr, g_both, 0.0)[:, :ko]
    g_te = g_both[:, ko:]
    dot = functools.partial(
        lax.dot_general, dimension_numbers=TN, precision=HI,
        preferred_element_type=jnp.float32,
    )
    c_in = dot(x_tr, x_tr)
    c_out = dot(g_tr, g_tr)
    half = ki // 2
    fac_ref[:half, :] = c_in[:half, :]
    fac_ref[half:ki, :half] = c_in[half:, half:]
    fac_ref[half:ki, half:] = c_out
    fac_ref[ki:, :] = jnp.full((8, ki), n_tr.astype(jnp.float32))
    grad_tr = dot(x_tr, g_tr) / n_tr.astype(jnp.float32)
    grad_te = dot(x_te, g_te) / n_te.astype(jnp.float32)
    gtr_ref[...] = grad_tr
    gte_ref[0, :, :ko] = grad_te[:half]
    gte_ref[0, :, ko:] = grad_te[half:]


def damped(c):
    n = c.shape[0]
    i = lax.broadcasted_iota(jnp.int32, (n, n), 0)
    j = lax.broadcasted_iota(jnp.int32, (n, n), 1)
    eye = (i == j).astype(jnp.float32)
    trace = jnp.sum(c * eye, axis=(0, 1), keepdims=True)
    low = 0.1 * trace / n
    a = c + low * eye
    high = jnp.max(jnp.sum(jnp.abs(a), axis=0, keepdims=True), axis=1, keepdims=True)
    return a, eye, low, jnp.minimum(high, trace + low)


def mm(a, b):
    return jnp.dot(a, b, precision=HI, preferred_element_type=jnp.float32)


def inverses(matrices):
    state = []
    for c in matrices:
        a, eye, low, high = damped(c)
        scale = 2.0 / (low + high)
        r = (high - low) / (high + low)
        state.append((a, scale * a, scale * eye, r))
    for step in range(NEWTON_STEPS):
        nxt = []
        for a, m, x, r in state:
            s = 2.0 / (2.0 - r * r)
            n = m.shape[0]
            if step == 0:
                mx = s * (2.0 * m - mm(m, m))
                xx = s * (2.0 * x - x[:1, :1] * m)
            else:
                both = mm(jnp.concatenate([m, x], axis=0), m)
                mx = s * (2.0 * m - both[:n])
                xx = s * (2.0 * x - both[n:])
            nxt.append((a, mx, xx, r * r / (2.0 - r * r)))
        state = nxt
    return [2.0 * x - mm(x, mm(a, x)) for a, m, x, r in state]


def side_kernel(fac_ref, gtr_ref, out_ref):
    ki = fac_ref.shape[1]
    half = ki // 2
    top = fac_ref[:half, :]
    low = fac_ref[half:ki, :]
    c_in = jnp.concatenate(
        [top, jnp.concatenate([top[:, half:].T, low[:, :half]], axis=1)], axis=0
    )
    count = fac_ref[ki : ki + 1, :1]
    inv_in, inv_out = inverses([c_in, low[:, half:]])
    side = mm(mm(inv_in, gtr_ref[...]), inv_out) * (count * count)
    out_ref[:, :half] = side[:half]
    out_ref[:, half:] = side[half:]


def scores_kernel(order, n_blk, side_ref, gte_ref, out_ref):
    z = lax.axis_index("dp")
    b = lax.axis_index("blk")
    lane = lax.broadcasted_iota(jnp.int32, out_ref.shape, 1)
    row = jnp.zeros(out_ref.shape, jnp.float32)
    side = side_ref[...]
    for p, (dz, db) in enumerate(order):
        value = jnp.sum(side * gte_ref[p], axis=(0, 1), keepdims=True)
        row = jnp.where(lane == (z ^ dz) * n_blk + (b ^ db), value, row)
    out_ref[...] = row


def project(xs, w_in, w_out, n_groups, n_dp, n_blk):
    tokens, width = xs[0].shape
    rin, rout = w_in.shape[0], w_out.shape[0]
    ki, ko = rin * n_dp, rout * n_dp
    out_shape = jax.ShapeDtypeStruct((3 * tokens, ki), jnp.float32)
    if (n_groups, n_dp, n_blk) != (2, 4, 2):
        w_in = lax.all_gather(w_in, "dp", axis=0, tiled=True)
        w_out = lax.all_gather(w_out, "dp", axis=0, tiled=True)
        return call(project_kernel, out_shape, [vmem()] * 6, (*xs, w_in, w_out))

    part = width // 8
    q = lax.axis_index(PLANE)
    mine = lax.dynamic_slice(
        jnp.concatenate([w_in, w_out], axis=0), (0, q * 2 * part), (rin + rout, 2 * part))
    xs = call(
        load_kernel,
        tuple(jax.ShapeDtypeStruct(x.shape, x.dtype) for x in xs),
        [pl.BlockSpec(memory_space=pltpu.HBM)] * 4,
        xs,
        flops=1 << 30,
        scratch_shapes=[pltpu.SemaphoreType.DMA((8,))],
    )
    halves = [mine[:, :part], mine[:, part:]]
    far = [swap(h, "dp", n_dp, 2) for h in halves]
    near = [swap(jnp.concatenate([h, f], axis=0), "dp", n_dp, 1) for h, f in zip(halves, far)]
    za, zb = [jnp.concatenate([f, n], axis=0) for f, n in zip(far, near)]
    shifts = (2, 1, 3)

    def accumulate(plan, pieces, acc):
        args = (*xs, w_in, w_out, *pieces) + (() if acc is None else (acc,))
        return call(
            functools.partial(
                project_pieces_kernel, plan, shifts, acc is not None, len(pieces)),
            out_shape,
            [vmem()] * len(args),
            args,
            flops=1 << 30,
            scratch_shapes=[
                pltpu.VMEM((ki, part * len(plan)), jnp.bfloat16),
                pltpu.VMEM((ko, part * len(plan)), jnp.bfloat16),
            ],
        )

    xa = swap(za, PLANE, 4, 1)
    yb = swap(zb, PLANE, 4, 2)
    acc = accumulate(((0, 0, 0, 0), (0, 1, 1, 0)), (za, zb), None)
    ya_da = swap(jnp.concatenate([za, xa], axis=0), PLANE, 4, 2)
    xb_db = swap(jnp.concatenate([zb, yb], axis=0), PLANE, 4, 1)
    acc = accumulate(((1, 0, 0, 0), (2, 1, 1, 0)), (xa, yb), acc)
    rows = za.shape[0]
    return accumulate(
        ((2, 0, 0, 0), (3, 0, 0, rows), (1, 1, 1, 0), (3, 1, 1, rows)), (ya_da, xb_db), acc)


def per_device(
    n_groups, n_dp, n_blk, train_inputs, train_cotangents, train_lengths,
    test_inputs, test_cotangents, test_lengths, proj_in, proj_out,
):
    _, tokens, width = train_inputs.shape
    xs = [a.reshape(tokens, width) for a in (
        train_inputs, train_cotangents, test_inputs, test_cotangents)]
    part = project(xs, proj_in.T, proj_out.T, n_groups, n_dp, n_blk)
    ki = part.shape[1]
    ko = ki // 2
    other = swap(part, "mp", 2, 1)
    fac, gte, gtr = call(
        moments_kernel,
        (
            jax.ShapeDtypeStruct((ki + 8, ki), jnp.float32),
            jax.ShapeDtypeStruct((1, ki // 2, ki), jnp.float32),
            jax.ShapeDtypeStruct((ki, ko), jnp.float32),
        ),
        [smem(), smem(), vmem(), vmem()],
        (train_lengths, test_lengths, part, other),
    )
    order = [(0, 0)]
    for axis, count in (("blk", n_blk), ("dp", n_dp)):
        for k in bits(count):
            fac = fac + swap(fac, axis, count, k)
            gte = jnp.concatenate([gte, swap(gte, axis, count, k)], axis=0)
            order += [(dz ^ k, db) if axis == "dp" else (dz, db ^ k) for dz, db in order]
    side = call(
        side_kernel,
        jax.ShapeDtypeStruct((ki // 2, ki), jnp.float32),
        [vmem()] * 2,
        (fac, gtr),
        flops=4 << 30,
    )
    return call(
        functools.partial(scores_kernel, order, n_blk),
        jax.ShapeDtypeStruct((1, n_dp * n_blk), jnp.float32),
        [vmem()] * 2,
        (side, gte),
    )


def solution(mesh):
    feature = P(("groups", "dp", "blk"), None, "mp")
    length = P(("groups", "dp", "blk"))
    weight = P("mp", "dp")
    shape = mesh.shape
    return jax.shard_map(
        functools.partial(per_device, shape["groups"], shape["dp"], shape["blk"]),
        mesh=mesh,
        in_specs=(feature, feature, length, feature, feature, length, weight, weight),
        out_specs=P(("groups", "dp", "blk"), None),
        check_vma=False,
    )
```

```python
import functools

import jax
import jax.numpy as jnp
from jax import lax
from jax.experimental import pallas as pl
from jax.experimental.pallas import tpu as pltpu
from jax.sharding import PartitionSpec as P

HI = lax.Precision.HIGHEST
NT = (((1,), (1,)), ((), ()))
TN = (((0,), (0,)), ((), ()))
NEWTON_STEPS = 7
PLANE = ("groups", "blk")


def vmem():
    return pl.BlockSpec(memory_space=pltpu.VMEM)


def smem():
    return pl.BlockSpec(memory_space=pltpu.SMEM)


def call(kernel, out_shape, in_specs, args, flops=0, **kw):
    return pl.pallas_call(
        kernel,
        out_shape=out_shape,
        in_specs=in_specs,
        out_specs=jax.tree.map(lambda _: vmem(), out_shape),
        compiler_params=pltpu.CompilerParams(vmem_limit_bytes=32 * 1024 * 1024),
        cost_estimate=pl.CostEstimate(flops=flops, bytes_accessed=4 << 20, transcendentals=0),
        **kw,
    )(*args)


def swap(x, axis, count, k):
    return lax.ppermute(x, axis, [(i, i ^ k) for i in range(count)])


def bits(count):
    return [1 << s for s in reversed(range(count.bit_length() - 1))]


def load_kernel(n, *refs):
    srcs, dsts, token, sem = refs[:n], refs[n : 2 * n], refs[2 * n], refs[2 * n + 1]
    copies = []
    for i, (src, dst) in enumerate(zip(srcs, dsts)):
        rows = src.shape[0] // 2
        for h in range(2):
            part = pl.ds(h * rows, rows)
            copies.append(pltpu.make_async_copy(src.at[part], dst.at[part], sem.at[2 * i + h]))
    for c in copies:
        c.start()
    token[...] = jnp.zeros_like(token)
    for c in copies:
        c.wait()


def store_products(x_parts, g_parts, acc_ref, out_ref):
    tokens = out_ref.shape[0] // 3
    ko = g_parts[0].shape[1]
    for n in range(2):
        rows = slice(n * tokens, (n + 1) * tokens)
        prior = 0.0 if acc_ref is None else acc_ref[rows, :]
        out_ref[rows, :] = prior + x_parts[n]
    rows = slice(2 * tokens, 3 * tokens)
    for n in range(2):
        cols = slice(n * ko, (n + 1) * ko)
        prior = 0.0 if acc_ref is None else acc_ref[rows, cols]
        out_ref[rows, cols] = prior + g_parts[n]


def nt(a, b):
    return lax.dot_general(a, b, NT, preferred_element_type=jnp.float32)


def project_kernel(*refs):
    x_refs, (w_in, w_out, out_ref) = refs[:4], refs[4:]
    xs = [nt(x_refs[n][...], w_in[...]) for n in (0, 2)]
    gs = [nt(x_refs[n][...], w_out[...]) for n in (1, 3)]
    store_products(xs, gs, None, out_ref)


def project_pieces_kernel(plan, with_acc, n_pieces, *refs):
    x_refs, (own_in, own_out) = refs[:4], refs[4:6]
    pieces = refs[6 : 6 + n_pieces]
    acc_ref = refs[6 + n_pieces] if with_acc else None
    out_ref, w_in, w_out = refs[6 + n_pieces + with_acc :]
    z = lax.axis_index("dp")
    q = lax.axis_index(PLANE)
    rin, rout = own_in.shape[0], own_out.shape[0]
    quarter = own_in.shape[1] // 4
    xs, gs = [0.0, 0.0], [0.0, 0.0]
    at = 0
    for dq, col, width, rows in plan:
        start = pl.multiple_of((q ^ dq) * quarter + col, 128)
        cols = pl.ds(start, width)
        here = slice(at, at + width)
        at += width
        w_in[pl.ds(pl.multiple_of(z * rin, rin), rin), here] = own_in[:, cols]
        w_out[pl.ds(pl.multiple_of(z * rout, rout), rout), here] = own_out[:, cols]
        for p, row, k in rows:
            dst_in = pl.multiple_of((z ^ k) * rin, rin)
            dst_out = pl.multiple_of((z ^ k) * rout, rout)
            w_in[pl.ds(dst_in, rin), here] = pieces[p][row : row + rin, :]
            w_out[pl.ds(dst_out, rout), here] = pieces[p][row + rin : row + rin + rout, :]
        for m in range(2):
            xs[m] += nt(x_refs[2 * m][:, cols], w_in[:, here])
            gs[m] += nt(x_refs[2 * m + 1][:, cols], w_out[:, here])
    store_products(xs, gs, acc_ref, out_ref)


def moments_kernel(len_tr, len_te, mine, other, fac_ref, gte_ref, gtr_ref):
    tokens = mine.shape[0] // 3
    ki = mine.shape[1]
    ko = ki // 2
    total = mine[...] + other[...]
    rows = lax.broadcasted_iota(jnp.int32, (tokens, ki), 0)
    n_tr, n_te = len_tr[0], len_te[0]
    x_tr = jnp.where(rows < n_tr, total[:tokens], 0.0)
    x_te = jnp.where(rows < n_te, total[tokens : 2 * tokens], 0.0)
    g_both = total[2 * tokens :]
    g_tr = jnp.where(rows < n_tr, g_both, 0.0)[:, :ko]
    g_te = g_both[:, ko:]
    dot = functools.partial(
        lax.dot_general, dimension_numbers=TN, precision=HI,
        preferred_element_type=jnp.float32,
    )
    c_in = dot(x_tr, x_tr)
    c_out = dot(g_tr, g_tr)
    half = ki // 2
    fac_ref[:half, :] = c_in[:half, :]
    fac_ref[half:ki, :half] = c_in[half:, half:]
    fac_ref[half:ki, half:] = c_out
    fac_ref[ki:, :] = jnp.full((8, ki), n_tr.astype(jnp.float32))
    grad_tr = dot(x_tr, g_tr) / n_tr.astype(jnp.float32)
    grad_te = dot(x_te, g_te) / n_te.astype(jnp.float32)
    gtr_ref[...] = grad_tr
    gte_ref[0, :, :ko] = grad_te[:half]
    gte_ref[0, :, ko:] = grad_te[half:]


def damped(c):
    n = c.shape[0]
    i = lax.broadcasted_iota(jnp.int32, (n, n), 0)
    j = lax.broadcasted_iota(jnp.int32, (n, n), 1)
    eye = (i == j).astype(jnp.float32)
    trace = jnp.sum(c * eye, axis=(0, 1), keepdims=True)
    low = 0.1 * trace / n
    a = c + low * eye
    high = jnp.max(jnp.sum(jnp.abs(a), axis=0, keepdims=True), axis=1, keepdims=True)
    return a, eye, low, jnp.minimum(high, trace + low)


def mm(a, b):
    return jnp.dot(a, b, precision=HI, preferred_element_type=jnp.float32)


def inverses(matrices):
    state = []
    for c in matrices:
        a, eye, low, high = damped(c)
        scale = 2.0 / (low + high)
        r = (high - low) / (high + low)
        state.append((a, scale * a, scale * eye, r))
    for step in range(NEWTON_STEPS):
        nxt = []
        for a, m, x, r in state:
            s = 2.0 / (2.0 - r * r)
            n = m.shape[0]
            if step == 0:
                mx = s * (2.0 * m - mm(m, m))
                xx = s * (2.0 * x - x[:1, :1] * m)
            else:
                both = mm(jnp.concatenate([m, x], axis=0), m)
                mx = s * (2.0 * m - both[:n])
                xx = s * (2.0 * x - both[n:])
            nxt.append((a, mx, xx, r * r / (2.0 - r * r)))
        state = nxt
    return [2.0 * x - mm(x, mm(a, x)) for a, m, x, r in state]


def side_kernel(fac_ref, gtr_ref, out_ref):
    ki = fac_ref.shape[1]
    half = ki // 2
    top = fac_ref[:half, :]
    low = fac_ref[half:ki, :]
    c_in = jnp.concatenate(
        [top, jnp.concatenate([top[:, half:].T, low[:, :half]], axis=1)], axis=0
    )
    count = fac_ref[ki : ki + 1, :1]
    inv_in, inv_out = inverses([c_in, low[:, half:]])
    side = mm(mm(inv_in, gtr_ref[...]), inv_out) * (count * count)
    out_ref[:, :half] = side[:half]
    out_ref[:, half:] = side[half:]


def scores_kernel(order, n_blk, side_ref, gte_ref, out_ref):
    z = lax.axis_index("dp")
    b = lax.axis_index("blk")
    lane = lax.broadcasted_iota(jnp.int32, out_ref.shape, 1)
    row = jnp.zeros(out_ref.shape, jnp.float32)
    side = side_ref[...]
    for p, (dz, db) in enumerate(order):
        value = jnp.sum(side * gte_ref[p], axis=(0, 1), keepdims=True)
        row = jnp.where(lane == (z ^ dz) * n_blk + (b ^ db), value, row)
    out_ref[...] = row


def project(xs, w_in, w_out, n_groups, n_dp, n_blk):
    tokens, width = xs[0].shape
    rin, rout = w_in.shape[0], w_out.shape[0]
    ki, ko = rin * n_dp, rout * n_dp
    out_shape = jax.ShapeDtypeStruct((3 * tokens, ki), jnp.float32)
    if (n_groups, n_dp, n_blk) != (2, 4, 2):
        w_in = lax.all_gather(w_in, "dp", axis=0, tiled=True)
        w_out = lax.all_gather(w_out, "dp", axis=0, tiled=True)
        return call(project_kernel, out_shape, [vmem()] * 6, (*xs, w_in, w_out))

    part = width // 8
    shard = rin + rout
    q = lax.axis_index(PLANE)
    whole = jnp.concatenate([w_in, w_out], axis=0)
    mine = lax.dynamic_slice(whole, (0, q * 2 * part), (shard, 2 * part))
    opposite = lax.dynamic_slice(whole, (0, (q ^ 3) * 2 * part), (shard, 2 * part))
    *xs, w_in, w_out, token = call(
        functools.partial(load_kernel, 6),
        tuple(pltpu.VMEM(x.shape, x.dtype) for x in (*xs, w_in, w_out))
        + (jax.ShapeDtypeStruct((1, part), jnp.bfloat16),),
        [pl.BlockSpec(memory_space=pltpu.HBM)] * 6,
        [pltpu.with_memory_space_constraint(x, pltpu.HBM) for x in (*xs, w_in, w_out)],
        flops=1 << 30,
        scratch_shapes=[pltpu.SemaphoreType.DMA((12,))],
    )
    halves = [mine[:, :part], mine[:, part:]]
    far = [swap(h, "dp", n_dp, 2) for h in halves]
    far_op = swap(opposite, "dp", n_dp, 2)
    doubled = [jnp.concatenate([h, f], axis=0) for h, f in zip(halves, far)]
    near = [swap(doubled[0] + token, "dp", n_dp, 1), swap(doubled[1], "dp", n_dp, 1)]
    near_op = swap(jnp.concatenate([opposite, far_op], axis=0), "dp", n_dp, 1)
    za, zb = [jnp.concatenate([f, n], axis=0) for f, n in zip(far, near)]
    xa, ya = swap(za, PLANE, 4, 1), swap(za, PLANE, 4, 2)
    xb, yb = swap(zb, PLANE, 4, 1), swap(zb, PLANE, 4, 2)

    def accumulate(plan, pieces, acc):
        args = (*xs, w_in, w_out, *pieces) + (() if acc is None else (acc,))
        total = sum(width for _, _, width, _ in plan)
        return call(
            functools.partial(project_pieces_kernel, plan, acc is not None, len(pieces)),
            out_shape,
            [vmem()] * len(args),
            args,
            flops=1 << 30,
            scratch_shapes=[
                pltpu.VMEM((ki, total), jnp.bfloat16),
                pltpu.VMEM((ko, total), jnp.bfloat16),
            ],
        )

    def stacked(p):
        return tuple((p, i * shard, k) for i, k in enumerate((2, 1, 3)))

    acc = accumulate(
        ((0, 0, part, stacked(0)), (0, part, part, stacked(1))), (za, zb), None)
    acc = accumulate(
        ((1, 0, part, stacked(0)), (2, 0, part, stacked(1))), (xa, ya), acc)
    return accumulate(
        (
            (1, part, part, stacked(0)),
            (2, part, part, stacked(1)),
            (3, 0, 2 * part, ((2, 0, 2), (3, 0, 1), (3, shard, 3))),
        ),
        (xb, yb, far_op, near_op),
        acc,
    )


def per_device(
    n_groups, n_dp, n_blk, train_inputs, train_cotangents, train_lengths,
    test_inputs, test_cotangents, test_lengths, proj_in, proj_out,
):
    _, tokens, width = train_inputs.shape
    xs = [a.reshape(tokens, width) for a in (
        train_inputs, train_cotangents, test_inputs, test_cotangents)]
    part = project(xs, proj_in.T, proj_out.T, n_groups, n_dp, n_blk)
    ki = part.shape[1]
    ko = ki // 2
    other = swap(part, "mp", 2, 1)
    fac, gte, gtr = call(
        moments_kernel,
        (
            jax.ShapeDtypeStruct((ki + 8, ki), jnp.float32),
            jax.ShapeDtypeStruct((1, ki // 2, ki), jnp.float32),
            jax.ShapeDtypeStruct((ki, ko), jnp.float32),
        ),
        [smem(), smem(), vmem(), vmem()],
        (train_lengths, test_lengths, part, other),
    )
    order = [(0, 0)]
    for axis, count in (("blk", n_blk), ("dp", n_dp)):
        for k in bits(count):
            fac = fac + swap(fac, axis, count, k)
            gte = jnp.concatenate([gte, swap(gte, axis, count, k)], axis=0)
            order += [(dz ^ k, db) if axis == "dp" else (dz, db ^ k) for dz, db in order]
    side = call(
        side_kernel,
        jax.ShapeDtypeStruct((ki // 2, ki), jnp.float32),
        [vmem()] * 2,
        (fac, gtr),
        flops=4 << 30,
    )
    return call(
        functools.partial(scores_kernel, order, n_blk),
        jax.ShapeDtypeStruct((1, n_dp * n_blk), jnp.float32),
        [vmem()] * 2,
        (side, gte),
    )


def solution(mesh):
    feature = P(("groups", "dp", "blk"), None, "mp")
    length = P(("groups", "dp", "blk"))
    weight = P("mp", "dp")
    shape = mesh.shape
    return jax.shard_map(
        functools.partial(per_device, shape["groups"], shape["dp"], shape["blk"]),
        mesh=mesh,
        in_specs=(feature, feature, length, feature, feature, length, weight, weight),
        out_specs=P(("groups", "dp", "blk"), None),
        check_vma=False,
    )
```

```python
import functools

import jax
import jax.numpy as jnp
from jax import lax
from jax.experimental import pallas as pl
from jax.experimental.pallas import tpu as pltpu
from jax.sharding import PartitionSpec as P

HI = lax.Precision.HIGHEST
NT = (((1,), (1,)), ((), ()))
TN = (((0,), (0,)), ((), ()))
NEWTON_STEPS = 7
PLANE = ("groups", "blk")


def vmem():
    return pl.BlockSpec(memory_space=pltpu.VMEM)


def smem():
    return pl.BlockSpec(memory_space=pltpu.SMEM)


def call(kernel, out_shape, in_specs, args, flops=0, **kw):
    return pl.pallas_call(
        kernel,
        out_shape=out_shape,
        in_specs=in_specs,
        out_specs=jax.tree.map(lambda _: vmem(), out_shape),
        compiler_params=pltpu.CompilerParams(vmem_limit_bytes=16 * 1024 * 1024),
        cost_estimate=pl.CostEstimate(flops=flops, bytes_accessed=4 << 20, transcendentals=0),
        **kw,
    )(*args)


def swap(x, axis, count, k):
    return lax.ppermute(x, axis, [(i, i ^ k) for i in range(count)])


def bits(count):
    return [1 << s for s in reversed(range(count.bit_length() - 1))]


def load_kernel(n, *refs):
    srcs, dsts, sem = refs[:n], refs[n + 1 : 2 * n + 1], refs[2 * n + 1]
    copies = []
    for i, (src, dst) in enumerate(zip(srcs, dsts)):
        rows = src.shape[0] // 2
        for h in range(2):
            part = pl.ds(h * rows, rows)
            copies.append(pltpu.make_async_copy(src.at[part], dst.at[part], sem.at[2 * i + h]))
    for c in copies:
        c.start()
    for c in copies:
        c.wait()


def store_products(x_parts, g_parts, acc_ref, out_ref):
    tokens = out_ref.shape[0] // 3
    ko = g_parts[0].shape[1]
    for n in range(2):
        rows = slice(n * tokens, (n + 1) * tokens)
        prior = 0.0 if acc_ref is None else acc_ref[rows, :]
        out_ref[rows, :] = prior + x_parts[n]
    rows = slice(2 * tokens, 3 * tokens)
    for n in range(2):
        cols = slice(n * ko, (n + 1) * ko)
        prior = 0.0 if acc_ref is None else acc_ref[rows, cols]
        out_ref[rows, cols] = prior + g_parts[n]


def nt(a, b):
    return lax.dot_general(a, b, NT, preferred_element_type=jnp.float32)


def project_kernel(*refs):
    x_refs, (w_in, w_out, out_ref) = refs[:4], refs[4:]
    xs = [nt(x_refs[n][...], w_in[...]) for n in (0, 2)]
    gs = [nt(x_refs[n][...], w_out[...]) for n in (1, 3)]
    store_products(xs, gs, None, out_ref)


def project_pieces_kernel(plan, with_acc, n_pieces, *refs):
    x_refs, (own_in, own_out) = refs[:4], refs[4:6]
    pieces = refs[6 : 6 + n_pieces]
    acc_ref = refs[6 + n_pieces] if with_acc else None
    out_ref, w_in, w_out = refs[6 + n_pieces + with_acc :]
    z = lax.axis_index("dp")
    q = lax.axis_index(PLANE)
    rin, rout = own_in.shape[0], own_out.shape[0]
    quarter = own_in.shape[1] // 4
    xs, gs = [0.0, 0.0], [0.0, 0.0]
    at = 0
    for dq, col, width, rows in plan:
        start = pl.multiple_of((q ^ dq) * quarter + col, 128)
        cols = pl.ds(start, width)
        here = slice(at, at + width)
        at += width
        w_in[pl.ds(pl.multiple_of(z * rin, rin), rin), here] = own_in[:, cols]
        w_out[pl.ds(pl.multiple_of(z * rout, rout), rout), here] = own_out[:, cols]
        for p, row, k in rows:
            dst_in = pl.multiple_of((z ^ k) * rin, rin)
            dst_out = pl.multiple_of((z ^ k) * rout, rout)
            w_in[pl.ds(dst_in, rin), here] = pieces[p][row : row + rin, :]
            w_out[pl.ds(dst_out, rout), here] = pieces[p][row + rin : row + rin + rout, :]
        for m in range(2):
            xs[m] += nt(x_refs[2 * m][:, cols], w_in[:, here])
            gs[m] += nt(x_refs[2 * m + 1][:, cols], w_out[:, here])
    store_products(xs, gs, acc_ref, out_ref)


def moments_kernel(len_tr, len_te, mine, other, fac_ref, gte_ref, gtr_ref):
    tokens = mine.shape[0] // 3
    ki = mine.shape[1]
    ko = ki // 2
    total = mine[...] + other[...]
    rows = lax.broadcasted_iota(jnp.int32, (tokens, ki), 0)
    n_tr, n_te = len_tr[0], len_te[0]
    x_tr = jnp.where(rows < n_tr, total[:tokens], 0.0)
    x_te = jnp.where(rows < n_te, total[tokens : 2 * tokens], 0.0)
    g_both = total[2 * tokens :]
    g_tr = jnp.where(rows < n_tr, g_both, 0.0)[:, :ko]
    g_te = g_both[:, ko:]
    dot = functools.partial(
        lax.dot_general, dimension_numbers=TN, precision=HI,
        preferred_element_type=jnp.float32,
    )
    c_in = dot(x_tr, x_tr)
    c_out = dot(g_tr, g_tr)
    half = ki // 2
    fac_ref[:half, :] = c_in[:half, :]
    fac_ref[half:ki, :half] = c_in[half:, half:]
    fac_ref[half:ki, half:] = c_out
    fac_ref[ki:, :] = jnp.full((8, ki), n_tr.astype(jnp.float32))
    grad_tr = dot(x_tr, g_tr) / n_tr.astype(jnp.float32)
    grad_te = dot(x_te, g_te) / n_te.astype(jnp.float32)
    gtr_ref[...] = grad_tr
    gte_ref[0, :, :ko] = grad_te[:half]
    gte_ref[0, :, ko:] = grad_te[half:]


def damped(c):
    n = c.shape[0]
    i = lax.broadcasted_iota(jnp.int32, (n, n), 0)
    j = lax.broadcasted_iota(jnp.int32, (n, n), 1)
    eye = (i == j).astype(jnp.float32)
    trace = jnp.sum(c * eye, axis=(0, 1), keepdims=True)
    low = 0.1 * trace / n
    a = c + low * eye
    high = jnp.max(jnp.sum(jnp.abs(a), axis=0, keepdims=True), axis=1, keepdims=True)
    return a, eye, low, jnp.minimum(high, trace + low)


def mm(a, b):
    return jnp.dot(a, b, precision=HI, preferred_element_type=jnp.float32)


def inverses(matrices):
    state = []
    for c in matrices:
        a, eye, low, high = damped(c)
        scale = 2.0 / (low + high)
        r = (high - low) / (high + low)
        state.append((a, scale * a, scale * eye, r))
    for step in range(NEWTON_STEPS):
        nxt = []
        for a, m, x, r in state:
            s = 2.0 / (2.0 - r * r)
            n = m.shape[0]
            if step == 0:
                mx = s * (2.0 * m - mm(m, m))
                xx = s * (2.0 * x - x[:1, :1] * m)
            else:
                both = mm(jnp.concatenate([m, x], axis=0), m)
                mx = s * (2.0 * m - both[:n])
                xx = s * (2.0 * x - both[n:])
            nxt.append((a, mx, xx, r * r / (2.0 - r * r)))
        state = nxt
    return [2.0 * x - mm(x, mm(a, x)) for a, m, x, r in state]


def side_kernel(fac_ref, gtr_ref, out_ref):
    ki = fac_ref.shape[1]
    half = ki // 2
    top = fac_ref[:half, :]
    low = fac_ref[half:ki, :]
    c_in = jnp.concatenate(
        [top, jnp.concatenate([top[:, half:].T, low[:, :half]], axis=1)], axis=0
    )
    count = fac_ref[ki : ki + 1, :1]
    inv_in, inv_out = inverses([c_in, low[:, half:]])
    side = mm(mm(inv_in, gtr_ref[...]), inv_out) * (count * count)
    out_ref[:, :half] = side[:half]
    out_ref[:, half:] = side[half:]


def scores_kernel(order, n_blk, side_ref, gte_ref, out_ref):
    z = lax.axis_index("dp")
    b = lax.axis_index("blk")
    lane = lax.broadcasted_iota(jnp.int32, out_ref.shape, 1)
    row = jnp.zeros(out_ref.shape, jnp.float32)
    side = side_ref[...]
    for p, (dz, db) in enumerate(order):
        value = jnp.sum(side * gte_ref[p], axis=(0, 1), keepdims=True)
        row = jnp.where(lane == (z ^ dz) * n_blk + (b ^ db), value, row)
    out_ref[...] = row


def project(xs, w_in, w_out, n_groups, n_dp, n_blk):
    tokens, width = xs[0].shape
    rin, rout = w_in.shape[0], w_out.shape[0]
    ki, ko = rin * n_dp, rout * n_dp
    out_shape = jax.ShapeDtypeStruct((3 * tokens, ki), jnp.float32)
    if (n_groups, n_dp, n_blk) != (2, 4, 2):
        w_in = lax.all_gather(w_in, "dp", axis=0, tiled=True)
        w_out = lax.all_gather(w_out, "dp", axis=0, tiled=True)
        return call(project_kernel, out_shape, [vmem()] * 6, (*xs, w_in, w_out))

    part = width // 8
    shard = rin + rout
    q = lax.axis_index(PLANE)
    whole = jnp.concatenate([w_in, w_out], axis=0)
    mine = lax.dynamic_slice(whole, (0, q * 2 * part), (shard, 2 * part))
    opposite = lax.dynamic_slice(whole, (0, (q ^ 3) * 2 * part), (shard, 2 * part))
    halves = [mine[:, :part], mine[:, part:]]
    far = [swap(h, "dp", n_dp, 2) for h in halves]
    far_op = swap(opposite, "dp", n_dp, 2)
    doubled = [jnp.concatenate([h, f], axis=0) for h, f in zip(halves, far)]
    near = [swap(d, "dp", n_dp, 1) for d in doubled]
    near_op = swap(jnp.concatenate([opposite, far_op], axis=0), "dp", n_dp, 1)
    za, zb = [jnp.concatenate([f, n], axis=0) for f, n in zip(far, near)]
    xa, ya = swap(za, PLANE, 4, 1), swap(za, PLANE, 4, 2)
    xb, yb = swap(zb, PLANE, 4, 1), swap(zb, PLANE, 4, 2)
    operands = (*xs, w_in, w_out)
    *xs, w_in, w_out = call(
        functools.partial(load_kernel, 6),
        tuple(pltpu.VMEM(x.shape, x.dtype) for x in operands),
        [pl.BlockSpec(memory_space=pltpu.HBM)] * 6 + [pl.BlockSpec(memory_space=pl.ANY)],
        [pltpu.with_memory_space_constraint(x, pltpu.HBM) for x in operands] + [zb],
        flops=1 << 30,
        scratch_shapes=[pltpu.SemaphoreType.DMA((12,))],
    )

    def accumulate(plan, pieces, acc):
        args = (*xs, w_in, w_out, *pieces) + (() if acc is None else (acc,))
        total = sum(width for _, _, width, _ in plan)
        return call(
            functools.partial(project_pieces_kernel, plan, acc is not None, len(pieces)),
            out_shape,
            [vmem()] * len(args),
            args,
            flops=1 << 30,
            scratch_shapes=[
                pltpu.VMEM((ki, total), jnp.bfloat16),
                pltpu.VMEM((ko, total), jnp.bfloat16),
            ],
        )

    def stacked(p):
        return tuple((p, i * shard, k) for i, k in enumerate((2, 1, 3)))

    acc = accumulate(
        ((0, 0, part, stacked(0)), (0, part, part, stacked(1))), (za, zb), None)
    acc = accumulate(
        ((1, 0, part, stacked(0)), (2, 0, part, stacked(1))), (xa, ya), acc)
    return accumulate(
        (
            (1, part, part, stacked(0)),
            (2, part, part, stacked(1)),
            (3, 0, 2 * part, ((2, 0, 2), (3, 0, 1), (3, shard, 3))),
        ),
        (xb, yb, far_op, near_op),
        acc,
    )


def per_device(
    n_groups, n_dp, n_blk, train_inputs, train_cotangents, train_lengths,
    test_inputs, test_cotangents, test_lengths, proj_in, proj_out,
):
    _, tokens, width = train_inputs.shape
    xs = [a.reshape(tokens, width) for a in (
        train_inputs, train_cotangents, test_inputs, test_cotangents)]
    part = project(xs, proj_in.T, proj_out.T, n_groups, n_dp, n_blk)
    ki = part.shape[1]
    ko = ki // 2
    other = swap(part, "mp", 2, 1)
    fac, gte, gtr = call(
        moments_kernel,
        (
            jax.ShapeDtypeStruct((ki + 8, ki), jnp.float32),
            jax.ShapeDtypeStruct((1, ki // 2, ki), jnp.float32),
            jax.ShapeDtypeStruct((ki, ko), jnp.float32),
        ),
        [smem(), smem(), vmem(), vmem()],
        (train_lengths, test_lengths, part, other),
    )
    order = [(0, 0)]
    for axis, count in (("blk", n_blk), ("dp", n_dp)):
        for k in bits(count):
            fac = fac + swap(fac, axis, count, k)
            gte = jnp.concatenate([gte, swap(gte, axis, count, k)], axis=0)
            order += [(dz ^ k, db) if axis == "dp" else (dz, db ^ k) for dz, db in order]
    side = call(
        side_kernel,
        jax.ShapeDtypeStruct((ki // 2, ki), jnp.float32),
        [vmem()] * 2,
        (fac, gtr),
        flops=4 << 30,
    )
    return call(
        functools.partial(scores_kernel, order, n_blk),
        jax.ShapeDtypeStruct((1, n_dp * n_blk), jnp.float32),
        [vmem()] * 2,
        (side, gte),
    )


def solution(mesh):
    feature = P(("groups", "dp", "blk"), None, "mp")
    length = P(("groups", "dp", "blk"))
    weight = P("mp", "dp")
    shape = mesh.shape
    return jax.shard_map(
        functools.partial(per_device, shape["groups"], shape["dp"], shape["blk"]),
        mesh=mesh,
        in_specs=(feature, feature, length, feature, feature, length, weight, weight),
        out_specs=P(("groups", "dp", "blk"), None),
        check_vma=False,
    )
```

```python
import functools

import jax
import jax.numpy as jnp
from jax import lax
from jax.experimental import pallas as pl
from jax.experimental.pallas import tpu as pltpu
from jax.sharding import PartitionSpec as P

HI = lax.Precision.HIGHEST
NT = (((1,), (1,)), ((), ()))
TN = (((0,), (0,)), ((), ()))
NEWTON_STEPS = 7
PLANE = ("groups", "blk")


def vmem():
    return pl.BlockSpec(memory_space=pltpu.VMEM)


def smem():
    return pl.BlockSpec(memory_space=pltpu.SMEM)


def call(kernel, out_shape, in_specs, args, flops=0, limit=16, **kw):
    return pl.pallas_call(
        kernel,
        out_shape=out_shape,
        in_specs=in_specs,
        out_specs=jax.tree.map(lambda _: vmem(), out_shape),
        compiler_params=pltpu.CompilerParams(vmem_limit_bytes=limit * 1024 * 1024),
        cost_estimate=pl.CostEstimate(flops=flops, bytes_accessed=1 << 16, transcendentals=0),
        **kw,
    )(*args)


def swap(x, axis, count, k):
    return lax.ppermute(x, axis, [(i, i ^ k) for i in range(count)])


def bits(count):
    return [1 << s for s in reversed(range(count.bit_length() - 1))]


def load_kernel(n, *refs):
    srcs, dsts, sem = refs[:n], refs[n : 2 * n], refs[2 * n]
    copies = []
    for i, (src, dst) in enumerate(zip(srcs, dsts)):
        rows = src.shape[0] // 2
        for h in range(2):
            part = pl.ds(h * rows, rows)
            copies.append(pltpu.make_async_copy(src.at[part], dst.at[part], sem.at[2 * i + h]))
    for c in copies:
        c.start()
    for c in copies:
        c.wait()


def stack_kernel(n, *refs):
    at = 0
    for src in refs[:n]:
        refs[-1][at : at + src.shape[0], :] = src[...]
        at += src.shape[0]


def stack(parts, after=None):
    rows = sum(p.shape[0] for p in parts)
    extra = () if after is None else (after,)
    return call(
        functools.partial(stack_kernel, len(parts)),
        pltpu.VMEM((rows, parts[0].shape[1]), parts[0].dtype),
        [vmem()] * len(parts) + [pl.BlockSpec(memory_space=pl.ANY)] * len(extra),
        (*parts, *extra),
        limit=1,
    )


def store_products(x_parts, g_parts, acc_ref, out_ref):
    tokens = out_ref.shape[0] // 3
    ko = g_parts[0].shape[1]
    for n in range(2):
        rows = slice(n * tokens, (n + 1) * tokens)
        prior = 0.0 if acc_ref is None else acc_ref[rows, :]
        out_ref[rows, :] = prior + x_parts[n]
    rows = slice(2 * tokens, 3 * tokens)
    for n in range(2):
        cols = slice(n * ko, (n + 1) * ko)
        prior = 0.0 if acc_ref is None else acc_ref[rows, cols]
        out_ref[rows, cols] = prior + g_parts[n]


def nt(a, b):
    return lax.dot_general(a, b, NT, preferred_element_type=jnp.float32)


def project_kernel(*refs):
    x_refs, (w_in, w_out, out_ref) = refs[:4], refs[4:]
    xs = [nt(x_refs[n][...], w_in[...]) for n in (0, 2)]
    gs = [nt(x_refs[n][...], w_out[...]) for n in (1, 3)]
    store_products(xs, gs, None, out_ref)


def project_pieces_kernel(plan, with_acc, n_pieces, *refs):
    x_refs, (own_in, own_out) = refs[:4], refs[4:6]
    pieces = refs[6 : 6 + n_pieces]
    acc_ref = refs[6 + n_pieces] if with_acc else None
    out_ref, w_in, w_out = refs[6 + n_pieces + with_acc :]
    z = lax.axis_index("dp")
    q = lax.axis_index(PLANE)
    rin, rout = own_in.shape[0], own_out.shape[0]
    quarter = own_in.shape[1] // 4
    xs, gs = [0.0, 0.0], [0.0, 0.0]
    at = 0
    for dq, col, width, rows in plan:
        start = pl.multiple_of((q ^ dq) * quarter + col, 128)
        cols = pl.ds(start, width)
        here = slice(at, at + width)
        at += width
        w_in[pl.ds(pl.multiple_of(z * rin, rin), rin), here] = own_in[:, cols]
        w_out[pl.ds(pl.multiple_of(z * rout, rout), rout), here] = own_out[:, cols]
        for p, row, k in rows:
            dst_in = pl.multiple_of((z ^ k) * rin, rin)
            dst_out = pl.multiple_of((z ^ k) * rout, rout)
            w_in[pl.ds(dst_in, rin), here] = pieces[p][row : row + rin, :]
            w_out[pl.ds(dst_out, rout), here] = pieces[p][row + rin : row + rin + rout, :]
        for m in range(2):
            xs[m] += nt(x_refs[2 * m][:, cols], w_in[:, here])
            gs[m] += nt(x_refs[2 * m + 1][:, cols], w_out[:, here])
    store_products(xs, gs, acc_ref, out_ref)


def moments_kernel(len_tr, len_te, mine, other, fac_ref, gte_ref, gtr_ref):
    tokens = mine.shape[0] // 3
    ki = mine.shape[1]
    ko = ki // 2
    total = mine[...] + other[...]
    rows = lax.broadcasted_iota(jnp.int32, (tokens, ki), 0)
    n_tr, n_te = len_tr[0], len_te[0]
    x_tr = jnp.where(rows < n_tr, total[:tokens], 0.0)
    x_te = jnp.where(rows < n_te, total[tokens : 2 * tokens], 0.0)
    g_both = total[2 * tokens :]
    g_tr = jnp.where(rows < n_tr, g_both, 0.0)[:, :ko]
    g_te = g_both[:, ko:]
    dot = functools.partial(
        lax.dot_general, dimension_numbers=TN, precision=HI,
        preferred_element_type=jnp.float32,
    )
    c_in = dot(x_tr, x_tr)
    c_out = dot(g_tr, g_tr)
    half = ki // 2
    fac_ref[:half, :] = c_in[:half, :]
    fac_ref[half:ki, :half] = c_in[half:, half:]
    fac_ref[half:ki, half:] = c_out
    fac_ref[ki:, :] = jnp.full((8, ki), n_tr.astype(jnp.float32))
    grad_tr = dot(x_tr, g_tr) / n_tr.astype(jnp.float32)
    grad_te = dot(x_te, g_te) / n_te.astype(jnp.float32)
    gtr_ref[...] = grad_tr
    gte_ref[0, :, :ko] = grad_te[:half]
    gte_ref[0, :, ko:] = grad_te[half:]


def damped(c):
    n = c.shape[0]
    i = lax.broadcasted_iota(jnp.int32, (n, n), 0)
    j = lax.broadcasted_iota(jnp.int32, (n, n), 1)
    eye = (i == j).astype(jnp.float32)
    trace = jnp.sum(c * eye, axis=(0, 1), keepdims=True)
    low = 0.1 * trace / n
    a = c + low * eye
    high = jnp.max(jnp.sum(jnp.abs(a), axis=0, keepdims=True), axis=1, keepdims=True)
    return a, eye, low, jnp.minimum(high, trace + low)


def mm(a, b):
    return jnp.dot(a, b, precision=HI, preferred_element_type=jnp.float32)


def inverses(matrices):
    state = []
    for c in matrices:
        a, eye, low, high = damped(c)
        scale = 2.0 / (low + high)
        r = (high - low) / (high + low)
        state.append((a, scale * a, scale * eye, r))
    for step in range(NEWTON_STEPS):
        nxt = []
        for a, m, x, r in state:
            s = 2.0 / (2.0 - r * r)
            n = m.shape[0]
            if step == 0:
                mx = s * (2.0 * m - mm(m, m))
                xx = s * (2.0 * x - x[:1, :1] * m)
            else:
                both = mm(jnp.concatenate([m, x], axis=0), m)
                mx = s * (2.0 * m - both[:n])
                xx = s * (2.0 * x - both[n:])
            nxt.append((a, mx, xx, r * r / (2.0 - r * r)))
        state = nxt
    return [2.0 * x - mm(x, mm(a, x)) for a, m, x, r in state]


def side_kernel(fac_ref, gtr_ref, out_ref):
    ki = fac_ref.shape[1]
    half = ki // 2
    top = fac_ref[:half, :]
    low = fac_ref[half:ki, :]
    c_in = jnp.concatenate(
        [top, jnp.concatenate([top[:, half:].T, low[:, :half]], axis=1)], axis=0
    )
    count = fac_ref[ki : ki + 1, :1]
    inv_in, inv_out = inverses([c_in, low[:, half:]])
    side = mm(mm(inv_in, gtr_ref[...]), inv_out) * (count * count)
    out_ref[:, :half] = side[:half]
    out_ref[:, half:] = side[half:]


def scores_kernel(order, n_blk, side_ref, gte_ref, out_ref):
    z = lax.axis_index("dp")
    b = lax.axis_index("blk")
    lane = lax.broadcasted_iota(jnp.int32, out_ref.shape, 1)
    row = jnp.zeros(out_ref.shape, jnp.float32)
    side = side_ref[...]
    for p, (dz, db) in enumerate(order):
        value = jnp.sum(side * gte_ref[p], axis=(0, 1), keepdims=True)
        row = jnp.where(lane == (z ^ dz) * n_blk + (b ^ db), value, row)
    out_ref[...] = row


def project(xs, w_in, w_out, n_groups, n_dp, n_blk):
    tokens, width = xs[0].shape
    rin, rout = w_in.shape[0], w_out.shape[0]
    ki, ko = rin * n_dp, rout * n_dp
    out_shape = jax.ShapeDtypeStruct((3 * tokens, ki), jnp.float32)
    if (n_groups, n_dp, n_blk) != (2, 4, 2):
        w_in = lax.all_gather(w_in, "dp", axis=0, tiled=True)
        w_out = lax.all_gather(w_out, "dp", axis=0, tiled=True)
        return call(project_kernel, out_shape, [vmem()] * 6, (*xs, w_in, w_out))

    part = width // 8
    shard = rin + rout
    q = lax.axis_index(PLANE)
    whole = jnp.concatenate([w_in, w_out], axis=0)
    mine = lax.dynamic_slice(whole, (0, q * 2 * part), (shard, 2 * part))
    opposite = lax.dynamic_slice(whole, (0, (q ^ 3) * 2 * part), (shard, 2 * part))
    operands = (*xs, w_in, w_out)
    *xs, w_in, w_out = call(
        functools.partial(load_kernel, 6),
        tuple(pltpu.VMEM(x.shape, x.dtype) for x in operands),
        [pl.BlockSpec(memory_space=pltpu.HBM)] * 6,
        [pltpu.with_memory_space_constraint(x, pltpu.HBM) for x in operands],
        flops=1 << 30,
        scratch_shapes=[pltpu.SemaphoreType.DMA((12,))],
    )
    halves = [mine[:, :part], mine[:, part:]]
    far = [swap(h, "dp", n_dp, 2) for h in halves]
    far_op = swap(opposite, "dp", n_dp, 2)
    both_a = stack((halves[0], far[0]), w_out)
    near_a = swap(both_a, "dp", n_dp, 1)
    both_b = stack((halves[1], far[1]))
    near_b = swap(both_b, "dp", n_dp, 1)
    za = stack((far[0], near_a))
    xa, ya = swap(za, PLANE, 4, 1), swap(za, PLANE, 4, 2)
    both_op = stack((opposite, far_op))
    near_op = swap(both_op, "dp", n_dp, 1)
    zb = stack((far[1], near_b))
    xb, yb = swap(zb, PLANE, 4, 1), swap(zb, PLANE, 4, 2)

    def accumulate(plan, pieces, acc):
        args = (*xs, w_in, w_out, *pieces) + (() if acc is None else (acc,))
        total = sum(width for _, _, width, _ in plan)
        return call(
            functools.partial(project_pieces_kernel, plan, acc is not None, len(pieces)),
            out_shape,
            [vmem()] * len(args),
            args,
            flops=1 << 30,
            scratch_shapes=[
                pltpu.VMEM((ki, total), jnp.bfloat16),
                pltpu.VMEM((ko, total), jnp.bfloat16),
            ],
        )

    def stacked(p):
        return tuple((p, i * shard, k) for i, k in enumerate((2, 1, 3)))

    acc = accumulate(
        ((0, 0, part, stacked(0)), (0, part, part, stacked(1))), (za, zb), None)
    acc = accumulate(
        ((1, 0, part, stacked(0)), (2, 0, part, stacked(1))), (xa, ya), acc)
    return accumulate(
        (
            (1, part, part, stacked(0)),
            (2, part, part, stacked(1)),
            (3, 0, 2 * part, ((2, 0, 2), (3, 0, 1), (3, shard, 3))),
        ),
        (xb, yb, far_op, near_op),
        acc,
    )


def per_device(
    n_groups, n_dp, n_blk, train_inputs, train_cotangents, train_lengths,
    test_inputs, test_cotangents, test_lengths, proj_in, proj_out,
):
    _, tokens, width = train_inputs.shape
    xs = [a.reshape(tokens, width) for a in (
        train_inputs, train_cotangents, test_inputs, test_cotangents)]
    part = project(xs, proj_in.T, proj_out.T, n_groups, n_dp, n_blk)
    ki = part.shape[1]
    ko = ki // 2
    other = swap(part, "mp", 2, 1)
    fac, gte, gtr = call(
        moments_kernel,
        (
            jax.ShapeDtypeStruct((ki + 8, ki), jnp.float32),
            jax.ShapeDtypeStruct((1, ki // 2, ki), jnp.float32),
            jax.ShapeDtypeStruct((ki, ko), jnp.float32),
        ),
        [smem(), smem(), vmem(), vmem()],
        (train_lengths, test_lengths, part, other),
    )
    order = [(0, 0)]
    for axis, count in (("blk", n_blk), ("dp", n_dp)):
        for k in bits(count):
            fac = fac + swap(fac, axis, count, k)
            gte = jnp.concatenate([gte, swap(gte, axis, count, k)], axis=0)
            order += [(dz ^ k, db) if axis == "dp" else (dz, db ^ k) for dz, db in order]
    side = call(
        side_kernel,
        jax.ShapeDtypeStruct((ki // 2, ki), jnp.float32),
        [vmem()] * 2,
        (fac, gtr),
        flops=4 << 30,
    )
    return call(
        functools.partial(scores_kernel, order, n_blk),
        jax.ShapeDtypeStruct((1, n_dp * n_blk), jnp.float32),
        [vmem()] * 2,
        (side, gte),
    )


def solution(mesh):
    feature = P(("groups", "dp", "blk"), None, "mp")
    length = P(("groups", "dp", "blk"))
    weight = P("mp", "dp")
    shape = mesh.shape
    return jax.shard_map(
        functools.partial(per_device, shape["groups"], shape["dp"], shape["blk"]),
        mesh=mesh,
        in_specs=(feature, feature, length, feature, feature, length, weight, weight),
        out_specs=P(("groups", "dp", "blk"), None),
        check_vma=False,
    )
```

```python
import functools

import jax
import jax.numpy as jnp
from jax import lax
from jax.experimental import pallas as pl
from jax.experimental.pallas import tpu as pltpu
from jax.sharding import PartitionSpec as P

HI = lax.Precision.HIGHEST
NT = (((1,), (1,)), ((), ()))
TN = (((0,), (0,)), ((), ()))
NEWTON_STEPS = 7
PLANE = ("groups", "blk")


def vmem():
    return pl.BlockSpec(memory_space=pltpu.VMEM)


def smem():
    return pl.BlockSpec(memory_space=pltpu.SMEM)


def call(kernel, out_shape, in_specs, args, flops=0, limit=16, **kw):
    return pl.pallas_call(
        kernel,
        out_shape=out_shape,
        in_specs=in_specs,
        out_specs=jax.tree.map(lambda _: vmem(), out_shape),
        compiler_params=pltpu.CompilerParams(vmem_limit_bytes=limit * 1024 * 1024),
        cost_estimate=pl.CostEstimate(flops=flops, bytes_accessed=1 << 16, transcendentals=0),
        **kw,
    )(*args)


def swap(x, axis, count, k):
    return lax.ppermute(x, axis, [(i, i ^ k) for i in range(count)])


def bits(count):
    return [1 << s for s in reversed(range(count.bit_length() - 1))]


def load_kernel(n, *refs):
    srcs, dsts, sem = refs[:n], refs[n : 2 * n], refs[2 * n]
    copies = []
    for i, (src, dst) in enumerate(zip(srcs, dsts)):
        rows = src.shape[0] // 2
        for h in range(2):
            part = pl.ds(h * rows, rows)
            copies.append(pltpu.make_async_copy(src.at[part], dst.at[part], sem.at[2 * i + h]))
    for c in copies:
        c.start()
    for c in copies:
        c.wait()


def stack_kernel(n, *refs):
    at = 0
    for src in refs[:n]:
        refs[-1][at : at + src.shape[0], :] = src[...]
        at += src.shape[0]


def stack(parts, after=None):
    rows = sum(p.shape[0] for p in parts)
    extra = () if after is None else (after,)
    return call(
        functools.partial(stack_kernel, len(parts)),
        pltpu.VMEM((rows, parts[0].shape[1]), parts[0].dtype),
        [vmem()] * len(parts) + [pl.BlockSpec(memory_space=pl.ANY)] * len(extra),
        (*parts, *extra),
        limit=1,
    )


def store_products(x_parts, g_parts, acc_ref, out_ref):
    tokens = out_ref.shape[0] // 3
    ko = g_parts[0].shape[1]
    for n in range(2):
        rows = slice(n * tokens, (n + 1) * tokens)
        prior = 0.0 if acc_ref is None else acc_ref[rows, :]
        out_ref[rows, :] = prior + x_parts[n]
    rows = slice(2 * tokens, 3 * tokens)
    for n in range(2):
        cols = slice(n * ko, (n + 1) * ko)
        prior = 0.0 if acc_ref is None else acc_ref[rows, cols]
        out_ref[rows, cols] = prior + g_parts[n]


def nt(a, b):
    return lax.dot_general(a, b, NT, preferred_element_type=jnp.float32)


def project_kernel(*refs):
    x_refs, (w_in, w_out, out_ref) = refs[:4], refs[4:]
    xs = [nt(x_refs[n][...], w_in[...]) for n in (0, 2)]
    gs = [nt(x_refs[n][...], w_out[...]) for n in (1, 3)]
    store_products(xs, gs, None, out_ref)


def project_pieces_kernel(plan, with_acc, n_pieces, *refs):
    x_refs, (own_in, own_out) = refs[:4], refs[4:6]
    pieces = refs[6 : 6 + n_pieces]
    acc_ref = refs[6 + n_pieces] if with_acc else None
    out_ref, w_in, w_out = refs[6 + n_pieces + with_acc :]
    z = lax.axis_index("dp")
    q = lax.axis_index(PLANE)
    rin, rout = own_in.shape[0], own_out.shape[0]
    quarter = own_in.shape[1] // 4
    xs, gs = [0.0, 0.0], [0.0, 0.0]
    at = 0
    for dq, col, width, rows in plan:
        start = pl.multiple_of((q ^ dq) * quarter + col, 128)
        cols = pl.ds(start, width)
        here = slice(at, at + width)
        at += width
        w_in[pl.ds(pl.multiple_of(z * rin, rin), rin), here] = own_in[:, cols]
        w_out[pl.ds(pl.multiple_of(z * rout, rout), rout), here] = own_out[:, cols]
        for p, row, k in rows:
            dst_in = pl.multiple_of((z ^ k) * rin, rin)
            dst_out = pl.multiple_of((z ^ k) * rout, rout)
            w_in[pl.ds(dst_in, rin), here] = pieces[p][row : row + rin, :]
            w_out[pl.ds(dst_out, rout), here] = pieces[p][row + rin : row + rin + rout, :]
        for m in range(2):
            xs[m] += nt(x_refs[2 * m][:, cols], w_in[:, here])
            gs[m] += nt(x_refs[2 * m + 1][:, cols], w_out[:, here])
    store_products(xs, gs, acc_ref, out_ref)


def moments_kernel(len_tr, len_te, mine, other, fac_ref, gte_ref, gtr_ref):
    tokens = mine.shape[0] // 3
    ki = mine.shape[1]
    ko = ki // 2
    total = mine[...] + other[...]
    rows = lax.broadcasted_iota(jnp.int32, (tokens, ki), 0)
    n_tr, n_te = len_tr[0], len_te[0]
    x_tr = jnp.where(rows < n_tr, total[:tokens], 0.0)
    x_te = jnp.where(rows < n_te, total[tokens : 2 * tokens], 0.0)
    g_both = total[2 * tokens :]
    g_tr = jnp.where(rows < n_tr, g_both, 0.0)[:, :ko]
    g_te = g_both[:, ko:]
    dot = functools.partial(
        lax.dot_general, dimension_numbers=TN, precision=HI,
        preferred_element_type=jnp.float32,
    )
    c_in = dot(x_tr, x_tr)
    c_out = dot(g_tr, g_tr)
    half = ki // 2
    fac_ref[:half, :] = c_in[:half, :]
    fac_ref[half:ki, :half] = c_in[half:, half:]
    fac_ref[half:ki, half:] = c_out
    fac_ref[ki:, :] = jnp.full((8, ki), n_tr.astype(jnp.float32))
    grad_tr = dot(x_tr, g_tr) / n_tr.astype(jnp.float32)
    grad_te = dot(x_te, g_te) / n_te.astype(jnp.float32)
    gtr_ref[...] = grad_tr
    gte_ref[0, :, :ko] = grad_te[:half]
    gte_ref[0, :, ko:] = grad_te[half:]


def damped(c):
    n = c.shape[0]
    i = lax.broadcasted_iota(jnp.int32, (n, n), 0)
    j = lax.broadcasted_iota(jnp.int32, (n, n), 1)
    eye = (i == j).astype(jnp.float32)
    trace = jnp.sum(c * eye, axis=(0, 1), keepdims=True)
    low = 0.1 * trace / n
    a = c + low * eye
    high = jnp.max(jnp.sum(jnp.abs(a), axis=0, keepdims=True), axis=1, keepdims=True)
    return a, eye, low, jnp.minimum(high, trace + low)


def mm(a, b):
    return jnp.dot(a, b, precision=HI, preferred_element_type=jnp.float32)


def inverses(matrices):
    state = []
    for c in matrices:
        a, eye, low, high = damped(c)
        scale = 2.0 / (low + high)
        r = (high - low) / (high + low)
        state.append((a, scale * a, scale * eye, r))
    for step in range(NEWTON_STEPS):
        nxt = []
        for a, m, x, r in state:
            s = 2.0 / (2.0 - r * r)
            n = m.shape[0]
            if step == 0:
                mx = s * (2.0 * m - mm(m, m))
                xx = s * (2.0 * x - x[:1, :1] * m)
            else:
                both = mm(jnp.concatenate([m, x], axis=0), m)
                mx = s * (2.0 * m - both[:n])
                xx = s * (2.0 * x - both[n:])
            nxt.append((a, mx, xx, r * r / (2.0 - r * r)))
        state = nxt
    return [2.0 * x - mm(x, mm(a, x)) for a, m, x, r in state]


def side_kernel(fac_ref, gtr_ref, out_ref):
    ki = fac_ref.shape[1]
    half = ki // 2
    top = fac_ref[:half, :]
    low = fac_ref[half:ki, :]
    c_in = jnp.concatenate(
        [top, jnp.concatenate([top[:, half:].T, low[:, :half]], axis=1)], axis=0
    )
    count = fac_ref[ki : ki + 1, :1]
    inv_in, inv_out = inverses([c_in, low[:, half:]])
    side = mm(mm(inv_in, gtr_ref[...]), inv_out) * (count * count)
    out_ref[:, :half] = side[:half]
    out_ref[:, half:] = side[half:]


def scores_kernel(order, n_blk, side_ref, gte_ref, out_ref):
    z = lax.axis_index("dp")
    b = lax.axis_index("blk")
    lane = lax.broadcasted_iota(jnp.int32, out_ref.shape, 1)
    row = jnp.zeros(out_ref.shape, jnp.float32)
    side = side_ref[...]
    sums = [jnp.sum(side * gte_ref[p], axis=0, keepdims=True) for p in range(len(order))]
    values = jnp.sum(jnp.concatenate(sums, axis=0), axis=1, keepdims=True)
    for p, (dz, db) in enumerate(order):
        row = jnp.where(lane == (z ^ dz) * n_blk + (b ^ db), values[p : p + 1, :], row)
    out_ref[...] = row


def project(xs, w_in, w_out, n_groups, n_dp, n_blk):
    tokens, width = xs[0].shape
    rin, rout = w_in.shape[0], w_out.shape[0]
    ki, ko = rin * n_dp, rout * n_dp
    out_shape = jax.ShapeDtypeStruct((3 * tokens, ki), jnp.float32)
    if (n_groups, n_dp, n_blk) != (2, 4, 2):
        w_in = lax.all_gather(w_in, "dp", axis=0, tiled=True)
        w_out = lax.all_gather(w_out, "dp", axis=0, tiled=True)
        return call(project_kernel, out_shape, [vmem()] * 6, (*xs, w_in, w_out))

    part = width // 8
    shard = rin + rout
    q = lax.axis_index(PLANE)
    whole = jnp.concatenate([w_in, w_out], axis=0)
    mine = lax.dynamic_slice(whole, (0, q * 2 * part), (shard, 2 * part))
    opposite = lax.dynamic_slice(whole, (0, (q ^ 3) * 2 * part), (shard, 2 * part))
    operands = (*xs, w_in, w_out)
    *xs, w_in, w_out = call(
        functools.partial(load_kernel, 6),
        tuple(pltpu.VMEM(x.shape, x.dtype) for x in operands),
        [pl.BlockSpec(memory_space=pltpu.HBM)] * 6,
        [pltpu.with_memory_space_constraint(x, pltpu.HBM) for x in operands],
        flops=1 << 30,
        scratch_shapes=[pltpu.SemaphoreType.DMA((12,))],
    )
    halves = [mine[:, :part], mine[:, part:]]
    far = [swap(h, "dp", n_dp, 2) for h in halves]
    far_op = swap(opposite, "dp", n_dp, 2)
    both_a = stack((halves[0], far[0]), w_out)
    near_a = swap(both_a, "dp", n_dp, 1)
    both_b = stack((halves[1], far[1]))
    near_b = swap(both_b, "dp", n_dp, 1)
    za = stack((far[0], near_a))
    xa, ya = swap(za, PLANE, 4, 1), swap(za, PLANE, 4, 2)
    both_op = stack((opposite, far_op))
    near_op = swap(both_op, "dp", n_dp, 1)
    zb = stack((far[1], near_b))
    xb, yb = swap(zb, PLANE, 4, 1), swap(zb, PLANE, 4, 2)

    def accumulate(plan, pieces, acc):
        args = (*xs, w_in, w_out, *pieces) + (() if acc is None else (acc,))
        total = sum(width for _, _, width, _ in plan)
        return call(
            functools.partial(project_pieces_kernel, plan, acc is not None, len(pieces)),
            out_shape,
            [vmem()] * len(args),
            args,
            flops=1 << 30,
            scratch_shapes=[
                pltpu.VMEM((ki, total), jnp.bfloat16),
                pltpu.VMEM((ko, total), jnp.bfloat16),
            ],
        )

    def stacked(p):
        return tuple((p, i * shard, k) for i, k in enumerate((2, 1, 3)))

    acc = accumulate(
        ((0, 0, part, stacked(0)), (0, part, part, stacked(1))), (za, zb), None)
    acc = accumulate(
        ((1, 0, part, stacked(0)), (2, 0, part, stacked(1))), (xa, ya), acc)
    return accumulate(
        (
            (1, part, part, stacked(0)),
            (2, part, part, stacked(1)),
            (3, 0, 2 * part, ((2, 0, 2), (3, 0, 1), (3, shard, 3))),
        ),
        (xb, yb, far_op, near_op),
        acc,
    )


def per_device(
    n_groups, n_dp, n_blk, train_inputs, train_cotangents, train_lengths,
    test_inputs, test_cotangents, test_lengths, proj_in, proj_out,
):
    _, tokens, width = train_inputs.shape
    xs = [a.reshape(tokens, width) for a in (
        train_inputs, train_cotangents, test_inputs, test_cotangents)]
    part = project(xs, proj_in.T, proj_out.T, n_groups, n_dp, n_blk)
    ki = part.shape[1]
    ko = ki // 2
    other = swap(part, "mp", 2, 1)
    fac, gte, gtr = call(
        moments_kernel,
        (
            jax.ShapeDtypeStruct((ki + 8, ki), jnp.float32),
            jax.ShapeDtypeStruct((1, ki // 2, ki), jnp.float32),
            jax.ShapeDtypeStruct((ki, ko), jnp.float32),
        ),
        [smem(), smem(), vmem(), vmem()],
        (train_lengths, test_lengths, part, other),
    )
    order = [(0, 0)]
    for axis, count in (("dp", n_dp), ("blk", n_blk)):
        for k in bits(count):
            gte = jnp.concatenate([gte, swap(gte, axis, count, k)], axis=0)
            order += [(dz ^ k, db) if axis == "dp" else (dz, db ^ k) for dz, db in order]
    for axis, count in (("blk", n_blk), ("dp", n_dp)):
        for k in bits(count):
            fac = fac + swap(fac, axis, count, k)
    side = call(
        side_kernel,
        jax.ShapeDtypeStruct((ki // 2, ki), jnp.float32),
        [vmem()] * 2,
        (fac, gtr),
        flops=4 << 30,
    )
    return call(
        functools.partial(scores_kernel, order, n_blk),
        jax.ShapeDtypeStruct((1, n_dp * n_blk), jnp.float32),
        [vmem()] * 2,
        (side, gte),
    )


def solution(mesh):
    feature = P(("groups", "dp", "blk"), None, "mp")
    length = P(("groups", "dp", "blk"))
    weight = P("mp", "dp")
    shape = mesh.shape
    return jax.shard_map(
        functools.partial(per_device, shape["groups"], shape["dp"], shape["blk"]),
        mesh=mesh,
        in_specs=(feature, feature, length, feature, feature, length, weight, weight),
        out_specs=P(("groups", "dp", "blk"), None),
        check_vma=False,
    )
```

```python
import functools

import jax
import jax.numpy as jnp
from jax import lax
from jax.experimental import pallas as pl
from jax.experimental.pallas import tpu as pltpu
from jax.sharding import PartitionSpec as P

HI = lax.Precision.HIGHEST
NT = (((1,), (1,)), ((), ()))
TN = (((0,), (0,)), ((), ()))
NEWTON_STEPS = 7
PLANE = ("groups", "blk")


def vmem():
    return pl.BlockSpec(memory_space=pltpu.VMEM)


def smem():
    return pl.BlockSpec(memory_space=pltpu.SMEM)


def call(kernel, out_shape, in_specs, args, flops=0, limit=16, **kw):
    return pl.pallas_call(
        kernel,
        out_shape=out_shape,
        in_specs=in_specs,
        out_specs=jax.tree.map(lambda _: vmem(), out_shape),
        compiler_params=pltpu.CompilerParams(vmem_limit_bytes=limit * 1024 * 1024),
        cost_estimate=pl.CostEstimate(flops=flops, bytes_accessed=1 << 16, transcendentals=0),
        **kw,
    )(*args)


def swap(x, axis, count, k):
    return lax.ppermute(x, axis, [(i, i ^ k) for i in range(count)])


def swap_on(x, axis, count, k, core):
    pairs = [(2 * i + core, 2 * (i ^ k) + core) for i in range(count)]
    return lax.ppermute(x, (axis, "mp"), pairs)


def bits(count):
    return [1 << s for s in reversed(range(count.bit_length() - 1))]


def load_kernel(n, *refs):
    srcs, dsts, sem = refs[:n], refs[n : 2 * n], refs[2 * n]
    copies = []
    for i, (src, dst) in enumerate(zip(srcs, dsts)):
        rows = src.shape[0] // 2
        for h in range(2):
            part = pl.ds(h * rows, rows)
            copies.append(pltpu.make_async_copy(src.at[part], dst.at[part], sem.at[2 * i + h]))
    for c in copies:
        c.start()
    for c in copies:
        c.wait()


def stack_kernel(n, *refs):
    at = 0
    for src in refs[:n]:
        refs[-1][at : at + src.shape[0], :] = src[...]
        at += src.shape[0]


def stack(parts, after=None):
    rows = sum(p.shape[0] for p in parts)
    extra = () if after is None else (after,)
    return call(
        functools.partial(stack_kernel, len(parts)),
        pltpu.VMEM((rows, parts[0].shape[1]), parts[0].dtype),
        [vmem()] * len(parts) + [pl.BlockSpec(memory_space=pl.ANY)] * len(extra),
        (*parts, *extra),
        limit=1,
    )


def store_products(x_parts, g_parts, acc_ref, out_ref):
    tokens = out_ref.shape[0] // 3
    ko = g_parts[0].shape[1]
    for n in range(2):
        rows = slice(n * tokens, (n + 1) * tokens)
        prior = 0.0 if acc_ref is None else acc_ref[rows, :]
        out_ref[rows, :] = prior + x_parts[n]
    rows = slice(2 * tokens, 3 * tokens)
    for n in range(2):
        cols = slice(n * ko, (n + 1) * ko)
        prior = 0.0 if acc_ref is None else acc_ref[rows, cols]
        out_ref[rows, cols] = prior + g_parts[n]


def nt(a, b):
    return lax.dot_general(a, b, NT, preferred_element_type=jnp.float32)


def project_kernel(*refs):
    x_refs, (w_in, w_out, out_ref) = refs[:4], refs[4:]
    xs = [nt(x_refs[n][...], w_in[...]) for n in (0, 2)]
    gs = [nt(x_refs[n][...], w_out[...]) for n in (1, 3)]
    store_products(xs, gs, None, out_ref)


def project_pieces_kernel(plan, with_acc, n_pieces, *refs):
    x_refs, (own_in, own_out) = refs[:4], refs[4:6]
    pieces = refs[6 : 6 + n_pieces]
    acc_ref = refs[6 + n_pieces] if with_acc else None
    out_ref, w_in, w_out = refs[6 + n_pieces + with_acc :]
    z = lax.axis_index("dp")
    q = lax.axis_index(PLANE)
    rin, rout = own_in.shape[0], own_out.shape[0]
    quarter = own_in.shape[1] // 4
    xs, gs = [0.0, 0.0], [0.0, 0.0]
    at = 0
    for dq, col, width, rows in plan:
        start = pl.multiple_of((q ^ dq) * quarter + col, 128)
        cols = pl.ds(start, width)
        here = slice(at, at + width)
        at += width
        w_in[pl.ds(pl.multiple_of(z * rin, rin), rin), here] = own_in[:, cols]
        w_out[pl.ds(pl.multiple_of(z * rout, rout), rout), here] = own_out[:, cols]
        for p, row, k in rows:
            dst_in = pl.multiple_of((z ^ k) * rin, rin)
            dst_out = pl.multiple_of((z ^ k) * rout, rout)
            w_in[pl.ds(dst_in, rin), here] = pieces[p][row : row + rin, :]
            w_out[pl.ds(dst_out, rout), here] = pieces[p][row + rin : row + rin + rout, :]
        for m in range(2):
            xs[m] += nt(x_refs[2 * m][:, cols], w_in[:, here])
            gs[m] += nt(x_refs[2 * m + 1][:, cols], w_out[:, here])
    store_products(xs, gs, acc_ref, out_ref)


def moments_kernel(len_tr, len_te, mine, other, fac_ref, gte_ref, gtr_ref):
    tokens = mine.shape[0] // 3
    ki = mine.shape[1]
    ko = ki // 2
    total = mine[...] + other[...]
    rows = lax.broadcasted_iota(jnp.int32, (tokens, ki), 0)
    n_tr, n_te = len_tr[0], len_te[0]
    x_tr = jnp.where(rows < n_tr, total[:tokens], 0.0)
    x_te = jnp.where(rows < n_te, total[tokens : 2 * tokens], 0.0)
    g_both = total[2 * tokens :]
    g_tr = jnp.where(rows < n_tr, g_both, 0.0)[:, :ko]
    g_te = g_both[:, ko:]
    dot = functools.partial(
        lax.dot_general, dimension_numbers=TN, precision=HI,
        preferred_element_type=jnp.float32,
    )
    c_in = dot(x_tr, x_tr)
    c_out = dot(g_tr, g_tr)
    half = ki // 2
    fac_ref[:half, :] = c_in[:half, :]
    fac_ref[half:ki, :half] = c_in[half:, half:]
    fac_ref[half:ki, half:] = c_out
    fac_ref[ki:, :] = jnp.full((8, ki), n_tr.astype(jnp.float32))
    grad_tr = dot(x_tr, g_tr) / n_tr.astype(jnp.float32)
    grad_te = dot(x_te, g_te) / n_te.astype(jnp.float32)
    gtr_ref[...] = grad_tr
    gte_ref[0, :, :ko] = grad_te[:half]
    gte_ref[0, :, ko:] = grad_te[half:]


def damped(c):
    n = c.shape[0]
    i = lax.broadcasted_iota(jnp.int32, (n, n), 0)
    j = lax.broadcasted_iota(jnp.int32, (n, n), 1)
    eye = (i == j).astype(jnp.float32)
    trace = jnp.sum(c * eye, axis=(0, 1), keepdims=True)
    low = 0.1 * trace / n
    a = c + low * eye
    high = jnp.max(jnp.sum(jnp.abs(a), axis=0, keepdims=True), axis=1, keepdims=True)
    return a, eye, low, jnp.minimum(high, trace + low)


def mm(a, b):
    return jnp.dot(a, b, precision=HI, preferred_element_type=jnp.float32)


def inverses(matrices):
    state = []
    for c in matrices:
        a, eye, low, high = damped(c)
        scale = 2.0 / (low + high)
        r = (high - low) / (high + low)
        state.append((a, scale * a, scale * eye, r))
    for step in range(NEWTON_STEPS):
        nxt = []
        for a, m, x, r in state:
            s = 2.0 / (2.0 - r * r)
            n = m.shape[0]
            if step == 0:
                mx = s * (2.0 * m - mm(m, m))
                xx = s * (2.0 * x - x[:1, :1] * m)
            else:
                both = mm(jnp.concatenate([m, x], axis=0), m)
                mx = s * (2.0 * m - both[:n])
                xx = s * (2.0 * x - both[n:])
            nxt.append((a, mx, xx, r * r / (2.0 - r * r)))
        state = nxt
    return [2.0 * x - mm(x, mm(a, x)) for a, m, x, r in state]


def side_kernel(fac_ref, other_ref, gtr_ref, out_ref):
    ki = fac_ref.shape[1]
    half = ki // 2
    total = jnp.where(lax.axis_index("mp") == 0, fac_ref[...], other_ref[...])
    top = total[:half]
    low = total[half:ki]
    c_in = jnp.concatenate(
        [top, jnp.concatenate([top[:, half:].T, low[:, :half]], axis=1)], axis=0
    )
    count = total[ki : ki + 1, :1]
    inv_in, inv_out = inverses([c_in, low[:, half:]])
    side = mm(mm(inv_in, gtr_ref[...]), inv_out) * (count * count)
    out_ref[:, :half] = side[:half]
    out_ref[:, half:] = side[half:]


def scores_kernel(order, n_blk, side_ref, gte_ref, other_ref, out_ref):
    z = lax.axis_index("dp")
    b = lax.axis_index("blk")
    lane = lax.broadcasted_iota(jnp.int32, out_ref.shape, 1)
    row = jnp.zeros(out_ref.shape, jnp.float32)
    side = side_ref[...]
    own = lax.axis_index("mp") == 1
    sums = [
        jnp.sum(side * jnp.where(own, gte_ref[p], other_ref[p]), axis=0, keepdims=True)
        for p in range(len(order))
    ]
    values = jnp.sum(jnp.concatenate(sums, axis=0), axis=1, keepdims=True)
    for p, (dz, db) in enumerate(order):
        row = jnp.where(lane == (z ^ dz) * n_blk + (b ^ db), values[p : p + 1, :], row)
    out_ref[...] = row


def project(xs, w_in, w_out, n_groups, n_dp, n_blk):
    tokens, width = xs[0].shape
    rin, rout = w_in.shape[0], w_out.shape[0]
    ki, ko = rin * n_dp, rout * n_dp
    out_shape = jax.ShapeDtypeStruct((3 * tokens, ki), jnp.float32)
    if (n_groups, n_dp, n_blk) != (2, 4, 2):
        w_in = lax.all_gather(w_in, "dp", axis=0, tiled=True)
        w_out = lax.all_gather(w_out, "dp", axis=0, tiled=True)
        return call(project_kernel, out_shape, [vmem()] * 6, (*xs, w_in, w_out))

    part = width // 8
    shard = rin + rout
    q = lax.axis_index(PLANE)
    whole = jnp.concatenate([w_in, w_out], axis=0)
    mine = lax.dynamic_slice(whole, (0, q * 2 * part), (shard, 2 * part))
    opposite = lax.dynamic_slice(whole, (0, (q ^ 3) * 2 * part), (shard, 2 * part))
    operands = (*xs, w_in, w_out)
    *xs, w_in, w_out = call(
        functools.partial(load_kernel, 6),
        tuple(pltpu.VMEM(x.shape, x.dtype) for x in operands),
        [pl.BlockSpec(memory_space=pltpu.HBM)] * 6,
        [pltpu.with_memory_space_constraint(x, pltpu.HBM) for x in operands],
        flops=1 << 30,
        scratch_shapes=[pltpu.SemaphoreType.DMA((12,))],
    )
    halves = [mine[:, :part], mine[:, part:]]
    far = [swap(h, "dp", n_dp, 2) for h in halves]
    far_op = swap(opposite, "dp", n_dp, 2)
    both_a = stack((halves[0], far[0]), w_out)
    near_a = swap(both_a, "dp", n_dp, 1)
    both_b = stack((halves[1], far[1]))
    near_b = swap(both_b, "dp", n_dp, 1)
    za = stack((far[0], near_a))
    xa, ya = swap(za, PLANE, 4, 1), swap(za, PLANE, 4, 2)
    both_op = stack((opposite, far_op))
    near_op = swap(both_op, "dp", n_dp, 1)
    zb = stack((far[1], near_b))
    xb, yb = swap(zb, PLANE, 4, 1), swap(zb, PLANE, 4, 2)

    def accumulate(plan, pieces, acc):
        args = (*xs, w_in, w_out, *pieces) + (() if acc is None else (acc,))
        total = sum(width for _, _, width, _ in plan)
        return call(
            functools.partial(project_pieces_kernel, plan, acc is not None, len(pieces)),
            out_shape,
            [vmem()] * len(args),
            args,
            flops=1 << 30,
            scratch_shapes=[
                pltpu.VMEM((ki, total), jnp.bfloat16),
                pltpu.VMEM((ko, total), jnp.bfloat16),
            ],
        )

    def stacked(p):
        return tuple((p, i * shard, k) for i, k in enumerate((2, 1, 3)))

    acc = accumulate(
        ((0, 0, part, stacked(0)), (0, part, part, stacked(1))), (za, zb), None)
    acc = accumulate(
        ((1, 0, part, stacked(0)), (2, 0, part, stacked(1))), (xa, ya), acc)
    return accumulate(
        (
            (1, part, part, stacked(0)),
            (2, part, part, stacked(1)),
            (3, 0, 2 * part, ((2, 0, 2), (3, 0, 1), (3, shard, 3))),
        ),
        (xb, yb, far_op, near_op),
        acc,
    )


def per_device(
    n_groups, n_dp, n_blk, train_inputs, train_cotangents, train_lengths,
    test_inputs, test_cotangents, test_lengths, proj_in, proj_out,
):
    _, tokens, width = train_inputs.shape
    xs = [a.reshape(tokens, width) for a in (
        train_inputs, train_cotangents, test_inputs, test_cotangents)]
    part = project(xs, proj_in.T, proj_out.T, n_groups, n_dp, n_blk)
    ki = part.shape[1]
    ko = ki // 2
    other = swap(part, "mp", 2, 1)
    fac, gte, gtr = call(
        moments_kernel,
        (
            jax.ShapeDtypeStruct((ki + 8, ki), jnp.float32),
            jax.ShapeDtypeStruct((1, ki // 2, ki), jnp.float32),
            jax.ShapeDtypeStruct((ki, ko), jnp.float32),
        ),
        [smem(), smem(), vmem(), vmem()],
        (train_lengths, test_lengths, part, other),
    )
    order = [(0, 0)]
    for axis, count in (("dp", n_dp), ("blk", n_blk)):
        for k in bits(count):
            gte = jnp.concatenate([gte, swap_on(gte, axis, count, k, 1)], axis=0)
            order += [(dz ^ k, db) if axis == "dp" else (dz, db ^ k) for dz, db in order]
    for axis, count in (("blk", n_blk), ("dp", n_dp)):
        for k in bits(count):
            fac = fac + swap_on(fac, axis, count, k, 0)
    fac_other = lax.ppermute(fac, "mp", [(0, 1)])
    gte_other = lax.ppermute(gte, "mp", [(1, 0)])
    side = call(
        side_kernel,
        jax.ShapeDtypeStruct((ki // 2, ki), jnp.float32),
        [vmem()] * 3,
        (fac, fac_other, gtr),
        flops=4 << 30,
    )
    return call(
        functools.partial(scores_kernel, order, n_blk),
        jax.ShapeDtypeStruct((1, n_dp * n_blk), jnp.float32),
        [vmem()] * 3,
        (side, gte, gte_other),
    )


def solution(mesh):
    feature = P(("groups", "dp", "blk"), None, "mp")
    length = P(("groups", "dp", "blk"))
    weight = P("mp", "dp")
    shape = mesh.shape
    return jax.shard_map(
        functools.partial(per_device, shape["groups"], shape["dp"], shape["blk"]),
        mesh=mesh,
        in_specs=(feature, feature, length, feature, feature, length, weight, weight),
        out_specs=P(("groups", "dp", "blk"), None),
        check_vma=False,
    )
```

```python
import functools

import jax
import jax.numpy as jnp
from jax import lax
from jax.experimental import pallas as pl
from jax.experimental.pallas import tpu as pltpu
from jax.sharding import PartitionSpec as P

HI = lax.Precision.HIGHEST
NT = (((1,), (1,)), ((), ()))
TN = (((0,), (0,)), ((), ()))
NEWTON_STEPS = 7
PLANE = ("groups", "blk")


def vmem():
    return pl.BlockSpec(memory_space=pltpu.VMEM)


def smem():
    return pl.BlockSpec(memory_space=pltpu.SMEM)


def call(kernel, out_shape, in_specs, args, flops=0, limit=16, **kw):
    return pl.pallas_call(
        kernel,
        out_shape=out_shape,
        in_specs=in_specs,
        out_specs=jax.tree.map(lambda _: vmem(), out_shape),
        compiler_params=pltpu.CompilerParams(vmem_limit_bytes=limit * 1024 * 1024),
        cost_estimate=pl.CostEstimate(flops=flops, bytes_accessed=1 << 16, transcendentals=0),
        **kw,
    )(*args)


def swap(x, axis, count, k):
    return lax.ppermute(x, axis, [(i, i ^ k) for i in range(count)])


def bits(count):
    return [1 << s for s in reversed(range(count.bit_length() - 1))]


def load_kernel(n, *refs):
    srcs, dsts, sem = refs[:n], refs[n : 2 * n], refs[2 * n]
    copies = []
    for i, (src, dst) in enumerate(zip(srcs, dsts)):
        rows = src.shape[0] // 2
        for h in range(2):
            part = pl.ds(h * rows, rows)
            copies.append(pltpu.make_async_copy(src.at[part], dst.at[part], sem.at[2 * i + h]))
    for c in copies:
        c.start()
    for c in copies:
        c.wait()


def stack_kernel(n, *refs):
    at = 0
    for src in refs[:n]:
        refs[-1][at : at + src.shape[0], :] = src[...]
        at += src.shape[0]


def stack(parts, after=None):
    rows = sum(p.shape[0] for p in parts)
    extra = () if after is None else (after,)
    return call(
        functools.partial(stack_kernel, len(parts)),
        pltpu.VMEM((rows, parts[0].shape[1]), parts[0].dtype),
        [vmem()] * len(parts) + [pl.BlockSpec(memory_space=pl.ANY)] * len(extra),
        (*parts, *extra),
        limit=1,
    )


def store_products(x_parts, g_parts, acc_ref, out_ref):
    tokens = out_ref.shape[0] // 3
    ko = g_parts[0].shape[1]
    for n in range(2):
        rows = slice(n * tokens, (n + 1) * tokens)
        prior = 0.0 if acc_ref is None else acc_ref[rows, :]
        out_ref[rows, :] = prior + x_parts[n]
    rows = slice(2 * tokens, 3 * tokens)
    for n in range(2):
        cols = slice(n * ko, (n + 1) * ko)
        prior = 0.0 if acc_ref is None else acc_ref[rows, cols]
        out_ref[rows, cols] = prior + g_parts[n]


def nt(a, b):
    return lax.dot_general(a, b, NT, preferred_element_type=jnp.float32)


def project_kernel(*refs):
    x_refs, (w_in, w_out, out_ref) = refs[:4], refs[4:]
    xs = [nt(x_refs[n][...], w_in[...]) for n in (0, 2)]
    gs = [nt(x_refs[n][...], w_out[...]) for n in (1, 3)]
    store_products(xs, gs, None, out_ref)


def project_pieces_kernel(plan, with_acc, n_pieces, *refs):
    x_refs, (own_in, own_out) = refs[:4], refs[4:6]
    pieces = refs[6 : 6 + n_pieces]
    acc_ref = refs[6 + n_pieces] if with_acc else None
    out_ref, w_in, w_out = refs[6 + n_pieces + with_acc :]
    z = lax.axis_index("dp")
    q = lax.axis_index(PLANE)
    rin, rout = own_in.shape[0], own_out.shape[0]
    quarter = own_in.shape[1] // 4
    xs, gs = [0.0, 0.0], [0.0, 0.0]
    at = 0
    for dq, col, width, rows in plan:
        start = pl.multiple_of((q ^ dq) * quarter + col, 128)
        cols = pl.ds(start, width)
        here = slice(at, at + width)
        at += width
        w_in[pl.ds(pl.multiple_of(z * rin, rin), rin), here] = own_in[:, cols]
        w_out[pl.ds(pl.multiple_of(z * rout, rout), rout), here] = own_out[:, cols]
        for p, row, k in rows:
            dst_in = pl.multiple_of((z ^ k) * rin, rin)
            dst_out = pl.multiple_of((z ^ k) * rout, rout)
            w_in[pl.ds(dst_in, rin), here] = pieces[p][row : row + rin, :]
            w_out[pl.ds(dst_out, rout), here] = pieces[p][row + rin : row + rin + rout, :]
        for m in range(2):
            xs[m] += nt(x_refs[2 * m][:, cols], w_in[:, here])
            gs[m] += nt(x_refs[2 * m + 1][:, cols], w_out[:, here])
    store_products(xs, gs, acc_ref, out_ref)


def moments_kernel(len_tr, len_te, mine, other, fac_ref, gte_ref, gtr_ref):
    tokens = mine.shape[0] // 3
    ki = mine.shape[1]
    ko = ki // 2
    total = mine[...] + other[...]
    rows = lax.broadcasted_iota(jnp.int32, (tokens, ki), 0)
    n_tr, n_te = len_tr[0], len_te[0]
    x_tr = jnp.where(rows < n_tr, total[:tokens], 0.0)
    x_te = jnp.where(rows < n_te, total[tokens : 2 * tokens], 0.0)
    g_both = total[2 * tokens :]
    g_tr = jnp.where(rows < n_tr, g_both, 0.0)[:, :ko]
    g_te = g_both[:, ko:]
    dot = functools.partial(
        lax.dot_general, dimension_numbers=TN, precision=HI,
        preferred_element_type=jnp.float32,
    )
    c_in = dot(x_tr, x_tr)
    c_out = dot(g_tr, g_tr)
    half = ki // 2
    fac_ref[:half, :] = c_in[:half, :]
    fac_ref[half:ki, :half] = c_in[half:, half:]
    fac_ref[half:ki, half:] = c_out
    grad_tr = dot(x_tr, g_tr) / n_tr.astype(jnp.float32)
    grad_te = dot(x_te, g_te) / n_te.astype(jnp.float32)
    gtr_ref[...] = grad_tr
    gte_ref[0, :half, :ko] = grad_te[:half]
    gte_ref[0, :half, ko:] = grad_te[half:]
    gte_ref[0, half:, :] = jnp.full((8, ki), n_tr.astype(jnp.float32))


def damped(c):
    n = c.shape[0]
    i = lax.broadcasted_iota(jnp.int32, (n, n), 0)
    j = lax.broadcasted_iota(jnp.int32, (n, n), 1)
    eye = (i == j).astype(jnp.float32)
    trace = jnp.sum(c * eye, axis=(0, 1), keepdims=True)
    low = 0.1 * trace / n
    a = c + low * eye
    high = jnp.max(jnp.sum(jnp.abs(a), axis=0, keepdims=True), axis=1, keepdims=True)
    return a, eye, low, jnp.minimum(high, trace + low)


def mm(a, b):
    return jnp.dot(a, b, precision=HI, preferred_element_type=jnp.float32)


def inverses(matrices):
    state = []
    for c in matrices:
        a, eye, low, high = damped(c)
        scale = 2.0 / (low + high)
        r = (high - low) / (high + low)
        state.append((a, scale * a, scale * eye, r))
    for step in range(NEWTON_STEPS):
        nxt = []
        for a, m, x, r in state:
            s = 2.0 / (2.0 - r * r)
            n = m.shape[0]
            if step == 0:
                mx = s * (2.0 * m - mm(m, m))
                xx = s * (2.0 * x - x[:1, :1] * m)
            else:
                both = mm(jnp.concatenate([m, x], axis=0), m)
                mx = s * (2.0 * m - both[:n])
                xx = s * (2.0 * x - both[n:])
            nxt.append((a, mx, xx, r * r / (2.0 - r * r)))
        state = nxt
    return [2.0 * x - mm(x, mm(a, x)) for a, m, x, r in state]


def side_kernel(fac_ref, gtr_ref, out_ref):
    ki = fac_ref.shape[1]
    half = ki // 2
    top = fac_ref[:half, :]
    low = fac_ref[half:ki, :]
    c_in = jnp.concatenate(
        [top, jnp.concatenate([top[:, half:].T, low[:, :half]], axis=1)], axis=0
    )
    inv_in, inv_out = inverses([c_in, low[:, half:]])
    side = mm(mm(inv_in, gtr_ref[...]), inv_out)
    out_ref[:, :half] = side[:half]
    out_ref[:, half:] = side[half:]


def scores_kernel(side_ref, gte_ref, out_ref):
    lane = lax.broadcasted_iota(jnp.int32, out_ref.shape, 1)
    row = jnp.zeros(out_ref.shape, jnp.float32)
    side = side_ref[...]
    half, peers = side.shape[0], gte_ref.shape[0]
    sums = [jnp.sum(side * gte_ref[p, :half], axis=0, keepdims=True) for p in range(peers)]
    values = jnp.sum(jnp.concatenate(sums, axis=0), axis=1, keepdims=True)
    count = gte_ref[0, half : half + 1, :1]
    for p in range(1, peers):
        count += gte_ref[p, half : half + 1, :1]
    for p in range(peers):
        row = jnp.where(lane == p, values[p : p + 1, :], row)
    out_ref[...] = row * (count * count)


def project(xs, w_in, w_out, n_groups, n_dp, n_blk):
    tokens, width = xs[0].shape
    rin, rout = w_in.shape[0], w_out.shape[0]
    ki, ko = rin * n_dp, rout * n_dp
    out_shape = jax.ShapeDtypeStruct((3 * tokens, ki), jnp.float32)
    if (n_groups, n_dp, n_blk) != (2, 4, 2):
        w_in = lax.all_gather(w_in, "dp", axis=0, tiled=True)
        w_out = lax.all_gather(w_out, "dp", axis=0, tiled=True)
        return call(project_kernel, out_shape, [vmem()] * 6, (*xs, w_in, w_out))

    part = width // 8
    shard = rin + rout
    q = lax.axis_index(PLANE)
    whole = jnp.concatenate([w_in, w_out], axis=0)
    mine = lax.dynamic_slice(whole, (0, q * 2 * part), (shard, 2 * part))
    opposite = lax.dynamic_slice(whole, (0, (q ^ 3) * 2 * part), (shard, 2 * part))
    operands = (*xs, w_in, w_out)
    *xs, w_in, w_out = call(
        functools.partial(load_kernel, 6),
        tuple(pltpu.VMEM(x.shape, x.dtype) for x in operands),
        [pl.BlockSpec(memory_space=pltpu.HBM)] * 6,
        [pltpu.with_memory_space_constraint(x, pltpu.HBM) for x in operands],
        flops=1 << 30,
        scratch_shapes=[pltpu.SemaphoreType.DMA((12,))],
    )
    halves = [mine[:, :part], mine[:, part:]]
    far = [swap(h, "dp", n_dp, 2) for h in halves]
    far_op = swap(opposite, "dp", n_dp, 2)
    both_a = stack((halves[0], far[0]), w_out)
    near_a = swap(both_a, "dp", n_dp, 1)
    both_b = stack((halves[1], far[1]))
    near_b = swap(both_b, "dp", n_dp, 1)
    za = stack((far[0], near_a))
    xa, ya = swap(za, PLANE, 4, 1), swap(za, PLANE, 4, 2)
    both_op = stack((opposite, far_op))
    near_op = swap(both_op, "dp", n_dp, 1)
    zb = stack((far[1], near_b))
    xb, yb = swap(zb, PLANE, 4, 1), swap(zb, PLANE, 4, 2)

    def accumulate(plan, pieces, acc):
        args = (*xs, w_in, w_out, *pieces) + (() if acc is None else (acc,))
        total = sum(width for _, _, width, _ in plan)
        return call(
            functools.partial(project_pieces_kernel, plan, acc is not None, len(pieces)),
            out_shape,
            [vmem()] * len(args),
            args,
            flops=1 << 30,
            scratch_shapes=[
                pltpu.VMEM((ki, total), jnp.bfloat16),
                pltpu.VMEM((ko, total), jnp.bfloat16),
            ],
        )

    def stacked(p):
        return tuple((p, i * shard, k) for i, k in enumerate((2, 1, 3)))

    acc = accumulate(
        ((0, 0, part, stacked(0)), (0, part, part, stacked(1))), (za, zb), None)
    acc = accumulate(
        ((1, 0, part, stacked(0)), (2, 0, part, stacked(1))), (xa, ya), acc)
    return accumulate(
        (
            (1, part, part, stacked(0)),
            (2, part, part, stacked(1)),
            (3, 0, 2 * part, ((2, 0, 2), (3, 0, 1), (3, shard, 3))),
        ),
        (xb, yb, far_op, near_op),
        acc,
    )


def per_device(
    n_groups, n_dp, n_blk, train_inputs, train_cotangents, train_lengths,
    test_inputs, test_cotangents, test_lengths, proj_in, proj_out,
):
    _, tokens, width = train_inputs.shape
    xs = [a.reshape(tokens, width) for a in (
        train_inputs, train_cotangents, test_inputs, test_cotangents)]
    part = project(xs, proj_in.T, proj_out.T, n_groups, n_dp, n_blk)
    ki = part.shape[1]
    ko = ki // 2
    other = swap(part, "mp", 2, 1)
    fac, gte, gtr = call(
        moments_kernel,
        (
            jax.ShapeDtypeStruct((ki, ki), jnp.float32),
            jax.ShapeDtypeStruct((1, ki // 2 + 8, ki), jnp.float32),
            jax.ShapeDtypeStruct((ki, ko), jnp.float32),
        ),
        [smem(), smem(), vmem(), vmem()],
        (train_lengths, test_lengths, part, other),
    )
    count = n_dp * n_blk
    peers = ("dp", "blk")
    slices = lax.all_to_all(fac.reshape(count, ki // count, ki), peers, 0, 0, tiled=True)
    mine = jnp.broadcast_to(jnp.sum(slices, axis=0, keepdims=True), slices.shape)
    fac = lax.all_to_all(mine, peers, 0, 0, tiled=True).reshape(ki, ki)
    gte = lax.all_to_all(jnp.broadcast_to(gte, (count, *gte.shape[1:])), peers, 0, 0, tiled=True)
    side = call(
        side_kernel,
        jax.ShapeDtypeStruct((ki // 2, ki), jnp.float32),
        [vmem()] * 2,
        (fac, gtr),
        flops=4 << 30,
    )
    return call(
        scores_kernel,
        jax.ShapeDtypeStruct((1, n_dp * n_blk), jnp.float32),
        [vmem()] * 2,
        (side, gte),
    )


def solution(mesh):
    feature = P(("groups", "dp", "blk"), None, "mp")
    length = P(("groups", "dp", "blk"))
    weight = P("mp", "dp")
    shape = mesh.shape
    return jax.shard_map(
        functools.partial(per_device, shape["groups"], shape["dp"], shape["blk"]),
        mesh=mesh,
        in_specs=(feature, feature, length, feature, feature, length, weight, weight),
        out_specs=P(("groups", "dp", "blk"), None),
        check_vma=False,
    )
```

```python
import functools

import jax
import jax.numpy as jnp
from jax import lax
from jax.experimental import pallas as pl
from jax.experimental.pallas import tpu as pltpu
from jax.sharding import PartitionSpec as P

HI = lax.Precision.HIGHEST
NT = (((1,), (1,)), ((), ()))
TN = (((0,), (0,)), ((), ()))
NEWTON_STEPS = 7
PLANE = ("groups", "blk")


def vmem():
    return pl.BlockSpec(memory_space=pltpu.VMEM)


def smem():
    return pl.BlockSpec(memory_space=pltpu.SMEM)


def call(kernel, out_shape, in_specs, args, flops=0, limit=16, **kw):
    return pl.pallas_call(
        kernel,
        out_shape=out_shape,
        in_specs=in_specs,
        out_specs=jax.tree.map(lambda _: vmem(), out_shape),
        compiler_params=pltpu.CompilerParams(vmem_limit_bytes=limit * 1024 * 1024),
        cost_estimate=pl.CostEstimate(flops=flops, bytes_accessed=1 << 16, transcendentals=0),
        **kw,
    )(*args)


def swap(x, axis, count, k):
    return lax.ppermute(x, axis, [(i, i ^ k) for i in range(count)])


def bits(count):
    return [1 << s for s in reversed(range(count.bit_length() - 1))]


def load_kernel(n, *refs):
    srcs, dsts, sem = refs[:n], refs[n : 2 * n], refs[2 * n]
    copies = []
    for i, (src, dst) in enumerate(zip(srcs, dsts)):
        rows = src.shape[0] // 2
        for h in range(2):
            part = pl.ds(h * rows, rows)
            copies.append(pltpu.make_async_copy(src.at[part], dst.at[part], sem.at[2 * i + h]))
    for c in copies:
        c.start()
    for c in copies:
        c.wait()


def stack_kernel(n, *refs):
    at = 0
    for src in refs[:n]:
        refs[-1][at : at + src.shape[0], :] = src[...]
        at += src.shape[0]


def stack(parts, after=None):
    rows = sum(p.shape[0] for p in parts)
    extra = () if after is None else (after,)
    return call(
        functools.partial(stack_kernel, len(parts)),
        pltpu.VMEM((rows, parts[0].shape[1]), parts[0].dtype),
        [vmem()] * len(parts) + [pl.BlockSpec(memory_space=pl.ANY)] * len(extra),
        (*parts, *extra),
        limit=1,
    )


def store_products(x_parts, g_parts, acc_ref, out_ref):
    tokens = out_ref.shape[0] // 3
    ko = g_parts[0].shape[1]
    for n in range(2):
        rows = slice(n * tokens, (n + 1) * tokens)
        prior = 0.0 if acc_ref is None else acc_ref[rows, :]
        out_ref[rows, :] = prior + x_parts[n]
    rows = slice(2 * tokens, 3 * tokens)
    for n in range(2):
        cols = slice(n * ko, (n + 1) * ko)
        prior = 0.0 if acc_ref is None else acc_ref[rows, cols]
        out_ref[rows, cols] = prior + g_parts[n]


def nt(a, b):
    return lax.dot_general(a, b, NT, preferred_element_type=jnp.float32)


def project_kernel(*refs):
    x_refs, (w_in, w_out, out_ref) = refs[:4], refs[4:]
    xs = [nt(x_refs[n][...], w_in[...]) for n in (0, 2)]
    gs = [nt(x_refs[n][...], w_out[...]) for n in (1, 3)]
    store_products(xs, gs, None, out_ref)


def project_pieces_kernel(plan, with_acc, n_pieces, *refs):
    x_refs, (own_in, own_out) = refs[:4], refs[4:6]
    pieces = refs[6 : 6 + n_pieces]
    acc_ref = refs[6 + n_pieces] if with_acc else None
    out_ref, w_in, w_out = refs[6 + n_pieces + with_acc :]
    z = lax.axis_index("dp")
    q = lax.axis_index(PLANE)
    rin, rout = own_in.shape[0], own_out.shape[0]
    quarter = own_in.shape[1] // 4
    xs, gs = [0.0, 0.0], [0.0, 0.0]
    at = 0
    for dq, col, width, rows in plan:
        start = pl.multiple_of((q ^ dq) * quarter + col, 128)
        cols = pl.ds(start, width)
        here = slice(at, at + width)
        at += width
        w_in[pl.ds(pl.multiple_of(z * rin, rin), rin), here] = own_in[:, cols]
        w_out[pl.ds(pl.multiple_of(z * rout, rout), rout), here] = own_out[:, cols]
        for p, row, k in rows:
            dst_in = pl.multiple_of((z ^ k) * rin, rin)
            dst_out = pl.multiple_of((z ^ k) * rout, rout)
            w_in[pl.ds(dst_in, rin), here] = pieces[p][row : row + rin, :]
            w_out[pl.ds(dst_out, rout), here] = pieces[p][row + rin : row + rin + rout, :]
        for m in range(2):
            xs[m] += nt(x_refs[2 * m][:, cols], w_in[:, here])
            gs[m] += nt(x_refs[2 * m + 1][:, cols], w_out[:, here])
    store_products(xs, gs, acc_ref, out_ref)


def moments_kernel(len_tr, len_te, mine, other, msg_ref, gtr_ref):
    tokens = mine.shape[0] // 3
    ki = mine.shape[1]
    ko = ki // 2
    total = mine[...] + other[...]
    rows = lax.broadcasted_iota(jnp.int32, (tokens, ki), 0)
    n_tr, n_te = len_tr[0], len_te[0]
    x_tr = jnp.where(rows < n_tr, total[:tokens], 0.0)
    x_te = jnp.where(rows < n_te, total[tokens : 2 * tokens], 0.0)
    g_both = total[2 * tokens :]
    g_tr = jnp.where(rows < n_tr, g_both, 0.0)[:, :ko]
    g_te = g_both[:, ko:]
    dot = functools.partial(
        lax.dot_general, dimension_numbers=TN, precision=HI,
        preferred_element_type=jnp.float32,
    )
    half = ki // 2
    core = lax.axis_index("mp")
    gtr_ref[...] = dot(x_tr, g_tr) / n_tr.astype(jnp.float32)

    @pl.when(core == 0)
    def _():
        c_in = dot(x_tr, x_tr)
        msg_ref[:half, :] = c_in[:half, :]
        msg_ref[half:ki, :half] = c_in[half:, half:]
        msg_ref[half:ki, half:] = dot(g_tr, g_tr)
        msg_ref[ki:, :] = jnp.full((8, ki), n_tr.astype(jnp.float32))

    @pl.when(core == 1)
    def _():
        grad_te = dot(x_te, g_te) / n_te.astype(jnp.float32)
        msg_ref[:half, :ko] = grad_te[:half]
        msg_ref[:half, ko:] = grad_te[half:]
        msg_ref[half:, :] = jnp.zeros((half + 8, ki), jnp.float32)


def round_kernel(fac_rows, grad_rows, mine, other, out_ref):
    core = lax.axis_index("mp")

    @pl.when(core == 0)
    def _():
        out_ref[:fac_rows, :] = mine[:fac_rows, :] + other[:fac_rows, :]

    @pl.when(core == 1)
    def _():
        out_ref[:grad_rows, :] = mine[:grad_rows, :]
        out_ref[grad_rows : 2 * grad_rows, :] = other[:grad_rows, :]


def damped(c):
    n = c.shape[0]
    i = lax.broadcasted_iota(jnp.int32, (n, n), 0)
    j = lax.broadcasted_iota(jnp.int32, (n, n), 1)
    eye = (i == j).astype(jnp.float32)
    trace = jnp.sum(c * eye, axis=(0, 1), keepdims=True)
    low = 0.1 * trace / n
    a = c + low * eye
    high = jnp.max(jnp.sum(jnp.abs(a), axis=0, keepdims=True), axis=1, keepdims=True)
    return a, eye, low, jnp.minimum(high, trace + low)


def mm(a, b):
    return jnp.dot(a, b, precision=HI, preferred_element_type=jnp.float32)


def inverses(matrices):
    state = []
    for c in matrices:
        a, eye, low, high = damped(c)
        scale = 2.0 / (low + high)
        r = (high - low) / (high + low)
        state.append((a, scale * a, scale * eye, r))
    for step in range(NEWTON_STEPS):
        nxt = []
        for a, m, x, r in state:
            s = 2.0 / (2.0 - r * r)
            n = m.shape[0]
            if step == 0:
                mx = s * (2.0 * m - mm(m, m))
                xx = s * (2.0 * x - x[:1, :1] * m)
            else:
                both = mm(jnp.concatenate([m, x], axis=0), m)
                mx = s * (2.0 * m - both[:n])
                xx = s * (2.0 * x - both[n:])
            nxt.append((a, mx, xx, r * r / (2.0 - r * r)))
        state = nxt
    return [2.0 * x - mm(x, mm(a, x)) for a, m, x, r in state]


def scores_kernel(order, n_blk, mine, other, gtr_ref, out_ref):
    ki, ko = gtr_ref.shape
    half = ki // 2
    first = lax.axis_index("mp") == 0
    total = jnp.where(first, mine[: ki + 8, :], other[: ki + 8, :])
    top = total[:half]
    low = total[half:ki]
    c_in = jnp.concatenate(
        [top, jnp.concatenate([top[:, half:].T, low[:, :half]], axis=1)], axis=0
    )
    count = total[ki : ki + 1, :1]
    inv_in, inv_out = inverses([c_in, low[:, half:]])
    side = mm(mm(inv_in, gtr_ref[...]), inv_out) * (count * count)
    side = jnp.concatenate([side[:half], side[half:]], axis=1)
    sums = []
    for p in range(len(order)):
        rows = slice(p * half, (p + 1) * half)
        grad = jnp.where(first, other[rows, :], mine[rows, :])
        sums.append(jnp.sum(side * grad, axis=0, keepdims=True))
    values = jnp.sum(jnp.concatenate(sums, axis=0), axis=1, keepdims=True)
    z = lax.axis_index("dp")
    b = lax.axis_index("blk")
    lane = lax.broadcasted_iota(jnp.int32, out_ref.shape, 1)
    row = jnp.zeros(out_ref.shape, jnp.float32)
    for p, (dz, db) in enumerate(order):
        row = jnp.where(lane == (z ^ dz) * n_blk + (b ^ db), values[p : p + 1, :], row)
    out_ref[...] = row


def project(xs, w_in, w_out, n_groups, n_dp, n_blk):
    tokens, width = xs[0].shape
    rin, rout = w_in.shape[0], w_out.shape[0]
    ki, ko = rin * n_dp, rout * n_dp
    out_shape = jax.ShapeDtypeStruct((3 * tokens, ki), jnp.float32)
    if (n_groups, n_dp, n_blk) != (2, 4, 2):
        w_in = lax.all_gather(w_in, "dp", axis=0, tiled=True)
        w_out = lax.all_gather(w_out, "dp", axis=0, tiled=True)
        return call(project_kernel, out_shape, [vmem()] * 6, (*xs, w_in, w_out))

    part = width // 8
    shard = rin + rout
    q = lax.axis_index(PLANE)
    whole = jnp.concatenate([w_in, w_out], axis=0)
    mine = lax.dynamic_slice(whole, (0, q * 2 * part), (shard, 2 * part))
    opposite = lax.dynamic_slice(whole, (0, (q ^ 3) * 2 * part), (shard, 2 * part))
    operands = (*xs, w_in, w_out)
    *xs, w_in, w_out = call(
        functools.partial(load_kernel, 6),
        tuple(pltpu.VMEM(x.shape, x.dtype) for x in operands),
        [pl.BlockSpec(memory_space=pltpu.HBM)] * 6,
        [pltpu.with_memory_space_constraint(x, pltpu.HBM) for x in operands],
        flops=1 << 30,
        scratch_shapes=[pltpu.SemaphoreType.DMA((12,))],
    )
    halves = [mine[:, :part], mine[:, part:]]
    far = [swap(h, "dp", n_dp, 2) for h in halves]
    far_op = swap(opposite, "dp", n_dp, 2)
    both_a = stack((halves[0], far[0]), w_out)
    near_a = swap(both_a, "dp", n_dp, 1)
    both_b = stack((halves[1], far[1]))
    near_b = swap(both_b, "dp", n_dp, 1)
    za = stack((far[0], near_a))
    xa, ya = swap(za, PLANE, 4, 1), swap(za, PLANE, 4, 2)
    both_op = stack((opposite, far_op))
    near_op = swap(both_op, "dp", n_dp, 1)
    zb = stack((far[1], near_b))
    xb, yb = swap(zb, PLANE, 4, 1), swap(zb, PLANE, 4, 2)

    def accumulate(plan, pieces, acc):
        args = (*xs, w_in, w_out, *pieces) + (() if acc is None else (acc,))
        total = sum(width for _, _, width, _ in plan)
        return call(
            functools.partial(project_pieces_kernel, plan, acc is not None, len(pieces)),
            out_shape,
            [vmem()] * len(args),
            args,
            flops=1 << 30,
            scratch_shapes=[
                pltpu.VMEM((ki, total), jnp.bfloat16),
                pltpu.VMEM((ko, total), jnp.bfloat16),
            ],
        )

    def stacked(p):
        return tuple((p, i * shard, k) for i, k in enumerate((2, 1, 3)))

    acc = accumulate(
        ((0, 0, part, stacked(0)), (0, part, part, stacked(1))), (za, zb), None)
    acc = accumulate(
        ((1, 0, part, stacked(0)), (2, 0, part, stacked(1))), (xa, ya), acc)
    return accumulate(
        (
            (1, part, part, stacked(0)),
            (2, part, part, stacked(1)),
            (3, 0, 2 * part, ((2, 0, 2), (3, 0, 1), (3, shard, 3))),
        ),
        (xb, yb, far_op, near_op),
        acc,
    )


def per_device(
    n_groups, n_dp, n_blk, train_inputs, train_cotangents, train_lengths,
    test_inputs, test_cotangents, test_lengths, proj_in, proj_out,
):
    _, tokens, width = train_inputs.shape
    xs = [a.reshape(tokens, width) for a in (
        train_inputs, train_cotangents, test_inputs, test_cotangents)]
    part = project(xs, proj_in.T, proj_out.T, n_groups, n_dp, n_blk)
    ki = part.shape[1]
    ko = ki // 2
    other = swap(part, "mp", 2, 1)
    fac_rows, grad_rows = ki + 8, ki // 2
    msg, gtr = call(
        moments_kernel,
        (
            jax.ShapeDtypeStruct((fac_rows, ki), jnp.float32),
            jax.ShapeDtypeStruct((ki, ko), jnp.float32),
        ),
        [smem(), smem(), vmem(), vmem()],
        (train_lengths, test_lengths, part, other),
    )
    steps_z = [(k, 0) for k in bits(n_dp)]
    steps_x = [(0, k) for k in bits(n_blk)]
    order = [(0, 0)]
    for step0, step1 in zip(steps_x + steps_z, steps_z + steps_x):
        pairs = []
        for z in range(n_dp):
            for b in range(n_blk):
                for core, (dz, db) in enumerate((step0, step1)):
                    pairs.append((
                        (z * n_blk + b) * 2 + core, ((z ^ dz) * n_blk + (b ^ db)) * 2 + core))
        recv = lax.ppermute(msg, ("dp", "blk", "mp"), pairs)
        rows = len(order) * grad_rows
        msg = call(
            functools.partial(round_kernel, fac_rows, rows),
            jax.ShapeDtypeStruct((max(fac_rows, 2 * rows), ki), jnp.float32),
            [vmem()] * 2,
            (msg, recv),
        )
        order += [(dz ^ step1[0], db ^ step1[1]) for dz, db in order]
    recv = swap(msg, "mp", 2, 1)
    return call(
        functools.partial(scores_kernel, order, n_blk),
        jax.ShapeDtypeStruct((1, n_dp * n_blk), jnp.float32),
        [vmem()] * 3,
        (msg, recv, gtr),
        flops=4 << 30,
    )


def solution(mesh):
    feature = P(("groups", "dp", "blk"), None, "mp")
    length = P(("groups", "dp", "blk"))
    weight = P("mp", "dp")
    shape = mesh.shape
    return jax.shard_map(
        functools.partial(per_device, shape["groups"], shape["dp"], shape["blk"]),
        mesh=mesh,
        in_specs=(feature, feature, length, feature, feature, length, weight, weight),
        out_specs=P(("groups", "dp", "blk"), None),
        check_vma=False,
    )
```

```python
import functools

import jax
import jax.numpy as jnp
from jax import lax
from jax.experimental import pallas as pl
from jax.experimental.pallas import tpu as pltpu
from jax.sharding import PartitionSpec as P

HI = lax.Precision.HIGHEST
NT = (((1,), (1,)), ((), ()))
TN = (((0,), (0,)), ((), ()))
NEWTON_STEPS = 7
PLANE = ("groups", "blk")


def vmem():
    return pl.BlockSpec(memory_space=pltpu.VMEM)


def smem():
    return pl.BlockSpec(memory_space=pltpu.SMEM)


def call(kernel, out_shape, in_specs, args, flops=0, limit=16, **kw):
    return pl.pallas_call(
        kernel,
        out_shape=out_shape,
        in_specs=in_specs,
        out_specs=jax.tree.map(lambda _: vmem(), out_shape),
        compiler_params=pltpu.CompilerParams(vmem_limit_bytes=limit * 1024 * 1024),
        cost_estimate=pl.CostEstimate(flops=flops, bytes_accessed=1 << 16, transcendentals=0),
        **kw,
    )(*args)


def swap(x, axis, count, k):
    return lax.ppermute(x, axis, [(i, i ^ k) for i in range(count)])


def mixed(x, axes, counts, step0, step1):
    pairs = []
    for i in range(counts[0]):
        for j in range(counts[1]):
            for core, (di, dj) in enumerate((step0, step1)):
                pairs.append((
                    (i * counts[1] + j) * 2 + core,
                    ((i ^ di) * counts[1] + (j ^ dj)) * 2 + core,
                ))
    return lax.ppermute(x, (*axes, "mp"), pairs)


def bits(count):
    return [1 << s for s in reversed(range(count.bit_length() - 1))]


def load_kernel(n, *refs):
    srcs, dsts, sem = refs[:n], refs[n : 2 * n], refs[2 * n]
    copies = []
    for i, (src, dst) in enumerate(zip(srcs, dsts)):
        rows = src.shape[0] // 2
        for h in range(2):
            part = pl.ds(h * rows, rows)
            copies.append(pltpu.make_async_copy(src.at[part], dst.at[part], sem.at[2 * i + h]))
    for c in copies:
        c.start()
    for c in copies:
        c.wait()


def stack_kernel(n, *refs):
    at = 0
    for src in refs[:n]:
        refs[-1][at : at + src.shape[0], :] = src[...]
        at += src.shape[0]


def stack(parts, after=None):
    rows = sum(p.shape[0] for p in parts)
    extra = () if after is None else (after,)
    return call(
        functools.partial(stack_kernel, len(parts)),
        pltpu.VMEM((rows, parts[0].shape[1]), parts[0].dtype),
        [vmem()] * len(parts) + [pl.BlockSpec(memory_space=pl.ANY)] * len(extra),
        (*parts, *extra),
        limit=1,
    )


def store_products(x_parts, g_parts, acc_ref, out_ref):
    tokens = out_ref.shape[0] // 3
    ko = g_parts[0].shape[1]
    for n in range(2):
        rows = slice(n * tokens, (n + 1) * tokens)
        prior = 0.0 if acc_ref is None else acc_ref[rows, :]
        out_ref[rows, :] = prior + x_parts[n]
    rows = slice(2 * tokens, 3 * tokens)
    for n in range(2):
        cols = slice(n * ko, (n + 1) * ko)
        prior = 0.0 if acc_ref is None else acc_ref[rows, cols]
        out_ref[rows, cols] = prior + g_parts[n]


def nt(a, b):
    return lax.dot_general(a, b, NT, preferred_element_type=jnp.float32)


def project_kernel(*refs):
    x_refs, (w_in, w_out, out_ref) = refs[:4], refs[4:]
    xs = [nt(x_refs[n][...], w_in[...]) for n in (0, 2)]
    gs = [nt(x_refs[n][...], w_out[...]) for n in (1, 3)]
    store_products(xs, gs, None, out_ref)


def project_pieces_kernel(plan, with_acc, n_pieces, *refs):
    x_refs, (own_in, own_out) = refs[:4], refs[4:6]
    pieces = refs[6 : 6 + n_pieces]
    acc_ref = refs[6 + n_pieces] if with_acc else None
    out_ref, w_in, w_out = refs[6 + n_pieces + with_acc :]
    z = lax.axis_index("dp")
    q = lax.axis_index(PLANE)
    core = lax.axis_index("mp")
    rin, rout = own_in.shape[0], own_out.shape[0]
    quarter = own_in.shape[1] // 4
    xs, gs = [0.0, 0.0], [0.0, 0.0]
    at = 0
    for dq, col, width, rows in plan:
        other = q ^ (core * (3 ^ dq) + (1 - core) * dq) if dq in (1, 2) else q ^ dq
        start = pl.multiple_of(other * quarter + col, 128)
        cols = pl.ds(start, width)
        here = slice(at, at + width)
        at += width
        w_in[pl.ds(pl.multiple_of(z * rin, rin), rin), here] = own_in[:, cols]
        w_out[pl.ds(pl.multiple_of(z * rout, rout), rout), here] = own_out[:, cols]
        for p, row, k in rows:
            dst_in = pl.multiple_of((z ^ k) * rin, rin)
            dst_out = pl.multiple_of((z ^ k) * rout, rout)
            w_in[pl.ds(dst_in, rin), here] = pieces[p][row : row + rin, :]
            w_out[pl.ds(dst_out, rout), here] = pieces[p][row + rin : row + rin + rout, :]
        for m in range(2):
            xs[m] += nt(x_refs[2 * m][:, cols], w_in[:, here])
            gs[m] += nt(x_refs[2 * m + 1][:, cols], w_out[:, here])
    store_products(xs, gs, acc_ref, out_ref)


def moments_kernel(len_tr, len_te, mine, other, fac_ref, gte_ref, gtr_ref):
    tokens = mine.shape[0] // 3
    ki = mine.shape[1]
    ko = ki // 2
    total = mine[...] + other[...]
    rows = lax.broadcasted_iota(jnp.int32, (tokens, ki), 0)
    n_tr, n_te = len_tr[0], len_te[0]
    x_tr = jnp.where(rows < n_tr, total[:tokens], 0.0)
    x_te = jnp.where(rows < n_te, total[tokens : 2 * tokens], 0.0)
    g_both = total[2 * tokens :]
    g_tr = jnp.where(rows < n_tr, g_both, 0.0)[:, :ko]
    g_te = g_both[:, ko:]
    dot = functools.partial(
        lax.dot_general, dimension_numbers=TN, precision=HI,
        preferred_element_type=jnp.float32,
    )
    c_in = dot(x_tr, x_tr)
    c_out = dot(g_tr, g_tr)
    half = ki // 2
    fac_ref[:half, :] = c_in[:half, :]
    fac_ref[half:ki, :half] = c_in[half:, half:]
    fac_ref[half:ki, half:] = c_out
    fac_ref[ki:, :] = jnp.full((8, ki), n_tr.astype(jnp.float32))
    grad_tr = dot(x_tr, g_tr) / n_tr.astype(jnp.float32)
    grad_te = dot(x_te, g_te) / n_te.astype(jnp.float32)
    gtr_ref[...] = grad_tr
    gte_ref[0, :, :ko] = grad_te[:half]
    gte_ref[0, :, ko:] = grad_te[half:]


def damped(c):
    n = c.shape[0]
    i = lax.broadcasted_iota(jnp.int32, (n, n), 0)
    j = lax.broadcasted_iota(jnp.int32, (n, n), 1)
    eye = (i == j).astype(jnp.float32)
    trace = jnp.sum(c * eye, axis=(0, 1), keepdims=True)
    low = 0.1 * trace / n
    a = c + low * eye
    high = jnp.max(jnp.sum(jnp.abs(a), axis=0, keepdims=True), axis=1, keepdims=True)
    return a, eye, low, jnp.minimum(high, trace + low)


def mm(a, b):
    return jnp.dot(a, b, precision=HI, preferred_element_type=jnp.float32)


def inverses(matrices):
    state = []
    for c in matrices:
        a, eye, low, high = damped(c)
        scale = 2.0 / (low + high)
        r = (high - low) / (high + low)
        state.append((a, scale * a, scale * eye, r))
    for step in range(NEWTON_STEPS):
        nxt = []
        for a, m, x, r in state:
            s = 2.0 / (2.0 - r * r)
            n = m.shape[0]
            if step == 0:
                mx = s * (2.0 * m - mm(m, m))
                xx = s * (2.0 * x - x[:1, :1] * m)
            else:
                both = mm(jnp.concatenate([m, x], axis=0), m)
                mx = s * (2.0 * m - both[:n])
                xx = s * (2.0 * x - both[n:])
            nxt.append((a, mx, xx, r * r / (2.0 - r * r)))
        state = nxt
    return [2.0 * x - mm(x, mm(a, x)) for a, m, x, r in state]


def side_kernel(fac_ref, gtr_ref, out_ref):
    ki = fac_ref.shape[1]
    half = ki // 2
    top = fac_ref[:half, :]
    low = fac_ref[half:ki, :]
    c_in = jnp.concatenate(
        [top, jnp.concatenate([top[:, half:].T, low[:, :half]], axis=1)], axis=0
    )
    count = fac_ref[ki : ki + 1, :1]
    inv_in, inv_out = inverses([c_in, low[:, half:]])
    side = mm(mm(inv_in, gtr_ref[...]), inv_out) * (count * count)
    out_ref[:, :half] = side[:half]
    out_ref[:, half:] = side[half:]


def scores_kernel(order, n_blk, side_ref, gte_ref, out_ref):
    z = lax.axis_index("dp")
    b = lax.axis_index("blk")
    lane = lax.broadcasted_iota(jnp.int32, out_ref.shape, 1)
    row = jnp.zeros(out_ref.shape, jnp.float32)
    side = side_ref[...]
    sums = [jnp.sum(side * gte_ref[p], axis=0, keepdims=True) for p in range(len(order))]
    values = jnp.sum(jnp.concatenate(sums, axis=0), axis=1, keepdims=True)
    for p, (dz, db) in enumerate(order):
        row = jnp.where(lane == (z ^ dz) * n_blk + (b ^ db), values[p : p + 1, :], row)
    out_ref[...] = row


def project(xs, w_in, w_out, n_groups, n_dp, n_blk):
    tokens, width = xs[0].shape
    rin, rout = w_in.shape[0], w_out.shape[0]
    ki, ko = rin * n_dp, rout * n_dp
    out_shape = jax.ShapeDtypeStruct((3 * tokens, ki), jnp.float32)
    if (n_groups, n_dp, n_blk) != (2, 4, 2):
        w_in = lax.all_gather(w_in, "dp", axis=0, tiled=True)
        w_out = lax.all_gather(w_out, "dp", axis=0, tiled=True)
        return call(project_kernel, out_shape, [vmem()] * 6, (*xs, w_in, w_out))

    part = width // 8
    shard = rin + rout
    q = lax.axis_index(PLANE)
    whole = jnp.concatenate([w_in, w_out], axis=0)
    mine = lax.dynamic_slice(whole, (0, q * 2 * part), (shard, 2 * part))
    opposite = lax.dynamic_slice(whole, (0, (q ^ 3) * 2 * part), (shard, 2 * part))
    operands = (*xs, w_in, w_out)
    *xs, w_in, w_out = call(
        functools.partial(load_kernel, 6),
        tuple(pltpu.VMEM(x.shape, x.dtype) for x in operands),
        [pl.BlockSpec(memory_space=pltpu.HBM)] * 6,
        [pltpu.with_memory_space_constraint(x, pltpu.HBM) for x in operands],
        flops=1 << 30,
        scratch_shapes=[pltpu.SemaphoreType.DMA((12,))],
    )
    halves = [mine[:, :part], mine[:, part:]]
    far = [swap(h, "dp", n_dp, 2) for h in halves]
    far_op = swap(opposite, "dp", n_dp, 2)
    both_a = stack((halves[0], far[0]), w_out)
    near_a = swap(both_a, "dp", n_dp, 1)
    both_b = stack((halves[1], far[1]))
    near_b = swap(both_b, "dp", n_dp, 1)
    za = stack((far[0], near_a))
    along_x, along_y = (0, 1), (1, 0)
    xa = mixed(za, PLANE, (n_groups, n_blk), along_x, along_y)
    ya = mixed(za, PLANE, (n_groups, n_blk), along_y, along_x)
    both_op = stack((opposite, far_op))
    near_op = swap(both_op, "dp", n_dp, 1)
    zb = stack((far[1], near_b))
    xb = mixed(zb, PLANE, (n_groups, n_blk), along_x, along_y)
    yb = mixed(zb, PLANE, (n_groups, n_blk), along_y, along_x)

    def accumulate(plan, pieces, acc):
        args = (*xs, w_in, w_out, *pieces) + (() if acc is None else (acc,))
        total = sum(width for _, _, width, _ in plan)
        return call(
            functools.partial(project_pieces_kernel, plan, acc is not None, len(pieces)),
            out_shape,
            [vmem()] * len(args),
            args,
            flops=1 << 30,
            scratch_shapes=[
                pltpu.VMEM((ki, total), jnp.bfloat16),
                pltpu.VMEM((ko, total), jnp.bfloat16),
            ],
        )

    def stacked(p):
        return tuple((p, i * shard, k) for i, k in enumerate((2, 1, 3)))

    acc = accumulate(
        ((0, 0, part, stacked(0)), (0, part, part, stacked(1))), (za, zb), None)
    acc = accumulate(
        ((1, 0, part, stacked(0)), (2, 0, part, stacked(1))), (xa, ya), acc)
    return accumulate(
        (
            (1, part, part, stacked(0)),
            (2, part, part, stacked(1)),
            (3, 0, 2 * part, ((2, 0, 2), (3, 0, 1), (3, shard, 3))),
        ),
        (xb, yb, far_op, near_op),
        acc,
    )


def per_device(
    n_groups, n_dp, n_blk, train_inputs, train_cotangents, train_lengths,
    test_inputs, test_cotangents, test_lengths, proj_in, proj_out,
):
    _, tokens, width = train_inputs.shape
    xs = [a.reshape(tokens, width) for a in (
        train_inputs, train_cotangents, test_inputs, test_cotangents)]
    part = project(xs, proj_in.T, proj_out.T, n_groups, n_dp, n_blk)
    ki = part.shape[1]
    ko = ki // 2
    other = swap(part, "mp", 2, 1)
    fac, gte, gtr = call(
        moments_kernel,
        (
            jax.ShapeDtypeStruct((ki + 8, ki), jnp.float32),
            jax.ShapeDtypeStruct((1, ki // 2, ki), jnp.float32),
            jax.ShapeDtypeStruct((ki, ko), jnp.float32),
        ),
        [smem(), smem(), vmem(), vmem()],
        (train_lengths, test_lengths, part, other),
    )
    order = [(0, 0)]
    for axis, count in (("dp", n_dp), ("blk", n_blk)):
        for k in bits(count):
            gte = jnp.concatenate([gte, swap(gte, axis, count, k)], axis=0)
            order += [(dz ^ k, db) if axis == "dp" else (dz, db ^ k) for dz, db in order]
    steps_z = [(k, 0) for k in bits(n_dp)]
    steps_x = [(0, k) for k in bits(n_blk)]
    for step0, step1 in zip(steps_x + steps_z, steps_z + steps_x):
        fac = fac + mixed(fac, ("dp", "blk"), (n_dp, n_blk), step0, step1)
    side = call(
        side_kernel,
        jax.ShapeDtypeStruct((ki // 2, ki), jnp.float32),
        [vmem()] * 2,
        (fac, gtr),
        flops=4 << 30,
    )
    return call(
        functools.partial(scores_kernel, order, n_blk),
        jax.ShapeDtypeStruct((1, n_dp * n_blk), jnp.float32),
        [vmem()] * 2,
        (side, gte),
    )


def solution(mesh):
    feature = P(("groups", "dp", "blk"), None, "mp")
    length = P(("groups", "dp", "blk"))
    weight = P("mp", "dp")
    shape = mesh.shape
    return jax.shard_map(
        functools.partial(per_device, shape["groups"], shape["dp"], shape["blk"]),
        mesh=mesh,
        in_specs=(feature, feature, length, feature, feature, length, weight, weight),
        out_specs=P(("groups", "dp", "blk"), None),
        check_vma=False,
    )
```

```python
import functools

import jax
import jax.numpy as jnp
from jax import lax
from jax.experimental import pallas as pl
from jax.experimental.pallas import tpu as pltpu
from jax.sharding import PartitionSpec as P

HI = lax.Precision.HIGHEST
NT = (((1,), (1,)), ((), ()))
TN = (((0,), (0,)), ((), ()))
NEWTON_STEPS = 7
PLANE = ("groups", "blk")
LANES = 128


def vmem():
    return pl.BlockSpec(memory_space=pltpu.VMEM)


def smem():
    return pl.BlockSpec(memory_space=pltpu.SMEM)


def call(kernel, out_shape, in_specs, args, flops=0, limit=16, **kw):
    return pl.pallas_call(
        kernel,
        out_shape=out_shape,
        in_specs=in_specs,
        out_specs=jax.tree.map(lambda _: vmem(), out_shape),
        compiler_params=pltpu.CompilerParams(vmem_limit_bytes=limit * 1024 * 1024),
        cost_estimate=pl.CostEstimate(flops=flops, bytes_accessed=1 << 16, transcendentals=0),
        **kw,
    )(*args)


def swap(x, axis, count, k):
    return lax.ppermute(x, axis, [(i, i ^ k) for i in range(count)])


def mixed(x, axes, counts, step0, step1):
    pairs = []
    for i in range(counts[0]):
        for j in range(counts[1]):
            for core, (di, dj) in enumerate((step0, step1)):
                pairs.append((
                    (i * counts[1] + j) * 2 + core,
                    ((i ^ di) * counts[1] + (j ^ dj)) * 2 + core,
                ))
    return lax.ppermute(x, (*axes, "mp"), pairs)


def bits(count):
    return [1 << s for s in reversed(range(count.bit_length() - 1))]


def load_kernel(n, *refs):
    srcs, dsts, sem = refs[:n], refs[n : 2 * n], refs[2 * n]
    copies = []
    for i, (src, dst) in enumerate(zip(srcs, dsts)):
        rows = src.shape[0] // 2
        for h in range(2):
            part = pl.ds(h * rows, rows)
            copies.append(pltpu.make_async_copy(src.at[part], dst.at[part], sem.at[2 * i + h]))
    for c in copies:
        c.start()
    for c in copies:
        c.wait()


def stack_kernel(n, *refs):
    at = 0
    for src in refs[:n]:
        refs[-1][at : at + src.shape[0], :] = src[...]
        at += src.shape[0]


def stack(parts, after=None):
    rows = sum(p.shape[0] for p in parts)
    extra = () if after is None else (after,)
    return call(
        functools.partial(stack_kernel, len(parts)),
        pltpu.VMEM((rows, parts[0].shape[1]), parts[0].dtype),
        [vmem()] * len(parts) + [pl.BlockSpec(memory_space=pl.ANY)] * len(extra),
        (*parts, *extra),
        limit=1,
    )


def store_products(x_parts, g_parts, acc_ref, out_ref):
    tokens = out_ref.shape[0] // 3
    ko = g_parts[0].shape[1]
    for n in range(2):
        rows = slice(n * tokens, (n + 1) * tokens)
        prior = 0.0 if acc_ref is None else acc_ref[rows, :]
        out_ref[rows, :] = prior + x_parts[n]
    rows = slice(2 * tokens, 3 * tokens)
    for n in range(2):
        cols = slice(n * ko, (n + 1) * ko)
        prior = 0.0 if acc_ref is None else acc_ref[rows, cols]
        out_ref[rows, cols] = prior + g_parts[n]


def nt(a, b):
    return lax.dot_general(a, b, NT, preferred_element_type=jnp.float32)


def project_kernel(*refs):
    x_refs, (w_in, w_out, out_ref) = refs[:4], refs[4:]
    xs = [nt(x_refs[n][...], w_in[...]) for n in (0, 2)]
    gs = [nt(x_refs[n][...], w_out[...]) for n in (1, 3)]
    store_products(xs, gs, None, out_ref)


def project_pieces_kernel(plan, with_acc, n_pieces, *refs):
    x_refs, (own_in, own_out) = refs[:4], refs[4:6]
    pieces = refs[6 : 6 + n_pieces]
    acc_ref = refs[6 + n_pieces] if with_acc else None
    out_ref, w_in, w_out = refs[6 + n_pieces + with_acc :]
    z = lax.axis_index("dp")
    q = lax.axis_index(PLANE)
    core = lax.axis_index("mp")
    rin, rout = own_in.shape[0], own_out.shape[0]
    quarter = own_in.shape[1] // 4
    xs, gs = [0.0, 0.0], [0.0, 0.0]
    at = 0
    for dq, col, width, rows in plan:
        other = q ^ (core * (3 ^ dq) + (1 - core) * dq) if dq in (1, 2) else q ^ dq
        start = pl.multiple_of(other * quarter + col, 128)
        cols = pl.ds(start, width)
        here = slice(at, at + width)
        at += width
        w_in[pl.ds(pl.multiple_of(z * rin, rin), rin), here] = own_in[:, cols]
        w_out[pl.ds(pl.multiple_of(z * rout, rout), rout), here] = own_out[:, cols]
        for p, row, k in rows:
            dst_in = pl.multiple_of((z ^ k) * rin, rin)
            dst_out = pl.multiple_of((z ^ k) * rout, rout)
            w_in[pl.ds(dst_in, rin), here] = pieces[p][row : row + rin, :]
            w_out[pl.ds(dst_out, rout), here] = pieces[p][row + rin : row + rin + rout, :]
        for m in range(2):
            xs[m] += nt(x_refs[2 * m][:, cols], w_in[:, here])
            gs[m] += nt(x_refs[2 * m + 1][:, cols], w_out[:, here])
    store_products(xs, gs, acc_ref, out_ref)


def moments_kernel(len_tr, len_te, mine, other, fac_ref, gte_ref, gtr_ref):
    tokens = mine.shape[0] // 3
    ki = mine.shape[1]
    ko = ki // 2
    total = mine[...] + other[...]
    rows = lax.broadcasted_iota(jnp.int32, (tokens, ki), 0)
    n_tr, n_te = len_tr[0], len_te[0]
    x_tr = jnp.where(rows < n_tr, total[:tokens], 0.0)
    x_te = jnp.where(rows < n_te, total[tokens : 2 * tokens], 0.0)
    g_both = total[2 * tokens :]
    g_tr = jnp.where(rows < n_tr, g_both, 0.0)[:, :ko]
    g_te = g_both[:, ko:]
    dot = functools.partial(
        lax.dot_general, dimension_numbers=TN, precision=HI,
        preferred_element_type=jnp.float32,
    )
    c_in = dot(x_tr, x_tr)
    c_out = dot(g_tr, g_tr)
    half = ki // 2
    fac_ref[:half, :] = c_in[:half, :]
    fac_ref[half:ki, :half] = c_in[half:, half:]
    fac_ref[half:ki, half:] = c_out
    fac_ref[ki:, :] = jnp.full((8, ki), n_tr.astype(jnp.float32))
    grad_tr = dot(x_tr, g_tr) / n_tr.astype(jnp.float32)
    grad_te = dot(x_te, g_te) / n_te.astype(jnp.float32)
    gtr_ref[...] = grad_tr
    gte_ref[0, :, :ko] = grad_te[:half]
    gte_ref[0, :, ko:] = grad_te[half:]


def wide(x, rows, cols=LANES):
    if x.shape[1] < cols:
        x = jnp.concatenate([x, jnp.zeros((x.shape[0], cols - x.shape[1]), x.dtype)], axis=1)
    if x.shape[0] < rows:
        x = jnp.concatenate([x, jnp.zeros((rows - x.shape[0], cols), x.dtype)], axis=0)
    return x


def parts(x):
    high = x.astype(jnp.bfloat16)
    return high, (x - high.astype(jnp.float32)).astype(jnp.bfloat16)


def right(x):
    high, low = parts(wide(x, LANES))
    upper = jnp.concatenate([high, low], axis=1)
    lower = jnp.concatenate([jnp.zeros_like(high), high], axis=1)
    return jnp.concatenate([upper, lower], axis=0)


def mm3(x, packed):
    both = jnp.dot(
        jnp.concatenate(parts(x), axis=1), packed, preferred_element_type=jnp.float32
    )
    return both[:, :LANES] + both[:, LANES:]


def damped(c):
    n = c.shape[0]
    i = lax.broadcasted_iota(jnp.int32, c.shape, 0)
    j = lax.broadcasted_iota(jnp.int32, c.shape, 1)
    eye = (i == j).astype(jnp.float32)
    trace = jnp.sum(jnp.sum(c * eye, axis=0, keepdims=True), axis=1, keepdims=True)
    low = 0.1 * trace / n
    a = c + low * eye
    high = jnp.max(jnp.sum(jnp.abs(a), axis=0, keepdims=True), axis=1, keepdims=True)
    return a, eye, low, jnp.minimum(high, trace + low)


def inverses(matrices):
    state = []
    for c in matrices:
        a, eye, low, high = damped(c)
        scale = 2.0 / (low + high)
        r = (high - low) / (high + low)
        state.append((a, eye, scale * a, scale * eye, scale, r))
    for step in range(NEWTON_STEPS):
        nxt = []
        for a, eye, m, x, scale, r in state:
            s = 2.0 / (2.0 - r * r)
            n = m.shape[0]
            if step == 0:
                mx = s * (2.0 * m - mm3(m, right(m)))
                xx = s * (2.0 * x - scale * m)
            else:
                both = mm3(jnp.concatenate([m, x], axis=0), right(m))
                mx = s * (2.0 * m - both[:n])
                xx = s * (2.0 * x - both[n:])
            nxt.append((a, eye, mx, xx, scale, r * r / (2.0 - r * r)))
        state = nxt
    result = []
    for a, eye, m, x, scale, r in state:
        n = a.shape[0]
        residual = eye - jnp.dot(
            a[:, :n], x, precision=HI, preferred_element_type=jnp.float32
        )
        result.append(x + mm3(x, right(residual)))
    return result


def side_kernel(fac_ref, gtr_ref, out_ref):
    ki = fac_ref.shape[1]
    half = ki // 2
    top = fac_ref[:half, :]
    low = fac_ref[half:ki, :]
    c_in = jnp.concatenate(
        [top, jnp.concatenate([top[:, half:].T, low[:, :half]], axis=1)], axis=0
    )
    count = fac_ref[ki : ki + 1, :1]
    inv_in, inv_out = inverses([c_in, wide(low[:, half:], half)])
    side = mm3(mm3(inv_in, right(gtr_ref[...])), right(inv_out)) * (count * count)
    out_ref[:, :half] = side[:half, :half]
    out_ref[:, half:] = side[half:, :half]


def scores_kernel(order, n_blk, side_ref, gte_ref, out_ref):
    z = lax.axis_index("dp")
    b = lax.axis_index("blk")
    lane = lax.broadcasted_iota(jnp.int32, out_ref.shape, 1)
    row = jnp.zeros(out_ref.shape, jnp.float32)
    side = side_ref[...]
    sums = [jnp.sum(side * gte_ref[p], axis=0, keepdims=True) for p in range(len(order))]
    values = jnp.sum(jnp.concatenate(sums, axis=0), axis=1, keepdims=True)
    for p, (dz, db) in enumerate(order):
        row = jnp.where(lane == (z ^ dz) * n_blk + (b ^ db), values[p : p + 1, :], row)
    out_ref[...] = row


def project(xs, w_in, w_out, n_groups, n_dp, n_blk):
    tokens, width = xs[0].shape
    rin, rout = w_in.shape[0], w_out.shape[0]
    ki, ko = rin * n_dp, rout * n_dp
    out_shape = jax.ShapeDtypeStruct((3 * tokens, ki), jnp.float32)
    if (n_groups, n_dp, n_blk) != (2, 4, 2):
        w_in = lax.all_gather(w_in, "dp", axis=0, tiled=True)
        w_out = lax.all_gather(w_out, "dp", axis=0, tiled=True)
        return call(project_kernel, out_shape, [vmem()] * 6, (*xs, w_in, w_out))

    part = width // 8
    shard = rin + rout
    q = lax.axis_index(PLANE)
    whole = jnp.concatenate([w_in, w_out], axis=0)
    mine = lax.dynamic_slice(whole, (0, q * 2 * part), (shard, 2 * part))
    opposite = lax.dynamic_slice(whole, (0, (q ^ 3) * 2 * part), (shard, 2 * part))
    operands = (*xs, w_in, w_out)
    *xs, w_in, w_out = call(
        functools.partial(load_kernel, 6),
        tuple(pltpu.VMEM(x.shape, x.dtype) for x in operands),
        [pl.BlockSpec(memory_space=pltpu.HBM)] * 6,
        [pltpu.with_memory_space_constraint(x, pltpu.HBM) for x in operands],
        flops=1 << 30,
        scratch_shapes=[pltpu.SemaphoreType.DMA((12,))],
    )
    halves = [mine[:, :part], mine[:, part:]]
    far = [swap(h, "dp", n_dp, 2) for h in halves]
    far_op = swap(opposite, "dp", n_dp, 2)
    both_a = stack((halves[0], far[0]), w_out)
    near_a = swap(both_a, "dp", n_dp, 1)
    both_b = stack((halves[1], far[1]))
    near_b = swap(both_b, "dp", n_dp, 1)
    za = stack((far[0], near_a))
    along_x, along_y = (0, 1), (1, 0)
    xa = mixed(za, PLANE, (n_groups, n_blk), along_x, along_y)
    ya = mixed(za, PLANE, (n_groups, n_blk), along_y, along_x)
    both_op = stack((opposite, far_op))
    near_op = swap(both_op, "dp", n_dp, 1)
    zb = stack((far[1], near_b))
    xb = mixed(zb, PLANE, (n_groups, n_blk), along_x, along_y)
    yb = mixed(zb, PLANE, (n_groups, n_blk), along_y, along_x)

    def accumulate(plan, pieces, acc):
        args = (*xs, w_in, w_out, *pieces) + (() if acc is None else (acc,))
        total = sum(width for _, _, width, _ in plan)
        return call(
            functools.partial(project_pieces_kernel, plan, acc is not None, len(pieces)),
            out_shape,
            [vmem()] * len(args),
            args,
            flops=1 << 30,
            scratch_shapes=[
                pltpu.VMEM((ki, total), jnp.bfloat16),
                pltpu.VMEM((ko, total), jnp.bfloat16),
            ],
        )

    def stacked(p):
        return tuple((p, i * shard, k) for i, k in enumerate((2, 1, 3)))

    acc = accumulate(
        ((0, 0, part, stacked(0)), (0, part, part, stacked(1))), (za, zb), None)
    acc = accumulate(
        ((1, 0, part, stacked(0)), (2, 0, part, stacked(1))), (xa, ya), acc)
    return accumulate(
        (
            (1, part, part, stacked(0)),
            (2, part, part, stacked(1)),
            (3, 0, 2 * part, ((2, 0, 2), (3, 0, 1), (3, shard, 3))),
        ),
        (xb, yb, far_op, near_op),
        acc,
    )


def per_device(
    n_groups, n_dp, n_blk, train_inputs, train_cotangents, train_lengths,
    test_inputs, test_cotangents, test_lengths, proj_in, proj_out,
):
    _, tokens, width = train_inputs.shape
    xs = [a.reshape(tokens, width) for a in (
        train_inputs, train_cotangents, test_inputs, test_cotangents)]
    part = project(xs, proj_in.T, proj_out.T, n_groups, n_dp, n_blk)
    ki = part.shape[1]
    ko = ki // 2
    other = swap(part, "mp", 2, 1)
    fac, gte, gtr = call(
        moments_kernel,
        (
            jax.ShapeDtypeStruct((ki + 8, ki), jnp.float32),
            jax.ShapeDtypeStruct((1, ki // 2, ki), jnp.float32),
            jax.ShapeDtypeStruct((ki, ko), jnp.float32),
        ),
        [smem(), smem(), vmem(), vmem()],
        (train_lengths, test_lengths, part, other),
    )
    order = [(0, 0)]
    for axis, count in (("dp", n_dp), ("blk", n_blk)):
        for k in bits(count):
            gte = jnp.concatenate([gte, swap(gte, axis, count, k)], axis=0)
            order += [(dz ^ k, db) if axis == "dp" else (dz, db ^ k) for dz, db in order]
    steps_z = [(k, 0) for k in bits(n_dp)]
    steps_x = [(0, k) for k in bits(n_blk)]
    for step0, step1 in zip(steps_x + steps_z, steps_z + steps_x):
        fac = fac + mixed(fac, ("dp", "blk"), (n_dp, n_blk), step0, step1)
    side = call(
        side_kernel,
        jax.ShapeDtypeStruct((ki // 2, ki), jnp.float32),
        [vmem()] * 2,
        (fac, gtr),
        flops=4 << 30,
    )
    return call(
        functools.partial(scores_kernel, order, n_blk),
        jax.ShapeDtypeStruct((1, n_dp * n_blk), jnp.float32),
        [vmem()] * 2,
        (side, gte),
    )


def solution(mesh):
    feature = P(("groups", "dp", "blk"), None, "mp")
    length = P(("groups", "dp", "blk"))
    weight = P("mp", "dp")
    shape = mesh.shape
    return jax.shard_map(
        functools.partial(per_device, shape["groups"], shape["dp"], shape["blk"]),
        mesh=mesh,
        in_specs=(feature, feature, length, feature, feature, length, weight, weight),
        out_specs=P(("groups", "dp", "blk"), None),
        check_vma=False,
    )
```

```python
import functools

import jax
import jax.numpy as jnp
from jax import lax
from jax.experimental import pallas as pl
from jax.experimental.pallas import tpu as pltpu
from jax.sharding import PartitionSpec as P

HI = lax.Precision.HIGHEST
NT = (((1,), (1,)), ((), ()))
TN = (((0,), (0,)), ((), ()))
NEWTON_STEPS = 7
PLANE = ("groups", "blk")
LANES = 128


def vmem():
    return pl.BlockSpec(memory_space=pltpu.VMEM)


def smem():
    return pl.BlockSpec(memory_space=pltpu.SMEM)


def call(kernel, out_shape, in_specs, args, flops=0, limit=16, **kw):
    return pl.pallas_call(
        kernel,
        out_shape=out_shape,
        in_specs=in_specs,
        out_specs=jax.tree.map(lambda _: vmem(), out_shape),
        compiler_params=pltpu.CompilerParams(vmem_limit_bytes=limit * 1024 * 1024),
        cost_estimate=pl.CostEstimate(flops=flops, bytes_accessed=1 << 16, transcendentals=0),
        **kw,
    )(*args)


def swap(x, axis, count, k):
    return lax.ppermute(x, axis, [(i, i ^ k) for i in range(count)])


def mixed(x, axes, counts, step0, step1):
    pairs = []
    for i in range(counts[0]):
        for j in range(counts[1]):
            for core, (di, dj) in enumerate((step0, step1)):
                pairs.append((
                    (i * counts[1] + j) * 2 + core,
                    ((i ^ di) * counts[1] + (j ^ dj)) * 2 + core,
                ))
    return lax.ppermute(x, (*axes, "mp"), pairs)


def bits(count):
    return [1 << s for s in reversed(range(count.bit_length() - 1))]


def load_kernel(n, *refs):
    srcs, dsts, sem = refs[:n], refs[n : 2 * n], refs[2 * n]
    copies = []
    for i, (src, dst) in enumerate(zip(srcs, dsts)):
        rows = src.shape[0] // 2
        for h in range(2):
            part = pl.ds(h * rows, rows)
            copies.append(pltpu.make_async_copy(src.at[part], dst.at[part], sem.at[2 * i + h]))
    for c in copies:
        c.start()
    for c in copies:
        c.wait()


def slice_kernel(w_in, w_out, first, second, opposite, sem):
    q = lax.axis_index(PLANE)
    rin = w_in.shape[0]
    half = first.shape[1]
    copies = []
    for dst, start in ((first, 2 * q * half), (second, (2 * q + 1) * half),
                       (opposite, 2 * (q ^ 3) * half)):
        cols = pl.ds(pl.multiple_of(start, half), dst.shape[1])
        for src, rows in ((w_in, pl.ds(0, rin)), (w_out, pl.ds(rin, w_out.shape[0]))):
            copies.append(pltpu.make_async_copy(
                src.at[:, cols], dst.at[rows, :], sem.at[len(copies)]))
    for c in copies:
        c.start()
    for c in copies:
        c.wait()


def stack_kernel(n, *refs):
    at = 0
    for src in refs[:n]:
        refs[-1][at : at + src.shape[0], :] = src[...]
        at += src.shape[0]


def stack(parts, after=None):
    rows = sum(p.shape[0] for p in parts)
    extra = () if after is None else (after,)
    return call(
        functools.partial(stack_kernel, len(parts)),
        pltpu.VMEM((rows, parts[0].shape[1]), parts[0].dtype),
        [vmem()] * len(parts) + [pl.BlockSpec(memory_space=pl.ANY)] * len(extra),
        (*parts, *extra),
        limit=1,
    )


def store_products(xs, gs, acc_ref, out_ref):
    tokens = out_ref.shape[0] // 3
    sides = jnp.concatenate([gs[:tokens], gs[tokens:]], axis=1)
    prior = 0.0 if acc_ref is None else acc_ref[: 2 * tokens, :]
    out_ref[: 2 * tokens, :] = prior + xs
    prior = 0.0 if acc_ref is None else acc_ref[2 * tokens :, :]
    out_ref[2 * tokens :, :] = prior + sides


def both(train, test, cols):
    return jnp.concatenate([train[:, cols], test[:, cols]], axis=0)


def nt(a, b):
    return lax.dot_general(a, b, NT, preferred_element_type=jnp.float32)


def project_kernel(*refs):
    x_refs, (w_in, w_out, out_ref) = refs[:4], refs[4:]
    every = slice(None)
    xs = nt(both(x_refs[0], x_refs[2], every), w_in[...])
    gs = nt(both(x_refs[1], x_refs[3], every), w_out[...])
    store_products(xs, gs, None, out_ref)


def project_pieces_kernel(plan, with_acc, n_pieces, *refs):
    x_refs, (own_in, own_out) = refs[:4], refs[4:6]
    pieces = refs[6 : 6 + n_pieces]
    acc_ref = refs[6 + n_pieces] if with_acc else None
    out_ref, w_in, w_out = refs[6 + n_pieces + with_acc :]
    z = lax.axis_index("dp")
    q = lax.axis_index(PLANE)
    core = lax.axis_index("mp")
    rin, rout = own_in.shape[0], own_out.shape[0]
    quarter = own_in.shape[1] // 4
    xs, gs = 0.0, 0.0
    at = 0
    for dq, col, width, rows in plan:
        other = q ^ (core * (3 ^ dq) + (1 - core) * dq) if dq in (1, 2) else q ^ dq
        start = pl.multiple_of(other * quarter + col, 128)
        cols = pl.ds(start, width)
        here = slice(at, at + width)
        at += width
        w_in[pl.ds(pl.multiple_of(z * rin, rin), rin), here] = own_in[:, cols]
        w_out[pl.ds(pl.multiple_of(z * rout, rout), rout), here] = own_out[:, cols]
        for p, row, k in rows:
            dst_in = pl.multiple_of((z ^ k) * rin, rin)
            dst_out = pl.multiple_of((z ^ k) * rout, rout)
            w_in[pl.ds(dst_in, rin), here] = pieces[p][row : row + rin, :]
            w_out[pl.ds(dst_out, rout), here] = pieces[p][row + rin : row + rin + rout, :]
        xs += nt(both(x_refs[0], x_refs[2], cols), w_in[:, here])
        gs += nt(both(x_refs[1], x_refs[3], cols), w_out[:, here])
    store_products(xs, gs, acc_ref, out_ref)


def moments_kernel(len_tr, len_te, mine, other, fac_ref, gte_ref, gtr_ref):
    tokens = mine.shape[0] // 3
    ki = mine.shape[1]
    ko = ki // 2
    total = mine[...] + other[...]
    rows = lax.broadcasted_iota(jnp.int32, (tokens, ki), 0)
    n_tr, n_te = len_tr[0], len_te[0]
    x_tr = jnp.where(rows < n_tr, total[:tokens], 0.0)
    x_te = jnp.where(rows < n_te, total[tokens : 2 * tokens], 0.0)
    g_both = total[2 * tokens :]
    g_tr = jnp.where(rows < n_tr, g_both, 0.0)[:, :ko]
    g_te = g_both[:, ko:]
    dot = functools.partial(
        lax.dot_general, dimension_numbers=TN, precision=HI,
        preferred_element_type=jnp.float32,
    )
    c_in = dot(x_tr, x_tr)
    c_out = dot(g_tr, g_tr)
    half = ki // 2
    fac_ref[:half, :] = c_in[:half, :]
    fac_ref[half:ki, :half] = c_in[half:, half:]
    fac_ref[half:ki, half:] = c_out
    fac_ref[ki:, :] = jnp.full((8, ki), n_tr.astype(jnp.float32))
    grad_tr = dot(x_tr, g_tr) / n_tr.astype(jnp.float32)
    grad_te = dot(x_te, g_te) / n_te.astype(jnp.float32)
    gtr_ref[...] = grad_tr
    gte_ref[0, :, :ko] = grad_te[:half]
    gte_ref[0, :, ko:] = grad_te[half:]


def wide(x, rows, cols=LANES):
    if x.shape[1] < cols:
        x = jnp.concatenate([x, jnp.zeros((x.shape[0], cols - x.shape[1]), x.dtype)], axis=1)
    if x.shape[0] < rows:
        x = jnp.concatenate([x, jnp.zeros((rows - x.shape[0], cols), x.dtype)], axis=0)
    return x


def parts(x):
    high = x.astype(jnp.bfloat16)
    return high, (x - high.astype(jnp.float32)).astype(jnp.bfloat16)


def right(x):
    high, low = parts(wide(x, LANES))
    upper = jnp.concatenate([high, low], axis=1)
    lower = jnp.concatenate([jnp.zeros_like(high), high], axis=1)
    return jnp.concatenate([upper, lower], axis=0)


def mm3(x, packed):
    both = jnp.dot(
        jnp.concatenate(parts(x), axis=1), packed, preferred_element_type=jnp.float32
    )
    return both[:, :LANES] + both[:, LANES:]


def damped(c):
    n = c.shape[0]
    i = lax.broadcasted_iota(jnp.int32, c.shape, 0)
    j = lax.broadcasted_iota(jnp.int32, c.shape, 1)
    eye = (i == j).astype(jnp.float32)
    trace = jnp.sum(jnp.sum(c * eye, axis=0, keepdims=True), axis=1, keepdims=True)
    low = 0.1 * trace / n
    a = c + low * eye
    high = jnp.max(jnp.sum(jnp.abs(a), axis=0, keepdims=True), axis=1, keepdims=True)
    return a, eye, low, jnp.minimum(high, trace + low)


def inverses(matrices):
    state = []
    for c in matrices:
        a, eye, low, high = damped(c)
        scale = 2.0 / (low + high)
        r = (high - low) / (high + low)
        state.append((a, eye, scale * a, scale * eye, scale, r))
    for step in range(NEWTON_STEPS):
        nxt = []
        for a, eye, m, x, scale, r in state:
            s = 2.0 / (2.0 - r * r)
            n = m.shape[0]
            if step == 0:
                mx = s * (2.0 * m - mm3(m, right(m)))
                xx = s * (2.0 * x - scale * m)
            else:
                both = mm3(jnp.concatenate([m, x], axis=0), right(m))
                mx = s * (2.0 * m - both[:n])
                xx = s * (2.0 * x - both[n:])
            nxt.append((a, eye, mx, xx, scale, r * r / (2.0 - r * r)))
        state = nxt
    result = []
    for a, eye, m, x, scale, r in state:
        n = a.shape[0]
        residual = eye - jnp.dot(
            a[:, :n], x, precision=HI, preferred_element_type=jnp.float32
        )
        result.append(x + mm3(x, right(residual)))
    return result


def side_kernel(fac_ref, gtr_ref, out_ref):
    ki = fac_ref.shape[1]
    half = ki // 2
    top = fac_ref[:half, :]
    low = fac_ref[half:ki, :]
    c_in = jnp.concatenate(
        [top, jnp.concatenate([top[:, half:].T, low[:, :half]], axis=1)], axis=0
    )
    count = fac_ref[ki : ki + 1, :1]
    inv_in, inv_out = inverses([c_in, wide(low[:, half:], half)])
    side = mm3(mm3(inv_in, right(gtr_ref[...])), right(inv_out)) * (count * count)
    out_ref[:, :half] = side[:half, :half]
    out_ref[:, half:] = side[half:, :half]


def scores_kernel(order, n_blk, side_ref, gte_ref, out_ref):
    z = lax.axis_index("dp")
    b = lax.axis_index("blk")
    lane = lax.broadcasted_iota(jnp.int32, out_ref.shape, 1)
    row = jnp.zeros(out_ref.shape, jnp.float32)
    side = side_ref[...]
    sums = [jnp.sum(side * gte_ref[p], axis=0, keepdims=True) for p in range(len(order))]
    values = jnp.sum(jnp.concatenate(sums, axis=0), axis=1, keepdims=True)
    for p, (dz, db) in enumerate(order):
        row = jnp.where(lane == (z ^ dz) * n_blk + (b ^ db), values[p : p + 1, :], row)
    out_ref[...] = row


def project(xs, w_in, w_out, n_groups, n_dp, n_blk):
    tokens, width = xs[0].shape
    rin, rout = w_in.shape[0], w_out.shape[0]
    ki, ko = rin * n_dp, rout * n_dp
    out_shape = jax.ShapeDtypeStruct((3 * tokens, ki), jnp.float32)
    if (n_groups, n_dp, n_blk) != (2, 4, 2):
        w_in = lax.all_gather(w_in, "dp", axis=0, tiled=True)
        w_out = lax.all_gather(w_out, "dp", axis=0, tiled=True)
        return call(project_kernel, out_shape, [vmem()] * 6, (*xs, w_in, w_out))

    part = width // 8
    shard = rin + rout
    in_hbm = [pltpu.with_memory_space_constraint(w, pltpu.HBM) for w in (w_in, w_out)]
    *halves, opposite = call(
        slice_kernel,
        tuple(
            pltpu.VMEM((shard, n), jnp.bfloat16) for n in (part, part, 2 * part)),
        [pl.BlockSpec(memory_space=pltpu.HBM)] * 2,
        in_hbm,
        limit=1,
        scratch_shapes=[pltpu.SemaphoreType.DMA((6,))],
    )
    operands = (*xs, w_in, w_out)
    *xs, w_in, w_out = call(
        functools.partial(load_kernel, 6),
        tuple(pltpu.VMEM(x.shape, x.dtype) for x in operands),
        [pl.BlockSpec(memory_space=pltpu.HBM)] * 6,
        [pltpu.with_memory_space_constraint(x, pltpu.HBM) for x in operands],
        flops=1 << 30,
        scratch_shapes=[pltpu.SemaphoreType.DMA((12,))],
    )
    far = [swap(h, "dp", n_dp, 2) for h in halves]
    far_op = swap(opposite, "dp", n_dp, 2)
    both_a = stack((halves[0], far[0]), w_out)
    near_a = swap(both_a, "dp", n_dp, 1)
    both_b = stack((halves[1], far[1]))
    near_b = swap(both_b, "dp", n_dp, 1)
    za = stack((far[0], near_a))
    along_x, along_y = (0, 1), (1, 0)
    xa = mixed(za, PLANE, (n_groups, n_blk), along_x, along_y)
    ya = mixed(za, PLANE, (n_groups, n_blk), along_y, along_x)
    both_op = stack((opposite, far_op))
    near_op = swap(both_op, "dp", n_dp, 1)
    zb = stack((far[1], near_b))
    xb = mixed(zb, PLANE, (n_groups, n_blk), along_x, along_y)
    yb = mixed(zb, PLANE, (n_groups, n_blk), along_y, along_x)

    def accumulate(plan, pieces, acc):
        args = (*xs, w_in, w_out, *pieces) + (() if acc is None else (acc,))
        total = sum(width for _, _, width, _ in plan)
        return call(
            functools.partial(project_pieces_kernel, plan, acc is not None, len(pieces)),
            out_shape,
            [vmem()] * len(args),
            args,
            flops=1 << 30,
            scratch_shapes=[
                pltpu.VMEM((ki, total), jnp.bfloat16),
                pltpu.VMEM((ko, total), jnp.bfloat16),
            ],
        )

    def stacked(p):
        return tuple((p, i * shard, k) for i, k in enumerate((2, 1, 3)))

    acc = accumulate(
        ((0, 0, part, stacked(0)), (0, part, part, stacked(1))), (za, zb), None)
    acc = accumulate(
        ((1, 0, part, stacked(0)), (2, 0, part, stacked(1))), (xa, ya), acc)
    return accumulate(
        (
            (1, part, part, stacked(0)),
            (2, part, part, stacked(1)),
            (3, 0, 2 * part, ((2, 0, 2), (3, 0, 1), (3, shard, 3))),
        ),
        (xb, yb, far_op, near_op),
        acc,
    )


def per_device(
    n_groups, n_dp, n_blk, train_inputs, train_cotangents, train_lengths,
    test_inputs, test_cotangents, test_lengths, proj_in, proj_out,
):
    _, tokens, width = train_inputs.shape
    xs = [a.reshape(tokens, width) for a in (
        train_inputs, train_cotangents, test_inputs, test_cotangents)]
    part = project(xs, proj_in.T, proj_out.T, n_groups, n_dp, n_blk)
    ki = part.shape[1]
    ko = ki // 2
    other = swap(part, "mp", 2, 1)
    fac, gte, gtr = call(
        moments_kernel,
        (
            jax.ShapeDtypeStruct((ki + 8, ki), jnp.float32),
            jax.ShapeDtypeStruct((1, ki // 2, ki), jnp.float32),
            jax.ShapeDtypeStruct((ki, ko), jnp.float32),
        ),
        [smem(), smem(), vmem(), vmem()],
        (train_lengths, test_lengths, part, other),
    )
    order = [(0, 0)]
    for axis, count in (("dp", n_dp), ("blk", n_blk)):
        for k in bits(count):
            gte = jnp.concatenate([gte, swap(gte, axis, count, k)], axis=0)
            order += [(dz ^ k, db) if axis == "dp" else (dz, db ^ k) for dz, db in order]
    steps_z = [(k, 0) for k in bits(n_dp)]
    steps_x = [(0, k) for k in bits(n_blk)]
    for step0, step1 in zip(steps_x + steps_z, steps_z + steps_x):
        fac = fac + mixed(fac, ("dp", "blk"), (n_dp, n_blk), step0, step1)
    side = call(
        side_kernel,
        jax.ShapeDtypeStruct((ki // 2, ki), jnp.float32),
        [vmem()] * 2,
        (fac, gtr),
        flops=4 << 30,
    )
    return call(
        functools.partial(scores_kernel, order, n_blk),
        jax.ShapeDtypeStruct((1, n_dp * n_blk), jnp.float32),
        [vmem()] * 2,
        (side, gte),
    )


def solution(mesh):
    feature = P(("groups", "dp", "blk"), None, "mp")
    length = P(("groups", "dp", "blk"))
    weight = P("mp", "dp")
    shape = mesh.shape
    return jax.shard_map(
        functools.partial(per_device, shape["groups"], shape["dp"], shape["blk"]),
        mesh=mesh,
        in_specs=(feature, feature, length, feature, feature, length, weight, weight),
        out_specs=P(("groups", "dp", "blk"), None),
        check_vma=False,
    )
```

```python
import functools

import jax
import jax.numpy as jnp
from jax import lax
from jax.experimental import pallas as pl
from jax.experimental.pallas import tpu as pltpu
from jax.sharding import PartitionSpec as P

HI = lax.Precision.HIGHEST
NT = (((1,), (1,)), ((), ()))
TN = (((0,), (0,)), ((), ()))
NEWTON_STEPS = 7
PLANE = ("groups", "blk")
LANES = 128


def vmem():
    return pl.BlockSpec(memory_space=pltpu.VMEM)


def smem():
    return pl.BlockSpec(memory_space=pltpu.SMEM)


def call(kernel, out_shape, in_specs, args, flops=0, limit=16, **kw):
    return pl.pallas_call(
        kernel,
        out_shape=out_shape,
        in_specs=in_specs,
        out_specs=jax.tree.map(lambda _: vmem(), out_shape),
        compiler_params=pltpu.CompilerParams(vmem_limit_bytes=limit * 1024 * 1024),
        cost_estimate=pl.CostEstimate(flops=flops, bytes_accessed=1 << 16, transcendentals=0),
        **kw,
    )(*args)


def swap(x, axis, count, k):
    return lax.ppermute(x, axis, [(i, i ^ k) for i in range(count)])


def mixed(x, axes, counts, step0, step1):
    pairs = []
    for i in range(counts[0]):
        for j in range(counts[1]):
            for core, (di, dj) in enumerate((step0, step1)):
                pairs.append((
                    (i * counts[1] + j) * 2 + core,
                    ((i ^ di) * counts[1] + (j ^ dj)) * 2 + core,
                ))
    return lax.ppermute(x, (*axes, "mp"), pairs)


def bits(count):
    return [1 << s for s in reversed(range(count.bit_length() - 1))]


def load_kernel(n, *refs):
    srcs, dsts, sem = refs[:n], refs[n : 2 * n], refs[2 * n]
    copies = []
    for i, (src, dst) in enumerate(zip(srcs, dsts)):
        rows = src.shape[0] // 2
        for h in range(2):
            part = pl.ds(h * rows, rows)
            copies.append(pltpu.make_async_copy(src.at[part], dst.at[part], sem.at[2 * i + h]))
    for c in copies:
        c.start()
    for c in copies:
        c.wait()


def stack_kernel(n, *refs):
    at = 0
    for src in refs[:n]:
        refs[-1][at : at + src.shape[0], :] = src[...]
        at += src.shape[0]


def stack(parts, after=None):
    rows = sum(p.shape[0] for p in parts)
    extra = () if after is None else (after,)
    return call(
        functools.partial(stack_kernel, len(parts)),
        pltpu.VMEM((rows, parts[0].shape[1]), parts[0].dtype),
        [vmem()] * len(parts) + [pl.BlockSpec(memory_space=pl.ANY)] * len(extra),
        (*parts, *extra),
        limit=1,
    )


def store_products(x_parts, g_parts, acc_ref, out_ref):
    tokens = out_ref.shape[0] // 3
    ko = g_parts[0].shape[1]
    for n in range(2):
        rows = slice(n * tokens, (n + 1) * tokens)
        prior = 0.0 if acc_ref is None else acc_ref[rows, :]
        out_ref[rows, :] = prior + x_parts[n]
    rows = slice(2 * tokens, 3 * tokens)
    for n in range(2):
        cols = slice(n * ko, (n + 1) * ko)
        prior = 0.0 if acc_ref is None else acc_ref[rows, cols]
        out_ref[rows, cols] = prior + g_parts[n]


def nt(a, b):
    return lax.dot_general(a, b, NT, preferred_element_type=jnp.float32)


def project_kernel(*refs):
    x_refs, (w_in, w_out, out_ref) = refs[:4], refs[4:]
    xs = [nt(x_refs[n][...], w_in[...]) for n in (0, 2)]
    gs = [nt(x_refs[n][...], w_out[...]) for n in (1, 3)]
    store_products(xs, gs, None, out_ref)


def project_pieces_kernel(plan, with_acc, n_pieces, *refs):
    x_refs, (own_in, own_out) = refs[:4], refs[4:6]
    pieces = refs[6 : 6 + n_pieces]
    acc_ref = refs[6 + n_pieces] if with_acc else None
    out_ref, w_in, w_out = refs[6 + n_pieces + with_acc :]
    z = lax.axis_index("dp")
    q = lax.axis_index(PLANE)
    core = lax.axis_index("mp")
    rin, rout = own_in.shape[0], own_out.shape[0]
    quarter = own_in.shape[1] // 4
    xs, gs = [0.0, 0.0], [0.0, 0.0]
    at = 0
    for dq, col, width, rows in plan:
        other = q ^ (core * (3 ^ dq) + (1 - core) * dq) if dq in (1, 2) else q ^ dq
        start = pl.multiple_of(other * quarter + col, 128)
        cols = pl.ds(start, width)
        here = slice(at, at + width)
        at += width
        w_in[pl.ds(pl.multiple_of(z * rin, rin), rin), here] = own_in[:, cols]
        w_out[pl.ds(pl.multiple_of(z * rout, rout), rout), here] = own_out[:, cols]
        for p, row, k in rows:
            dst_in = pl.multiple_of((z ^ k) * rin, rin)
            dst_out = pl.multiple_of((z ^ k) * rout, rout)
            w_in[pl.ds(dst_in, rin), here] = pieces[p][row : row + rin, :]
            w_out[pl.ds(dst_out, rout), here] = pieces[p][row + rin : row + rin + rout, :]
        for m in range(2):
            xs[m] += nt(x_refs[2 * m][:, cols], w_in[:, here])
            gs[m] += nt(x_refs[2 * m + 1][:, cols], w_out[:, here])
    store_products(xs, gs, acc_ref, out_ref)


def moments_kernel(len_tr, len_te, mine, other, fac_ref, gte_ref, gtr_ref):
    tokens = mine.shape[0] // 3
    ki = mine.shape[1]
    ko = ki // 2
    total = mine[...] + other[...]
    rows = lax.broadcasted_iota(jnp.int32, (tokens, ki), 0)
    n_tr, n_te = len_tr[0], len_te[0]
    x_tr = jnp.where(rows < n_tr, total[:tokens], 0.0)
    x_te = jnp.where(rows < n_te, total[tokens : 2 * tokens], 0.0)
    g_both = total[2 * tokens :]
    g_tr = jnp.where(rows < n_tr, g_both, 0.0)[:, :ko]
    g_te = g_both[:, ko:]
    dot = functools.partial(
        lax.dot_general, dimension_numbers=TN, precision=HI,
        preferred_element_type=jnp.float32,
    )
    c_in = dot(x_tr, x_tr)
    c_out = dot(g_tr, g_tr)
    half = ki // 2
    fac_ref[:half, :] = c_in[:half, :]
    fac_ref[half:ki, :half] = c_in[half:, half:]
    fac_ref[half:ki, half:] = c_out
    fac_ref[ki:, :] = jnp.full((8, ki), n_tr.astype(jnp.float32))
    grad_tr = dot(x_tr, g_tr) / n_tr.astype(jnp.float32)
    grad_te = dot(x_te, g_te) / n_te.astype(jnp.float32)
    gtr_ref[...] = grad_tr
    gte_ref[0, :, :ko] = grad_te[:half]
    gte_ref[0, :, ko:] = grad_te[half:]


def wide(x, rows, cols=LANES):
    if x.shape[1] < cols:
        x = jnp.concatenate([x, jnp.zeros((x.shape[0], cols - x.shape[1]), x.dtype)], axis=1)
    if x.shape[0] < rows:
        x = jnp.concatenate([x, jnp.zeros((rows - x.shape[0], cols), x.dtype)], axis=0)
    return x


def parts(x):
    high = x.astype(jnp.bfloat16)
    return high, (x - high.astype(jnp.float32)).astype(jnp.bfloat16)


def right(x):
    high, low = parts(wide(x, LANES))
    upper = jnp.concatenate([high, low], axis=1)
    lower = jnp.concatenate([jnp.zeros_like(high), high], axis=1)
    return jnp.concatenate([upper, lower], axis=0)


def mm3(x, packed):
    both = jnp.dot(
        jnp.concatenate(parts(x), axis=1), packed, preferred_element_type=jnp.float32
    )
    return both[:, :LANES] + both[:, LANES:]


def damped(c):
    n = c.shape[0]
    i = lax.broadcasted_iota(jnp.int32, c.shape, 0)
    j = lax.broadcasted_iota(jnp.int32, c.shape, 1)
    eye = (i == j).astype(jnp.float32)
    trace = jnp.sum(jnp.sum(c * eye, axis=0, keepdims=True), axis=1, keepdims=True)
    low = 0.1 * trace / n
    a = c + low * eye
    high = jnp.max(jnp.sum(jnp.abs(a), axis=0, keepdims=True), axis=1, keepdims=True)
    return a, eye, low, jnp.minimum(high, trace + low)


def inverses(matrices):
    state = []
    for c in matrices:
        a, eye, low, high = damped(c)
        scale = 2.0 / (low + high)
        r = (high - low) / (high + low)
        state.append((a, eye, scale * a, scale * eye, scale, r))
    for step in range(NEWTON_STEPS):
        nxt = []
        for a, eye, m, x, scale, r in state:
            s = 2.0 / (2.0 - r * r)
            n = m.shape[0]
            if step == 0:
                mx = s * (2.0 * m - mm3(m, right(m)))
                xx = s * (2.0 * x - scale * m)
            else:
                both = mm3(jnp.concatenate([m, x], axis=0), right(m))
                mx = s * (2.0 * m - both[:n])
                xx = s * (2.0 * x - both[n:])
            nxt.append((a, eye, mx, xx, scale, r * r / (2.0 - r * r)))
        state = nxt
    result = []
    for a, eye, m, x, scale, r in state:
        n = a.shape[0]
        residual = eye - jnp.dot(
            a[:, :n], x, precision=HI, preferred_element_type=jnp.float32
        )
        result.append(x + mm3(x, right(residual)))
    return result


def side_kernel(fac_ref, gtr_ref, out_ref):
    ki = fac_ref.shape[1]
    half = ki // 2
    top = fac_ref[:half, :]
    low = fac_ref[half:ki, :]
    c_in = jnp.concatenate(
        [top, jnp.concatenate([top[:, half:].T, low[:, :half]], axis=1)], axis=0
    )
    count = fac_ref[ki : ki + 1, :1]
    inv_in, inv_out = inverses([c_in, wide(low[:, half:], half)])
    side = mm3(mm3(inv_in, right(gtr_ref[...])), right(inv_out)) * (count * count)
    out_ref[:, :half] = side[:half, :half]
    out_ref[:, half:] = side[half:, :half]


def scores_kernel(order, n_blk, side_ref, gte_ref, out_ref):
    z = lax.axis_index("dp")
    b = lax.axis_index("blk")
    side = side_ref[...]
    peers = gte_ref.shape[0]
    sums = jnp.sum(side[None] * gte_ref[...], axis=1)
    values = jnp.sum(sums, axis=1, keepdims=True)
    where = lax.broadcasted_iota(jnp.int32, (peers, out_ref.shape[1]), 0)
    lane = lax.broadcasted_iota(jnp.int32, (peers, out_ref.shape[1]), 1)
    place = jnp.zeros_like(lane)
    for p, (dz, db) in enumerate(order):
        place = jnp.where(where == p, (z ^ dz) * n_blk + (b ^ db), place)
    out_ref[...] = jnp.sum(jnp.where(lane == place, values, 0.0), axis=0, keepdims=True)


def project(xs, w_in, w_out, n_groups, n_dp, n_blk):
    tokens, width = xs[0].shape
    rin, rout = w_in.shape[0], w_out.shape[0]
    ki, ko = rin * n_dp, rout * n_dp
    out_shape = jax.ShapeDtypeStruct((3 * tokens, ki), jnp.float32)
    if (n_groups, n_dp, n_blk) != (2, 4, 2):
        w_in = lax.all_gather(w_in, "dp", axis=0, tiled=True)
        w_out = lax.all_gather(w_out, "dp", axis=0, tiled=True)
        return call(project_kernel, out_shape, [vmem()] * 6, (*xs, w_in, w_out))

    part = width // 8
    shard = rin + rout
    q = lax.axis_index(PLANE)
    whole = jnp.concatenate([w_in, w_out], axis=0)
    mine = lax.dynamic_slice(whole, (0, q * 2 * part), (shard, 2 * part))
    opposite = lax.dynamic_slice(whole, (0, (q ^ 3) * 2 * part), (shard, 2 * part))
    operands = (*xs, w_in, w_out)
    *xs, w_in, w_out = call(
        functools.partial(load_kernel, 6),
        tuple(pltpu.VMEM(x.shape, x.dtype) for x in operands),
        [pl.BlockSpec(memory_space=pltpu.HBM)] * 6,
        [pltpu.with_memory_space_constraint(x, pltpu.HBM) for x in operands],
        flops=1 << 30,
        scratch_shapes=[pltpu.SemaphoreType.DMA((12,))],
    )
    halves = [mine[:, :part], mine[:, part:]]
    far = [swap(h, "dp", n_dp, 2) for h in halves]
    far_op = swap(opposite, "dp", n_dp, 2)
    both_a = stack((halves[0], far[0]), w_out)
    near_a = swap(both_a, "dp", n_dp, 1)
    both_b = stack((halves[1], far[1]))
    near_b = swap(both_b, "dp", n_dp, 1)
    za = stack((far[0], near_a))
    along_x, along_y = (0, 1), (1, 0)
    xa = mixed(za, PLANE, (n_groups, n_blk), along_x, along_y)
    ya = mixed(za, PLANE, (n_groups, n_blk), along_y, along_x)
    both_op = stack((opposite, far_op))
    near_op = swap(both_op, "dp", n_dp, 1)
    zb = stack((far[1], near_b))
    xb = mixed(zb, PLANE, (n_groups, n_blk), along_x, along_y)
    yb = mixed(zb, PLANE, (n_groups, n_blk), along_y, along_x)

    def accumulate(plan, pieces, acc):
        args = (*xs, w_in, w_out, *pieces) + (() if acc is None else (acc,))
        total = sum(width for _, _, width, _ in plan)
        return call(
            functools.partial(project_pieces_kernel, plan, acc is not None, len(pieces)),
            out_shape,
            [vmem()] * len(args),
            args,
            flops=1 << 30,
            scratch_shapes=[
                pltpu.VMEM((ki, total), jnp.bfloat16),
                pltpu.VMEM((ko, total), jnp.bfloat16),
            ],
        )

    def stacked(p):
        return tuple((p, i * shard, k) for i, k in enumerate((2, 1, 3)))

    acc = accumulate(
        ((0, 0, part, stacked(0)), (0, part, part, stacked(1))), (za, zb), None)
    acc = accumulate(
        ((1, 0, part, stacked(0)), (2, 0, part, stacked(1))), (xa, ya), acc)
    acc = accumulate(
        ((3, 0, 2 * part, ((0, 0, 2), (1, 0, 1), (1, shard, 3))),), (far_op, near_op), acc)
    return accumulate(
        ((1, part, part, stacked(0)), (2, part, part, stacked(1))), (xb, yb), acc)


def per_device(
    n_groups, n_dp, n_blk, train_inputs, train_cotangents, train_lengths,
    test_inputs, test_cotangents, test_lengths, proj_in, proj_out,
):
    _, tokens, width = train_inputs.shape
    xs = [a.reshape(tokens, width) for a in (
        train_inputs, train_cotangents, test_inputs, test_cotangents)]
    part = project(xs, proj_in.T, proj_out.T, n_groups, n_dp, n_blk)
    ki = part.shape[1]
    ko = ki // 2
    other = swap(part, "mp", 2, 1)
    fac, gte, gtr = call(
        moments_kernel,
        (
            jax.ShapeDtypeStruct((ki + 8, ki), jnp.float32),
            jax.ShapeDtypeStruct((1, ki // 2, ki), jnp.float32),
            jax.ShapeDtypeStruct((ki, ko), jnp.float32),
        ),
        [smem(), smem(), vmem(), vmem()],
        (train_lengths, test_lengths, part, other),
    )
    order = [(0, 0)]
    for axis, count in (("dp", n_dp), ("blk", n_blk)):
        for k in bits(count):
            gte = jnp.concatenate([gte, swap(gte, axis, count, k)], axis=0)
            order += [(dz ^ k, db) if axis == "dp" else (dz, db ^ k) for dz, db in order]
    steps_z = [(k, 0) for k in bits(n_dp)]
    steps_x = [(0, k) for k in bits(n_blk)]
    for step0, step1 in zip(steps_x + steps_z, steps_z + steps_x):
        fac = fac + mixed(fac, ("dp", "blk"), (n_dp, n_blk), step0, step1)
    side = call(
        side_kernel,
        jax.ShapeDtypeStruct((ki // 2, ki), jnp.float32),
        [vmem()] * 2,
        (fac, gtr),
        flops=4 << 30,
    )
    return call(
        functools.partial(scores_kernel, order, n_blk),
        jax.ShapeDtypeStruct((1, n_dp * n_blk), jnp.float32),
        [vmem()] * 2,
        (side, gte),
    )


def solution(mesh):
    feature = P(("groups", "dp", "blk"), None, "mp")
    length = P(("groups", "dp", "blk"))
    weight = P("mp", "dp")
    shape = mesh.shape
    return jax.shard_map(
        functools.partial(per_device, shape["groups"], shape["dp"], shape["blk"]),
        mesh=mesh,
        in_specs=(feature, feature, length, feature, feature, length, weight, weight),
        out_specs=P(("groups", "dp", "blk"), None),
        check_vma=False,
    )
```

```python
import functools

import jax
import jax.numpy as jnp
from jax import lax
from jax.experimental import pallas as pl
from jax.experimental.pallas import tpu as pltpu
from jax.sharding import PartitionSpec as P

HI = lax.Precision.HIGHEST
NT = (((1,), (1,)), ((), ()))
TN = (((0,), (0,)), ((), ()))
NEWTON_STEPS = 7
PLANE = ("groups", "blk")
LANES = 128


def vmem():
    return pl.BlockSpec(memory_space=pltpu.VMEM)


def smem():
    return pl.BlockSpec(memory_space=pltpu.SMEM)


def call(kernel, out_shape, in_specs, args, flops=0, limit=16, **kw):
    return pl.pallas_call(
        kernel,
        out_shape=out_shape,
        in_specs=in_specs,
        out_specs=jax.tree.map(lambda _: vmem(), out_shape),
        compiler_params=pltpu.CompilerParams(vmem_limit_bytes=limit * 1024 * 1024),
        cost_estimate=pl.CostEstimate(flops=flops, bytes_accessed=1 << 16, transcendentals=0),
        **kw,
    )(*args)


def swap(x, axis, count, k):
    return lax.ppermute(x, axis, [(i, i ^ k) for i in range(count)])


def mixed(x, axes, counts, step0, step1):
    pairs = []
    for i in range(counts[0]):
        for j in range(counts[1]):
            for core, (di, dj) in enumerate((step0, step1)):
                pairs.append((
                    (i * counts[1] + j) * 2 + core,
                    ((i ^ di) * counts[1] + (j ^ dj)) * 2 + core,
                ))
    return lax.ppermute(x, (*axes, "mp"), pairs)


def bits(count):
    return [1 << s for s in reversed(range(count.bit_length() - 1))]


def load_kernel(n, *refs):
    srcs, dsts, sem = refs[:n], refs[n : 2 * n], refs[2 * n]
    copies = []
    for i, (src, dst) in enumerate(zip(srcs, dsts)):
        rows = src.shape[0] // 2
        for h in range(2):
            part = pl.ds(h * rows, rows)
            copies.append(pltpu.make_async_copy(src.at[part], dst.at[part], sem.at[2 * i + h]))
    for c in copies:
        c.start()
    for c in copies:
        c.wait()


def stack_kernel(n, *refs):
    at = 0
    for src in refs[:n]:
        refs[-1][at : at + src.shape[0], :] = src[...]
        at += src.shape[0]


def stack(parts, after=None):
    rows = sum(p.shape[0] for p in parts)
    extra = () if after is None else (after,)
    return call(
        functools.partial(stack_kernel, len(parts)),
        pltpu.VMEM((rows, parts[0].shape[1]), parts[0].dtype),
        [vmem()] * len(parts) + [pl.BlockSpec(memory_space=pl.ANY)] * len(extra),
        (*parts, *extra),
        limit=1,
    )


def store_products(x_parts, g_parts, acc_ref, out_ref):
    tokens = out_ref.shape[0] // 3
    ko = g_parts[0].shape[1]
    for n in range(2):
        rows = slice(n * tokens, (n + 1) * tokens)
        prior = 0.0 if acc_ref is None else acc_ref[rows, :]
        out_ref[rows, :] = prior + x_parts[n]
    rows = slice(2 * tokens, 3 * tokens)
    for n in range(2):
        cols = slice(n * ko, (n + 1) * ko)
        prior = 0.0 if acc_ref is None else acc_ref[rows, cols]
        out_ref[rows, cols] = prior + g_parts[n]


def nt(a, b):
    return lax.dot_general(a, b, NT, preferred_element_type=jnp.float32)


def project_kernel(*refs):
    x_refs, (w_in, w_out, out_ref) = refs[:4], refs[4:]
    xs = [nt(x_refs[n][...], w_in[...]) for n in (0, 2)]
    gs = [nt(x_refs[n][...], w_out[...]) for n in (1, 3)]
    store_products(xs, gs, None, out_ref)


def project_pieces_kernel(plan, with_acc, n_pieces, *refs):
    x_refs, (own_in, own_out) = refs[:4], refs[4:6]
    pieces = refs[6 : 6 + n_pieces]
    acc_ref = refs[6 + n_pieces] if with_acc else None
    out_ref, w_in, w_out = refs[6 + n_pieces + with_acc :]
    z = lax.axis_index("dp")
    q = lax.axis_index(PLANE)
    core = lax.axis_index("mp")
    rin, rout = own_in.shape[0], own_out.shape[0]
    quarter = own_in.shape[1] // 4
    xs, gs = [0.0, 0.0], [0.0, 0.0]
    at = 0
    for dq, col, width, rows in plan:
        other = q ^ (core * (3 ^ dq) + (1 - core) * dq) if dq in (1, 2) else q ^ dq
        start = pl.multiple_of(other * quarter + col, 128)
        cols = pl.ds(start, width)
        here = slice(at, at + width)
        at += width
        w_in[pl.ds(pl.multiple_of(z * rin, rin), rin), here] = own_in[:, cols]
        w_out[pl.ds(pl.multiple_of(z * rout, rout), rout), here] = own_out[:, cols]
        for p, row, k in rows:
            dst_in = pl.multiple_of((z ^ k) * rin, rin)
            dst_out = pl.multiple_of((z ^ k) * rout, rout)
            w_in[pl.ds(dst_in, rin), here] = pieces[p][row : row + rin, :]
            w_out[pl.ds(dst_out, rout), here] = pieces[p][row + rin : row + rin + rout, :]
        for m in range(2):
            xs[m] += nt(x_refs[2 * m][:, cols], w_in[:, here])
            gs[m] += nt(x_refs[2 * m + 1][:, cols], w_out[:, here])
    store_products(xs, gs, acc_ref, out_ref)


def moments_kernel(len_tr, len_te, mine, other, fac_ref, gte_ref, gtr_ref):
    tokens = mine.shape[0] // 3
    ki = mine.shape[1]
    ko = ki // 2
    total = mine[...] + other[...]
    rows = lax.broadcasted_iota(jnp.int32, (tokens, ki), 0)
    n_tr, n_te = len_tr[0], len_te[0]
    x_tr = jnp.where(rows < n_tr, total[:tokens], 0.0)
    x_te = jnp.where(rows < n_te, total[tokens : 2 * tokens], 0.0)
    g_both = total[2 * tokens :]
    g_tr = jnp.where(rows < n_tr, g_both, 0.0)[:, :ko]
    g_te = g_both[:, ko:]
    dot = functools.partial(
        lax.dot_general, dimension_numbers=TN, precision=HI,
        preferred_element_type=jnp.float32,
    )
    c_in = dot(x_tr, x_tr)
    c_out = dot(g_tr, g_tr)
    half = ki // 2
    fac_ref[:half, :] = c_in[:half, :]
    fac_ref[half:ki, :half] = c_in[half:, half:]
    fac_ref[half:ki, half:] = c_out
    fac_ref[ki:, :] = jnp.full((8, ki), n_tr.astype(jnp.float32))
    grad_tr = dot(x_tr, g_tr) / n_tr.astype(jnp.float32)
    grad_te = dot(x_te, g_te) / n_te.astype(jnp.float32)
    gtr_ref[...] = grad_tr
    gte_ref[0, :, :ko] = grad_te[:half]
    gte_ref[0, :, ko:] = grad_te[half:]


def wide(x, rows, cols=LANES):
    if x.shape[1] < cols:
        x = jnp.concatenate([x, jnp.zeros((x.shape[0], cols - x.shape[1]), x.dtype)], axis=1)
    if x.shape[0] < rows:
        x = jnp.concatenate([x, jnp.zeros((rows - x.shape[0], cols), x.dtype)], axis=0)
    return x


def parts(x):
    high = x.astype(jnp.bfloat16)
    return high, (x - high.astype(jnp.float32)).astype(jnp.bfloat16)


def right(x):
    high, low = parts(wide(x, LANES))
    upper = jnp.concatenate([high, low], axis=1)
    lower = jnp.concatenate([jnp.zeros_like(high), high], axis=1)
    return jnp.concatenate([upper, lower], axis=0)


def mm3(x, packed):
    both = jnp.dot(
        jnp.concatenate(parts(x), axis=1), packed, preferred_element_type=jnp.float32
    )
    return both[:, :LANES] + both[:, LANES:]


def damped(c):
    n = c.shape[0]
    i = lax.broadcasted_iota(jnp.int32, c.shape, 0)
    j = lax.broadcasted_iota(jnp.int32, c.shape, 1)
    eye = (i == j).astype(jnp.float32)
    trace = jnp.sum(jnp.sum(c * eye, axis=0, keepdims=True), axis=1, keepdims=True)
    low = 0.1 * trace / n
    a = c + low * eye
    high = jnp.max(jnp.sum(jnp.abs(a), axis=0, keepdims=True), axis=1, keepdims=True)
    return a, eye, low, jnp.minimum(high, trace + low)


def inverses(matrices):
    state = []
    for c in matrices:
        a, eye, low, high = damped(c)
        scale = 2.0 / (low + high)
        r = (high - low) / (high + low)
        state.append((a, eye, scale * a, scale * eye, scale, r))
    for step in range(NEWTON_STEPS):
        nxt = []
        for a, eye, m, x, scale, r in state:
            s = 2.0 / (2.0 - r * r)
            n = m.shape[0]
            if step == 0:
                mx = s * (2.0 * m - mm3(m, right(m)))
                xx = s * (2.0 * x - scale * m)
            else:
                both = mm3(jnp.concatenate([m, x], axis=0), right(m))
                mx = s * (2.0 * m - both[:n])
                xx = s * (2.0 * x - both[n:])
            nxt.append((a, eye, mx, xx, scale, r * r / (2.0 - r * r)))
        state = nxt
    result = []
    for a, eye, m, x, scale, r in state:
        n = a.shape[0]
        residual = eye - jnp.dot(
            a[:, :n], x, precision=HI, preferred_element_type=jnp.float32
        )
        result.append(x + mm3(x, right(residual)))
    return result


def side_kernel(fac_ref, gtr_ref, out_ref):
    ki = fac_ref.shape[1]
    half = ki // 2
    top = fac_ref[:half, :]
    low = fac_ref[half:ki, :]
    c_in = jnp.concatenate(
        [top, jnp.concatenate([top[:, half:].T, low[:, :half]], axis=1)], axis=0
    )
    count = fac_ref[ki : ki + 1, :1]
    inv_in, inv_out = inverses([c_in, wide(low[:, half:], half)])
    side = mm3(mm3(inv_in, right(gtr_ref[...])), right(inv_out)) * (count * count)
    out_ref[:, :half] = side[:half, :half]
    out_ref[:, half:] = side[half:, :half]


def scores_kernel(order, n_blk, side_ref, gte_ref, out_ref):
    z = lax.axis_index("dp")
    b = lax.axis_index("blk")
    lane = lax.broadcasted_iota(jnp.int32, out_ref.shape, 1)
    row = jnp.zeros(out_ref.shape, jnp.float32)
    side = side_ref[...]
    sums = [jnp.sum(side * gte_ref[p], axis=0, keepdims=True) for p in range(len(order))]
    values = jnp.sum(jnp.concatenate(sums, axis=0), axis=1, keepdims=True)
    for p, (dz, db) in enumerate(order):
        row = jnp.where(lane == (z ^ dz) * n_blk + (b ^ db), values[p : p + 1, :], row)
    out_ref[...] = row


def project(xs, w_in, w_out, n_groups, n_dp, n_blk):
    tokens, width = xs[0].shape
    rin, rout = w_in.shape[0], w_out.shape[0]
    ki, ko = rin * n_dp, rout * n_dp
    out_shape = jax.ShapeDtypeStruct((3 * tokens, ki), jnp.float32)
    if (n_groups, n_dp, n_blk) != (2, 4, 2):
        w_in = lax.all_gather(w_in, "dp", axis=0, tiled=True)
        w_out = lax.all_gather(w_out, "dp", axis=0, tiled=True)
        return call(project_kernel, out_shape, [vmem()] * 6, (*xs, w_in, w_out))

    part = width // 8
    shard = rin + rout
    q = lax.axis_index(PLANE)
    whole = jnp.concatenate([w_in, w_out], axis=0)
    mine = lax.dynamic_slice(whole, (0, q * 2 * part), (shard, 2 * part))
    opposite = lax.dynamic_slice(whole, (0, (q ^ 3) * 2 * part), (shard, 2 * part))
    operands = (*xs, w_in, w_out)
    *xs, w_in, w_out = call(
        functools.partial(load_kernel, 6),
        tuple(pltpu.VMEM(x.shape, x.dtype) for x in operands),
        [pl.BlockSpec(memory_space=pltpu.HBM)] * 6,
        [pltpu.with_memory_space_constraint(x, pltpu.HBM) for x in operands],
        flops=1 << 30,
        scratch_shapes=[pltpu.SemaphoreType.DMA((12,))],
    )
    halves = [mine[:, :part], mine[:, part:]]
    far = [swap(h, "dp", n_dp, 2) for h in halves]
    far_op = swap(opposite, "dp", n_dp, 2)
    both_a = stack((halves[0], far[0]), w_out)
    near_a = swap(both_a, "dp", n_dp, 1)
    both_b = stack((halves[1], far[1]))
    near_b = swap(both_b, "dp", n_dp, 1)
    za = stack((far[0], near_a))
    along_x, along_y = (0, 1), (1, 0)
    xa = mixed(za, PLANE, (n_groups, n_blk), along_x, along_y)
    ya = mixed(za, PLANE, (n_groups, n_blk), along_y, along_x)
    both_op = stack((opposite, far_op))
    near_op = swap(both_op, "dp", n_dp, 1)
    zb = stack((far[1], near_b))
    xb = mixed(zb, PLANE, (n_groups, n_blk), along_x, along_y)
    yb = mixed(zb, PLANE, (n_groups, n_blk), along_y, along_x)

    def accumulate(plan, pieces, acc):
        args = (*xs, w_in, w_out, *pieces) + (() if acc is None else (acc,))
        total = sum(width for _, _, width, _ in plan)
        return call(
            functools.partial(project_pieces_kernel, plan, acc is not None, len(pieces)),
            out_shape,
            [vmem()] * len(args),
            args,
            flops=1 << 28,
            scratch_shapes=[
                pltpu.VMEM((ki, total), jnp.bfloat16),
                pltpu.VMEM((ko, total), jnp.bfloat16),
            ],
        )

    def stacked(p):
        return tuple((p, i * shard, k) for i, k in enumerate((2, 1, 3)))

    acc = accumulate(
        ((0, 0, part, stacked(0)), (0, part, part, stacked(1))), (za, zb), None)
    acc = accumulate(
        ((1, 0, part, stacked(0)), (2, 0, part, stacked(1))), (xa, ya), acc)
    return accumulate(
        (
            (1, part, part, stacked(0)),
            (2, part, part, stacked(1)),
            (3, 0, 2 * part, ((2, 0, 2), (3, 0, 1), (3, shard, 3))),
        ),
        (xb, yb, far_op, near_op),
        acc,
    )


def per_device(
    n_groups, n_dp, n_blk, train_inputs, train_cotangents, train_lengths,
    test_inputs, test_cotangents, test_lengths, proj_in, proj_out,
):
    _, tokens, width = train_inputs.shape
    xs = [a.reshape(tokens, width) for a in (
        train_inputs, train_cotangents, test_inputs, test_cotangents)]
    part = project(xs, proj_in.T, proj_out.T, n_groups, n_dp, n_blk)
    ki = part.shape[1]
    ko = ki // 2
    other = swap(part, "mp", 2, 1)
    fac, gte, gtr = call(
        moments_kernel,
        (
            jax.ShapeDtypeStruct((ki + 8, ki), jnp.float32),
            jax.ShapeDtypeStruct((1, ki // 2, ki), jnp.float32),
            jax.ShapeDtypeStruct((ki, ko), jnp.float32),
        ),
        [smem(), smem(), vmem(), vmem()],
        (train_lengths, test_lengths, part, other),
    )
    order = [(0, 0)]
    for axis, count in (("dp", n_dp), ("blk", n_blk)):
        for k in bits(count):
            gte = jnp.concatenate([gte, swap(gte, axis, count, k)], axis=0)
            order += [(dz ^ k, db) if axis == "dp" else (dz, db ^ k) for dz, db in order]
    steps_z = [(k, 0) for k in bits(n_dp)]
    steps_x = [(0, k) for k in bits(n_blk)]
    for step0, step1 in zip(steps_x + steps_z, steps_z + steps_x):
        fac = fac + mixed(fac, ("dp", "blk"), (n_dp, n_blk), step0, step1)
    side = call(
        side_kernel,
        jax.ShapeDtypeStruct((ki // 2, ki), jnp.float32),
        [vmem()] * 2,
        (fac, gtr),
        flops=4 << 30,
    )
    return call(
        functools.partial(scores_kernel, order, n_blk),
        jax.ShapeDtypeStruct((1, n_dp * n_blk), jnp.float32),
        [vmem()] * 2,
        (side, gte),
    )


def solution(mesh):
    feature = P(("groups", "dp", "blk"), None, "mp")
    length = P(("groups", "dp", "blk"))
    weight = P("mp", "dp")
    shape = mesh.shape
    return jax.shard_map(
        functools.partial(per_device, shape["groups"], shape["dp"], shape["blk"]),
        mesh=mesh,
        in_specs=(feature, feature, length, feature, feature, length, weight, weight),
        out_specs=P(("groups", "dp", "blk"), None),
        check_vma=False,
    )
```

```python
import functools

import jax
import jax.numpy as jnp
from jax import lax
from jax.experimental import pallas as pl
from jax.experimental.pallas import tpu as pltpu
from jax.sharding import PartitionSpec as P

HI = lax.Precision.HIGHEST
NT = (((1,), (1,)), ((), ()))
TN = (((0,), (0,)), ((), ()))
NEWTON_STEPS = 7
PLANE = ("groups", "blk")
LANES = 128


def vmem():
    return pl.BlockSpec(memory_space=pltpu.VMEM)


def smem():
    return pl.BlockSpec(memory_space=pltpu.SMEM)


def call(kernel, out_shape, in_specs, args, flops=0, limit=16, **kw):
    return pl.pallas_call(
        kernel,
        out_shape=out_shape,
        in_specs=in_specs,
        out_specs=jax.tree.map(lambda _: vmem(), out_shape),
        compiler_params=pltpu.CompilerParams(vmem_limit_bytes=limit * 1024 * 1024),
        cost_estimate=pl.CostEstimate(flops=flops, bytes_accessed=1 << 16, transcendentals=0),
        **kw,
    )(*args)


def swap(x, axis, count, k):
    return lax.ppermute(x, axis, [(i, i ^ k) for i in range(count)])


def mixed(x, axes, counts, step0, step1):
    pairs = []
    for i in range(counts[0]):
        for j in range(counts[1]):
            for core, (di, dj) in enumerate((step0, step1)):
                pairs.append((
                    (i * counts[1] + j) * 2 + core,
                    ((i ^ di) * counts[1] + (j ^ dj)) * 2 + core,
                ))
    return lax.ppermute(x, (*axes, "mp"), pairs)


def bits(count):
    return [1 << s for s in reversed(range(count.bit_length() - 1))]


def load_kernel(n, *refs):
    srcs, dsts, sem = refs[:n], refs[n : 2 * n], refs[2 * n]
    copies = []
    for i, (src, dst) in enumerate(zip(srcs, dsts)):
        rows = src.shape[0] // 2
        for h in range(2):
            part = pl.ds(h * rows, rows)
            copies.append(pltpu.make_async_copy(src.at[part], dst.at[part], sem.at[2 * i + h]))
    for c in copies:
        c.start()
    for c in copies:
        c.wait()


def stack_kernel(n, *refs):
    at = 0
    for src in refs[:n]:
        refs[-1][at : at + src.shape[0], :] = src[...]
        at += src.shape[0]


def stack(parts, after=None):
    rows = sum(p.shape[0] for p in parts)
    extra = () if after is None else (after,)
    return call(
        functools.partial(stack_kernel, len(parts)),
        pltpu.VMEM((rows, parts[0].shape[1]), parts[0].dtype),
        [vmem()] * len(parts) + [pl.BlockSpec(memory_space=pl.ANY)] * len(extra),
        (*parts, *extra),
        limit=1,
    )


def store_products(x_parts, g_parts, acc_ref, out_ref):
    tokens = out_ref.shape[0] // 3
    ko = g_parts[0].shape[1]
    for n in range(2):
        rows = slice(n * tokens, (n + 1) * tokens)
        prior = 0.0 if acc_ref is None else acc_ref[rows, :]
        out_ref[rows, :] = prior + x_parts[n]
    rows = slice(2 * tokens, 3 * tokens)
    for n in range(2):
        cols = slice(n * ko, (n + 1) * ko)
        prior = 0.0 if acc_ref is None else acc_ref[rows, cols]
        out_ref[rows, cols] = prior + g_parts[n]


def nt(a, b):
    return lax.dot_general(a, b, NT, preferred_element_type=jnp.float32)


def project_kernel(*refs):
    x_refs, (w_in, w_out, out_ref) = refs[:4], refs[4:]
    xs = [nt(x_refs[n][...], w_in[...]) for n in (0, 2)]
    gs = [nt(x_refs[n][...], w_out[...]) for n in (1, 3)]
    store_products(xs, gs, None, out_ref)


def project_pieces_kernel(plan, with_acc, n_pieces, *refs):
    x_refs, (own_in, own_out) = refs[:4], refs[4:6]
    pieces = refs[6 : 6 + n_pieces]
    acc_ref = refs[6 + n_pieces] if with_acc else None
    out_ref, w_in, w_out = refs[6 + n_pieces + with_acc :]
    z = lax.axis_index("dp")
    q = lax.axis_index(PLANE)
    core = lax.axis_index("mp")
    rin, rout = own_in.shape[0], own_out.shape[0]
    quarter = own_in.shape[1] // 4
    xs, gs = [0.0, 0.0], [0.0, 0.0]
    at = 0
    for dq, col, width, rows in plan:
        other = q ^ (core * (3 ^ dq) + (1 - core) * dq) if dq in (1, 2) else q ^ dq
        start = pl.multiple_of(other * quarter + col, 128)
        cols = pl.ds(start, width)
        here = slice(at, at + width)
        at += width
        w_in[pl.ds(pl.multiple_of(z * rin, rin), rin), here] = own_in[:, cols]
        w_out[pl.ds(pl.multiple_of(z * rout, rout), rout), here] = own_out[:, cols]
        for p, row, k in rows:
            dst_in = pl.multiple_of((z ^ k) * rin, rin)
            dst_out = pl.multiple_of((z ^ k) * rout, rout)
            w_in[pl.ds(dst_in, rin), here] = pieces[p][row : row + rin, :]
            w_out[pl.ds(dst_out, rout), here] = pieces[p][row + rin : row + rin + rout, :]
        for m in range(2):
            xs[m] += nt(x_refs[2 * m][:, cols], w_in[:, here])
            gs[m] += nt(x_refs[2 * m + 1][:, cols], w_out[:, here])
    store_products(xs, gs, acc_ref, out_ref)


def moments_kernel(len_tr, len_te, mine, other, fac_ref, gte_ref, gtr_ref):
    tokens = mine.shape[0] // 3
    ki = mine.shape[1]
    ko = ki // 2
    total = mine[...] + other[...]
    rows = lax.broadcasted_iota(jnp.int32, (tokens, ki), 0)
    n_tr, n_te = len_tr[0], len_te[0]
    x_tr = jnp.where(rows < n_tr, total[:tokens], 0.0)
    x_te = jnp.where(rows < n_te, total[tokens : 2 * tokens], 0.0)
    g_both = total[2 * tokens :]
    g_tr = jnp.where(rows < n_tr, g_both, 0.0)[:, :ko]
    g_te = g_both[:, ko:]
    dot = functools.partial(
        lax.dot_general, dimension_numbers=TN, precision=HI,
        preferred_element_type=jnp.float32,
    )
    c_in = dot(x_tr, x_tr)
    c_out = dot(g_tr, g_tr)
    half = ki // 2
    fac_ref[:half, :] = c_in[:half, :]
    fac_ref[half:ki, :half] = c_in[half:, half:]
    fac_ref[half:ki, half:] = c_out
    fac_ref[ki:, :] = jnp.full((8, ki), n_tr.astype(jnp.float32))
    grad_tr = dot(x_tr, g_tr) / n_tr.astype(jnp.float32)
    grad_te = dot(x_te, g_te) / n_te.astype(jnp.float32)
    gtr_ref[...] = grad_tr
    gte_ref[0, :, :ko] = grad_te[:half]
    gte_ref[0, :, ko:] = grad_te[half:]


def wide(x, rows, cols=LANES):
    if x.shape[1] < cols:
        x = jnp.concatenate([x, jnp.zeros((x.shape[0], cols - x.shape[1]), x.dtype)], axis=1)
    if x.shape[0] < rows:
        x = jnp.concatenate([x, jnp.zeros((rows - x.shape[0], cols), x.dtype)], axis=0)
    return x


def parts(x):
    high = x.astype(jnp.bfloat16)
    return high, (x - high.astype(jnp.float32)).astype(jnp.bfloat16)


def right(x):
    high, low = parts(wide(x, LANES))
    upper = jnp.concatenate([high, low], axis=1)
    lower = jnp.concatenate([jnp.zeros_like(high), high], axis=1)
    return jnp.concatenate([upper, lower], axis=0)


def mm3(x, packed):
    both = jnp.dot(
        jnp.concatenate(parts(x), axis=1), packed, preferred_element_type=jnp.float32
    )
    return both[:, :LANES] + both[:, LANES:]


def damped(c):
    n = c.shape[0]
    i = lax.broadcasted_iota(jnp.int32, c.shape, 0)
    j = lax.broadcasted_iota(jnp.int32, c.shape, 1)
    eye = (i == j).astype(jnp.float32)
    trace = jnp.sum(jnp.sum(c * eye, axis=0, keepdims=True), axis=1, keepdims=True)
    low = 0.1 * trace / n
    a = c + low * eye
    high = jnp.max(jnp.sum(jnp.abs(a), axis=0, keepdims=True), axis=1, keepdims=True)
    return a, eye, low, jnp.minimum(high, trace + low)


def inverses(matrices):
    state = []
    for c in matrices:
        a, eye, low, high = damped(c)
        scale = 2.0 / (low + high)
        r = (high - low) / (high + low)
        state.append((a, eye, scale * a, scale * eye, scale, r))
    for step in range(NEWTON_STEPS):
        nxt = []
        for a, eye, m, x, scale, r in state:
            s = 2.0 / (2.0 - r * r)
            n = m.shape[0]
            if step == 0:
                mx = s * (2.0 * m - mm3(m, right(m)))
                xx = s * (2.0 * x - scale * m)
            else:
                both = mm3(jnp.concatenate([m, x], axis=0), right(m))
                mx = s * (2.0 * m - both[:n])
                xx = s * (2.0 * x - both[n:])
            nxt.append((a, eye, mx, xx, scale, r * r / (2.0 - r * r)))
        state = nxt
    result = []
    for a, eye, m, x, scale, r in state:
        n = a.shape[0]
        residual = eye - jnp.dot(
            a[:, :n], x, precision=HI, preferred_element_type=jnp.float32
        )
        result.append(x + mm3(x, right(residual)))
    return result


def side_kernel(fac_ref, gtr_ref, out_ref):
    ki = fac_ref.shape[1]
    half = ki // 2
    top = fac_ref[:half, :]
    low = fac_ref[half:ki, :]
    c_in = jnp.concatenate(
        [top, jnp.concatenate([top[:, half:].T, low[:, :half]], axis=1)], axis=0
    )
    count = fac_ref[ki : ki + 1, :1]
    inv_in, inv_out = inverses([c_in, wide(low[:, half:], half)])
    side = mm3(mm3(inv_in, right(gtr_ref[...])), right(inv_out)) * (count * count)
    out_ref[:, :half] = side[:half, :half]
    out_ref[:, half:] = side[half:, :half]


def scores_kernel(order, n_blk, side_ref, gte_ref, out_ref):
    z = lax.axis_index("dp")
    b = lax.axis_index("blk")
    lane = lax.broadcasted_iota(jnp.int32, out_ref.shape, 1)
    row = jnp.zeros(out_ref.shape, jnp.float32)
    side = side_ref[...]
    sums = [jnp.sum(side * gte_ref[p], axis=0, keepdims=True) for p in range(len(order))]
    values = jnp.sum(jnp.concatenate(sums, axis=0), axis=1, keepdims=True)
    for p, (dz, db) in enumerate(order):
        row = jnp.where(lane == (z ^ dz) * n_blk + (b ^ db), values[p : p + 1, :], row)
    out_ref[...] = row


def project(xs, w_in, w_out, n_groups, n_dp, n_blk):
    tokens, width = xs[0].shape
    rin, rout = w_in.shape[0], w_out.shape[0]
    ki, ko = rin * n_dp, rout * n_dp
    out_shape = jax.ShapeDtypeStruct((3 * tokens, ki), jnp.float32)
    if (n_groups, n_dp, n_blk) != (2, 4, 2):
        w_in = lax.all_gather(w_in, "dp", axis=0, tiled=True)
        w_out = lax.all_gather(w_out, "dp", axis=0, tiled=True)
        return call(project_kernel, out_shape, [vmem()] * 6, (*xs, w_in, w_out))

    part = width // 8
    shard = rin + rout
    q = lax.axis_index(PLANE)
    whole = jnp.concatenate([w_in, w_out], axis=0)
    mine = lax.dynamic_slice(whole, (0, q * 2 * part), (shard, 2 * part))
    opposite = lax.dynamic_slice(whole, (0, (q ^ 3) * 2 * part), (shard, 2 * part))
    operands = (*xs, w_in, w_out)
    *xs, w_in, w_out = call(
        functools.partial(load_kernel, 6),
        tuple(pltpu.VMEM(x.shape, x.dtype) for x in operands),
        [pl.BlockSpec(memory_space=pltpu.HBM)] * 6,
        [pltpu.with_memory_space_constraint(x, pltpu.HBM) for x in operands],
        flops=1 << 30,
        scratch_shapes=[pltpu.SemaphoreType.DMA((12,))],
    )
    halves = [mine[:, :part], mine[:, part:]]
    far = [swap(h, "dp", n_dp, 2) for h in halves]
    near_a, cross_a = [swap(halves[0], "dp", n_dp, k) for k in (1, 3)]
    za = stack((far[0], near_a, cross_a))
    along_x, along_y = (0, 1), (1, 0)
    xa = mixed(za, PLANE, (n_groups, n_blk), along_x, along_y)
    ya = mixed(za, PLANE, (n_groups, n_blk), along_y, along_x)
    both_b = stack((halves[1], far[1]), za)
    near_b = swap(both_b, "dp", n_dp, 1)
    far_op = swap(opposite, "dp", n_dp, 2)
    both_op = stack((opposite, far_op))
    near_op = swap(both_op, "dp", n_dp, 1)
    zb = stack((far[1], near_b))
    xb = mixed(zb, PLANE, (n_groups, n_blk), along_x, along_y)
    yb = mixed(zb, PLANE, (n_groups, n_blk), along_y, along_x)

    def accumulate(plan, pieces, acc):
        args = (*xs, w_in, w_out, *pieces) + (() if acc is None else (acc,))
        total = sum(width for _, _, width, _ in plan)
        return call(
            functools.partial(project_pieces_kernel, plan, acc is not None, len(pieces)),
            out_shape,
            [vmem()] * len(args),
            args,
            flops=1 << 30,
            scratch_shapes=[
                pltpu.VMEM((ki, total), jnp.bfloat16),
                pltpu.VMEM((ko, total), jnp.bfloat16),
            ],
        )

    def stacked(p):
        return tuple((p, i * shard, k) for i, k in enumerate((2, 1, 3)))

    acc = accumulate(
        ((0, 0, part, stacked(0)), (0, part, part, stacked(1))), (za, zb), None)
    acc = accumulate(
        ((1, 0, part, stacked(0)), (2, 0, part, stacked(1))), (xa, ya), acc)
    return accumulate(
        (
            (1, part, part, stacked(0)),
            (2, part, part, stacked(1)),
            (3, 0, 2 * part, ((2, 0, 2), (3, 0, 1), (3, shard, 3))),
        ),
        (xb, yb, far_op, near_op),
        acc,
    )


def per_device(
    n_groups, n_dp, n_blk, train_inputs, train_cotangents, train_lengths,
    test_inputs, test_cotangents, test_lengths, proj_in, proj_out,
):
    _, tokens, width = train_inputs.shape
    xs = [a.reshape(tokens, width) for a in (
        train_inputs, train_cotangents, test_inputs, test_cotangents)]
    part = project(xs, proj_in.T, proj_out.T, n_groups, n_dp, n_blk)
    ki = part.shape[1]
    ko = ki // 2
    other = swap(part, "mp", 2, 1)
    fac, gte, gtr = call(
        moments_kernel,
        (
            jax.ShapeDtypeStruct((ki + 8, ki), jnp.float32),
            jax.ShapeDtypeStruct((1, ki // 2, ki), jnp.float32),
            jax.ShapeDtypeStruct((ki, ko), jnp.float32),
        ),
        [smem(), smem(), vmem(), vmem()],
        (train_lengths, test_lengths, part, other),
    )
    order = [(0, 0)]
    for axis, count in (("dp", n_dp), ("blk", n_blk)):
        for k in bits(count):
            gte = jnp.concatenate([gte, swap(gte, axis, count, k)], axis=0)
            order += [(dz ^ k, db) if axis == "dp" else (dz, db ^ k) for dz, db in order]
    steps_z = [(k, 0) for k in bits(n_dp)]
    steps_x = [(0, k) for k in bits(n_blk)]
    for step0, step1 in zip(steps_x + steps_z, steps_z + steps_x):
        fac = fac + mixed(fac, ("dp", "blk"), (n_dp, n_blk), step0, step1)
    side = call(
        side_kernel,
        jax.ShapeDtypeStruct((ki // 2, ki), jnp.float32),
        [vmem()] * 2,
        (fac, gtr),
        flops=4 << 30,
    )
    return call(
        functools.partial(scores_kernel, order, n_blk),
        jax.ShapeDtypeStruct((1, n_dp * n_blk), jnp.float32),
        [vmem()] * 2,
        (side, gte),
    )


def solution(mesh):
    feature = P(("groups", "dp", "blk"), None, "mp")
    length = P(("groups", "dp", "blk"))
    weight = P("mp", "dp")
    shape = mesh.shape
    return jax.shard_map(
        functools.partial(per_device, shape["groups"], shape["dp"], shape["blk"]),
        mesh=mesh,
        in_specs=(feature, feature, length, feature, feature, length, weight, weight),
        out_specs=P(("groups", "dp", "blk"), None),
        check_vma=False,
    )
```

```python
import functools

import jax
import jax.numpy as jnp
from jax import lax
from jax.experimental import pallas as pl
from jax.experimental.pallas import tpu as pltpu
from jax.sharding import PartitionSpec as P

HI = lax.Precision.HIGHEST
NT = (((1,), (1,)), ((), ()))
TN = (((0,), (0,)), ((), ()))
NEWTON_STEPS = 7
PLANE = ("groups", "blk")
LANES = 128


def vmem():
    return pl.BlockSpec(memory_space=pltpu.VMEM)


def smem():
    return pl.BlockSpec(memory_space=pltpu.SMEM)


def call(kernel, out_shape, in_specs, args, flops=0, limit=16, **kw):
    return pl.pallas_call(
        kernel,
        out_shape=out_shape,
        in_specs=in_specs,
        out_specs=jax.tree.map(lambda _: vmem(), out_shape),
        compiler_params=pltpu.CompilerParams(vmem_limit_bytes=limit * 1024 * 1024),
        cost_estimate=pl.CostEstimate(flops=flops, bytes_accessed=1 << 16, transcendentals=0),
        **kw,
    )(*args)


def swap(x, axis, count, k):
    return lax.ppermute(x, axis, [(i, i ^ k) for i in range(count)])


def mixed(x, axes, counts, step0, step1):
    pairs = []
    for i in range(counts[0]):
        for j in range(counts[1]):
            for core, (di, dj) in enumerate((step0, step1)):
                pairs.append((
                    (i * counts[1] + j) * 2 + core,
                    ((i ^ di) * counts[1] + (j ^ dj)) * 2 + core,
                ))
    return lax.ppermute(x, (*axes, "mp"), pairs)


def bits(count):
    return [1 << s for s in reversed(range(count.bit_length() - 1))]


def load_kernel(n, *refs):
    srcs, dsts, sem = refs[:n], refs[n : 2 * n], refs[2 * n]
    copies = []
    for i, (src, dst) in enumerate(zip(srcs, dsts)):
        rows = src.shape[0] // 2
        for h in range(2):
            part = pl.ds(h * rows, rows)
            copies.append(pltpu.make_async_copy(src.at[part], dst.at[part], sem.at[2 * i + h]))
    for c in copies:
        c.start()
    for c in copies:
        c.wait()


def stack_kernel(n, *refs):
    at = 0
    for src in refs[:n]:
        refs[-1][at : at + src.shape[0], :] = src[...]
        at += src.shape[0]


def stack(parts, after=None):
    rows = sum(p.shape[0] for p in parts)
    extra = () if after is None else (after,)
    return call(
        functools.partial(stack_kernel, len(parts)),
        pltpu.VMEM((rows, parts[0].shape[1]), parts[0].dtype),
        [vmem()] * len(parts) + [pl.BlockSpec(memory_space=pl.ANY)] * len(extra),
        (*parts, *extra),
        limit=1,
    )


def store_products(x_parts, g_parts, acc_ref, out_ref):
    tokens = out_ref.shape[0] // 3
    ko = g_parts[0].shape[1]
    for n in range(2):
        rows = slice(n * tokens, (n + 1) * tokens)
        prior = 0.0 if acc_ref is None else acc_ref[rows, :]
        out_ref[rows, :] = prior + x_parts[n]
    rows = slice(2 * tokens, 3 * tokens)
    for n in range(2):
        cols = slice(n * ko, (n + 1) * ko)
        prior = 0.0 if acc_ref is None else acc_ref[rows, cols]
        out_ref[rows, cols] = prior + g_parts[n]


def nt(a, b):
    return lax.dot_general(a, b, NT, preferred_element_type=jnp.float32)


def project_kernel(*refs):
    x_refs, (w_in, w_out, out_ref) = refs[:4], refs[4:]
    xs = [nt(x_refs[n][...], w_in[...]) for n in (0, 2)]
    gs = [nt(x_refs[n][...], w_out[...]) for n in (1, 3)]
    store_products(xs, gs, None, out_ref)


def project_pieces_kernel(plan, with_acc, n_pieces, *refs):
    x_refs, (own_in, own_out) = refs[:4], refs[4:6]
    pieces = refs[6 : 6 + n_pieces]
    acc_ref = refs[6 + n_pieces] if with_acc else None
    out_ref, w_in, w_out = refs[6 + n_pieces + with_acc :]
    z = lax.axis_index("dp")
    q = lax.axis_index(PLANE)
    core = lax.axis_index("mp")
    rin, rout = own_in.shape[0], own_out.shape[0]
    quarter = own_in.shape[1] // 4
    xs, gs = [0.0, 0.0], [0.0, 0.0]
    at = 0
    for dq, col, width, rows in plan:
        other = q ^ (core * (3 ^ dq) + (1 - core) * dq) if dq in (1, 2) else q ^ dq
        start = pl.multiple_of(other * quarter + col, 128)
        cols = pl.ds(start, width)
        here = slice(at, at + width)
        at += width
        w_in[pl.ds(pl.multiple_of(z * rin, rin), rin), here] = own_in[:, cols]
        w_out[pl.ds(pl.multiple_of(z * rout, rout), rout), here] = own_out[:, cols]
        for p, row, k in rows:
            dst_in = pl.multiple_of((z ^ k) * rin, rin)
            dst_out = pl.multiple_of((z ^ k) * rout, rout)
            w_in[pl.ds(dst_in, rin), here] = pieces[p][row : row + rin, :]
            w_out[pl.ds(dst_out, rout), here] = pieces[p][row + rin : row + rin + rout, :]
        for m in range(2):
            xs[m] += nt(x_refs[2 * m][:, cols], w_in[:, here])
            gs[m] += nt(x_refs[2 * m + 1][:, cols], w_out[:, here])
    store_products(xs, gs, acc_ref, out_ref)


def moments_kernel(len_tr, len_te, mine, other, fac_ref, gte_ref, gtr_ref):
    tokens = mine.shape[0] // 3
    ki = mine.shape[1]
    ko = ki // 2
    total = mine[...] + other[...]
    rows = lax.broadcasted_iota(jnp.int32, (tokens, ki), 0)
    n_tr, n_te = len_tr[0], len_te[0]
    x_tr = jnp.where(rows < n_tr, total[:tokens], 0.0)
    x_te = jnp.where(rows < n_te, total[tokens : 2 * tokens], 0.0)
    g_both = total[2 * tokens :]
    g_tr = jnp.where(rows < n_tr, g_both, 0.0)[:, :ko]
    g_te = g_both[:, ko:]
    dot = functools.partial(
        lax.dot_general, dimension_numbers=TN, precision=HI,
        preferred_element_type=jnp.float32,
    )
    c_in = dot(x_tr, x_tr)
    c_out = dot(g_tr, g_tr)
    half = ki // 2
    fac_ref[:half, :] = c_in[:half, :]
    fac_ref[half:ki, :half] = c_in[half:, half:]
    fac_ref[half:ki, half:] = c_out
    fac_ref[ki:, :] = jnp.full((8, ki), n_tr.astype(jnp.float32))
    grad_tr = dot(x_tr, g_tr) / n_tr.astype(jnp.float32)
    grad_te = dot(x_te, g_te) / n_te.astype(jnp.float32)
    gtr_ref[...] = grad_tr
    gte_ref[0, :, :ko] = grad_te[:half]
    gte_ref[0, :, ko:] = grad_te[half:]


def wide(x, rows, cols=LANES):
    if x.shape[1] < cols:
        x = jnp.concatenate([x, jnp.zeros((x.shape[0], cols - x.shape[1]), x.dtype)], axis=1)
    if x.shape[0] < rows:
        x = jnp.concatenate([x, jnp.zeros((rows - x.shape[0], cols), x.dtype)], axis=0)
    return x


def parts(x):
    high = x.astype(jnp.bfloat16)
    return high, (x - high.astype(jnp.float32)).astype(jnp.bfloat16)


def right(x):
    high, low = parts(wide(x, LANES))
    upper = jnp.concatenate([high, low], axis=1)
    lower = jnp.concatenate([jnp.zeros_like(high), high], axis=1)
    return jnp.concatenate([upper, lower], axis=0)


def mm3(x, packed):
    both = jnp.dot(
        jnp.concatenate(parts(x), axis=1), packed, preferred_element_type=jnp.float32
    )
    return both[:, :LANES] + both[:, LANES:]


def damped(c):
    n = c.shape[0]
    i = lax.broadcasted_iota(jnp.int32, c.shape, 0)
    j = lax.broadcasted_iota(jnp.int32, c.shape, 1)
    eye = (i == j).astype(jnp.float32)
    trace = jnp.sum(jnp.sum(c * eye, axis=0, keepdims=True), axis=1, keepdims=True)
    low = 0.1 * trace / n
    a = c + low * eye
    high = jnp.max(jnp.sum(jnp.abs(a), axis=0, keepdims=True), axis=1, keepdims=True)
    return a, eye, low, jnp.minimum(high, trace + low)


def inverses(matrices):
    state = []
    for c in matrices:
        a, eye, low, high = damped(c)
        scale = 2.0 / (low + high)
        r = (high - low) / (high + low)
        state.append((a, eye, scale * a, scale * eye, scale, r))
    for step in range(NEWTON_STEPS):
        nxt = []
        for a, eye, m, x, scale, r in state:
            s = 2.0 / (2.0 - r * r)
            n = m.shape[0]
            if step == 0:
                mx = s * (2.0 * m - mm3(m, right(m)))
                xx = s * (2.0 * x - scale * m)
            else:
                both = mm3(jnp.concatenate([m, x], axis=0), right(m))
                mx = s * (2.0 * m - both[:n])
                xx = s * (2.0 * x - both[n:])
            nxt.append((a, eye, mx, xx, scale, r * r / (2.0 - r * r)))
        state = nxt
    result = []
    for a, eye, m, x, scale, r in state:
        n = a.shape[0]
        residual = eye - jnp.dot(
            a[:, :n], x, precision=HI, preferred_element_type=jnp.float32
        )
        result.append(x + mm3(x, right(residual)))
    return result


def side_kernel(fac_ref, gtr_ref, out_ref):
    ki = fac_ref.shape[1]
    half = ki // 2
    top = fac_ref[:half, :]
    low = fac_ref[half:ki, :]
    c_in = jnp.concatenate(
        [top, jnp.concatenate([top[:, half:].T, low[:, :half]], axis=1)], axis=0
    )
    count = fac_ref[ki : ki + 1, :1]
    inv_in, inv_out = inverses([c_in, wide(low[:, half:], half)])
    side = mm3(mm3(inv_in, right(gtr_ref[...])), right(inv_out)) * (count * count)
    out_ref[:, :half] = side[:half, :half]
    out_ref[:, half:] = side[half:, :half]


def scores_kernel(order, n_blk, side_ref, gte_ref, out_ref):
    z = lax.axis_index("dp")
    b = lax.axis_index("blk")
    lane = lax.broadcasted_iota(jnp.int32, out_ref.shape, 1)
    row = jnp.zeros(out_ref.shape, jnp.float32)
    side = side_ref[...]
    sums = [jnp.sum(side * gte_ref[p], axis=0, keepdims=True) for p in range(len(order))]
    values = jnp.sum(jnp.concatenate(sums, axis=0), axis=1, keepdims=True)
    for p, (dz, db) in enumerate(order):
        row = jnp.where(lane == (z ^ dz) * n_blk + (b ^ db), values[p : p + 1, :], row)
    out_ref[...] = row


def project(xs, w_in, w_out, n_groups, n_dp, n_blk):
    tokens, width = xs[0].shape
    rin, rout = w_in.shape[0], w_out.shape[0]
    ki, ko = rin * n_dp, rout * n_dp
    out_shape = jax.ShapeDtypeStruct((3 * tokens, ki), jnp.float32)
    if (n_groups, n_dp, n_blk) != (2, 4, 2):
        w_in = lax.all_gather(w_in, "dp", axis=0, tiled=True)
        w_out = lax.all_gather(w_out, "dp", axis=0, tiled=True)
        return call(project_kernel, out_shape, [vmem()] * 6, (*xs, w_in, w_out))

    quarter = width // 4
    part = quarter * 3 // 8
    shard = rin + rout
    q = lax.axis_index(PLANE)
    whole = jnp.concatenate([w_in, w_out], axis=0)
    mine = lax.dynamic_slice(whole, (0, q * quarter), (shard, quarter))
    opposite = lax.dynamic_slice(whole, (0, (q ^ 3) * quarter), (shard, quarter))
    operands = (*xs, w_in, w_out)
    *xs, w_in, w_out = call(
        functools.partial(load_kernel, 6),
        tuple(pltpu.VMEM(x.shape, x.dtype) for x in operands),
        [pl.BlockSpec(memory_space=pltpu.HBM)] * 6,
        [pltpu.with_memory_space_constraint(x, pltpu.HBM) for x in operands],
        flops=1 << 30,
        scratch_shapes=[pltpu.SemaphoreType.DMA((12,))],
    )
    halves = [mine[:, :part], mine[:, part:]]
    far = [swap(h, "dp", n_dp, 2) for h in halves]
    far_op = swap(opposite, "dp", n_dp, 2)
    both_a = stack((halves[0], far[0]), w_out)
    near_a = swap(both_a, "dp", n_dp, 1)
    both_b = stack((halves[1], far[1]))
    near_b = swap(both_b, "dp", n_dp, 1)
    za = stack((far[0], near_a))
    along_x, along_y = (0, 1), (1, 0)
    xa = mixed(za, PLANE, (n_groups, n_blk), along_x, along_y)
    ya = mixed(za, PLANE, (n_groups, n_blk), along_y, along_x)
    both_op = stack((opposite, far_op))
    near_op = swap(both_op, "dp", n_dp, 1)
    zb = stack((far[1], near_b))
    xb = mixed(zb, PLANE, (n_groups, n_blk), along_x, along_y)
    yb = mixed(zb, PLANE, (n_groups, n_blk), along_y, along_x)

    def accumulate(plan, pieces, acc):
        args = (*xs, w_in, w_out, *pieces) + (() if acc is None else (acc,))
        total = sum(width for _, _, width, _ in plan)
        return call(
            functools.partial(project_pieces_kernel, plan, acc is not None, len(pieces)),
            out_shape,
            [vmem()] * len(args),
            args,
            flops=1 << 28,
            scratch_shapes=[
                pltpu.VMEM((ki, total), jnp.bfloat16),
                pltpu.VMEM((ko, total), jnp.bfloat16),
            ],
        )

    def stacked(p):
        return tuple((p, i * shard, k) for i, k in enumerate((2, 1, 3)))

    rest = quarter - part
    acc = accumulate(
        ((0, 0, part, stacked(0)), (0, part, rest, stacked(1))), (za, zb), None)
    acc = accumulate(
        ((1, 0, part, stacked(0)), (2, 0, part, stacked(1))), (xa, ya), acc)
    return accumulate(
        (
            (1, part, rest, stacked(0)),
            (2, part, rest, stacked(1)),
            (3, 0, quarter, ((2, 0, 2), (3, 0, 1), (3, shard, 3))),
        ),
        (xb, yb, far_op, near_op),
        acc,
    )


def per_device(
    n_groups, n_dp, n_blk, train_inputs, train_cotangents, train_lengths,
    test_inputs, test_cotangents, test_lengths, proj_in, proj_out,
):
    _, tokens, width = train_inputs.shape
    xs = [a.reshape(tokens, width) for a in (
        train_inputs, train_cotangents, test_inputs, test_cotangents)]
    part = project(xs, proj_in.T, proj_out.T, n_groups, n_dp, n_blk)
    ki = part.shape[1]
    ko = ki // 2
    other = swap(part, "mp", 2, 1)
    fac, gte, gtr = call(
        moments_kernel,
        (
            jax.ShapeDtypeStruct((ki + 8, ki), jnp.float32),
            jax.ShapeDtypeStruct((1, ki // 2, ki), jnp.float32),
            jax.ShapeDtypeStruct((ki, ko), jnp.float32),
        ),
        [smem(), smem(), vmem(), vmem()],
        (train_lengths, test_lengths, part, other),
    )
    order = [(0, 0)]
    for axis, count in (("dp", n_dp), ("blk", n_blk)):
        for k in bits(count):
            gte = jnp.concatenate([gte, swap(gte, axis, count, k)], axis=0)
            order += [(dz ^ k, db) if axis == "dp" else (dz, db ^ k) for dz, db in order]
    steps_z = [(k, 0) for k in bits(n_dp)]
    steps_x = [(0, k) for k in bits(n_blk)]
    for step0, step1 in zip(steps_x + steps_z, steps_z + steps_x):
        fac = fac + mixed(fac, ("dp", "blk"), (n_dp, n_blk), step0, step1)
    side = call(
        side_kernel,
        jax.ShapeDtypeStruct((ki // 2, ki), jnp.float32),
        [vmem()] * 2,
        (fac, gtr),
        flops=4 << 30,
    )
    return call(
        functools.partial(scores_kernel, order, n_blk),
        jax.ShapeDtypeStruct((1, n_dp * n_blk), jnp.float32),
        [vmem()] * 2,
        (side, gte),
    )


def solution(mesh):
    feature = P(("groups", "dp", "blk"), None, "mp")
    length = P(("groups", "dp", "blk"))
    weight = P("mp", "dp")
    shape = mesh.shape
    return jax.shard_map(
        functools.partial(per_device, shape["groups"], shape["dp"], shape["blk"]),
        mesh=mesh,
        in_specs=(feature, feature, length, feature, feature, length, weight, weight),
        out_specs=P(("groups", "dp", "blk"), None),
        check_vma=False,
    )
```

```python
import functools

import jax
import jax.numpy as jnp
from jax import lax
from jax.experimental import pallas as pl
from jax.experimental.pallas import tpu as pltpu
from jax.sharding import PartitionSpec as P

HI = lax.Precision.HIGHEST
NT = (((1,), (1,)), ((), ()))
TN = (((0,), (0,)), ((), ()))
NEWTON_STEPS = 7
PLANE = ("groups", "blk")
LANES = 128


def vmem():
    return pl.BlockSpec(memory_space=pltpu.VMEM)


def smem():
    return pl.BlockSpec(memory_space=pltpu.SMEM)


def call(kernel, out_shape, in_specs, args, flops=0, limit=16, **kw):
    return pl.pallas_call(
        kernel,
        out_shape=out_shape,
        in_specs=in_specs,
        out_specs=jax.tree.map(lambda _: vmem(), out_shape),
        compiler_params=pltpu.CompilerParams(vmem_limit_bytes=limit * 1024 * 1024),
        cost_estimate=pl.CostEstimate(flops=flops, bytes_accessed=1 << 16, transcendentals=0),
        **kw,
    )(*args)


def swap(x, axis, count, k):
    return lax.ppermute(x, axis, [(i, i ^ k) for i in range(count)])


def mixed(x, axes, counts, step0, step1):
    pairs = []
    for i in range(counts[0]):
        for j in range(counts[1]):
            for core, (di, dj) in enumerate((step0, step1)):
                pairs.append((
                    (i * counts[1] + j) * 2 + core,
                    ((i ^ di) * counts[1] + (j ^ dj)) * 2 + core,
                ))
    return lax.ppermute(x, (*axes, "mp"), pairs)


def bits(count):
    return [1 << s for s in reversed(range(count.bit_length() - 1))]


def load_kernel(n, *refs):
    srcs, dsts, sem = refs[:n], refs[n : 2 * n], refs[2 * n]
    copies = []
    for i, (src, dst) in enumerate(zip(srcs, dsts)):
        rows = src.shape[0] // 2
        for h in range(2):
            part = pl.ds(h * rows, rows)
            copies.append(pltpu.make_async_copy(src.at[part], dst.at[part], sem.at[2 * i + h]))
    for c in copies:
        c.start()
    for c in copies:
        c.wait()


def stack_kernel(n, *refs):
    at = 0
    for src in refs[:n]:
        refs[-1][at : at + src.shape[0], :] = src[...]
        at += src.shape[0]


def stack(parts, after=None):
    rows = sum(p.shape[0] for p in parts)
    extra = () if after is None else (after,)
    return call(
        functools.partial(stack_kernel, len(parts)),
        pltpu.VMEM((rows, parts[0].shape[1]), parts[0].dtype),
        [vmem()] * len(parts) + [pl.BlockSpec(memory_space=pl.ANY)] * len(extra),
        (*parts, *extra),
        limit=1,
    )


def store_products(x_parts, g_parts, acc_ref, out_ref):
    tokens = out_ref.shape[0] // 3
    ko = g_parts[0].shape[1]
    for n in range(2):
        rows = slice(n * tokens, (n + 1) * tokens)
        prior = 0.0 if acc_ref is None else acc_ref[rows, :]
        out_ref[rows, :] = prior + x_parts[n]
    rows = slice(2 * tokens, 3 * tokens)
    for n in range(2):
        cols = slice(n * ko, (n + 1) * ko)
        prior = 0.0 if acc_ref is None else acc_ref[rows, cols]
        out_ref[rows, cols] = prior + g_parts[n]


def nt(a, b):
    return lax.dot_general(a, b, NT, preferred_element_type=jnp.float32)


def project_kernel(*refs):
    x_refs, (w_in, w_out, out_ref) = refs[:4], refs[4:]
    xs = [nt(x_refs[n][...], w_in[...]) for n in (0, 2)]
    gs = [nt(x_refs[n][...], w_out[...]) for n in (1, 3)]
    store_products(xs, gs, None, out_ref)


def project_pieces_kernel(plan, with_acc, n_pieces, *refs):
    x_refs, (own_in, own_out) = refs[:4], refs[4:6]
    pieces = refs[6 : 6 + n_pieces]
    acc_ref = refs[6 + n_pieces] if with_acc else None
    out_ref, w_in, w_out = refs[6 + n_pieces + with_acc :]
    z = lax.axis_index("dp")
    q = lax.axis_index(PLANE)
    core = lax.axis_index("mp")
    rin, rout = own_in.shape[0], own_out.shape[0]
    quarter = own_in.shape[1] // 4
    xs, gs = [0.0, 0.0], [0.0, 0.0]
    at = 0
    for dq, col, width, rows in plan:
        other = q ^ (core * (3 ^ dq) + (1 - core) * dq) if dq in (1, 2) else q ^ dq
        start = pl.multiple_of(other * quarter + col, 128)
        cols = pl.ds(start, width)
        here = slice(at, at + width)
        at += width
        w_in[pl.ds(pl.multiple_of(z * rin, rin), rin), here] = own_in[:, cols]
        w_out[pl.ds(pl.multiple_of(z * rout, rout), rout), here] = own_out[:, cols]
        for p, row, k in rows:
            dst_in = pl.multiple_of((z ^ k) * rin, rin)
            dst_out = pl.multiple_of((z ^ k) * rout, rout)
            w_in[pl.ds(dst_in, rin), here] = pieces[p][row : row + rin, :]
            w_out[pl.ds(dst_out, rout), here] = pieces[p][row + rin : row + rin + rout, :]
        for m in range(2):
            xs[m] += nt(x_refs[2 * m][:, cols], w_in[:, here])
            gs[m] += nt(x_refs[2 * m + 1][:, cols], w_out[:, here])
    store_products(xs, gs, acc_ref, out_ref)


def moments_kernel(len_tr, len_te, mine, other, fac_ref, gte_ref, gtr_ref):
    tokens = mine.shape[0] // 3
    ki = mine.shape[1]
    ko = ki // 2
    total = mine[...] + other[...]
    rows = lax.broadcasted_iota(jnp.int32, (tokens, ki), 0)
    n_tr, n_te = len_tr[0], len_te[0]
    x_tr = jnp.where(rows < n_tr, total[:tokens], 0.0)
    x_te = jnp.where(rows < n_te, total[tokens : 2 * tokens], 0.0)
    g_both = total[2 * tokens :]
    g_tr = jnp.where(rows < n_tr, g_both, 0.0)[:, :ko]
    g_te = g_both[:, ko:]
    dot = functools.partial(
        lax.dot_general, dimension_numbers=TN, precision=HI,
        preferred_element_type=jnp.float32,
    )
    products = jnp.dot(
        x_tr.T, jnp.concatenate([x_tr, g_tr], axis=1), precision=HI,
        preferred_element_type=jnp.float32,
    )
    c_in = products[:, :ki]
    c_out = dot(g_tr, g_tr)
    half = ki // 2
    fac_ref[:half, :] = c_in[:half, :]
    fac_ref[half:ki, :half] = c_in[half:, half:]
    fac_ref[half:ki, half:] = c_out
    fac_ref[ki:, :] = jnp.full((8, ki), n_tr.astype(jnp.float32))
    grad_tr = products[:, ki:] / n_tr.astype(jnp.float32)
    grad_te = dot(x_te, g_te) / n_te.astype(jnp.float32)
    gtr_ref[...] = grad_tr
    gte_ref[0, :, :ko] = grad_te[:half]
    gte_ref[0, :, ko:] = grad_te[half:]


def wide(x, rows, cols=LANES):
    if x.shape[1] < cols:
        x = jnp.concatenate([x, jnp.zeros((x.shape[0], cols - x.shape[1]), x.dtype)], axis=1)
    if x.shape[0] < rows:
        x = jnp.concatenate([x, jnp.zeros((rows - x.shape[0], cols), x.dtype)], axis=0)
    return x


def parts(x):
    high = x.astype(jnp.bfloat16)
    return high, (x - high.astype(jnp.float32)).astype(jnp.bfloat16)


def right(x):
    high, low = parts(wide(x, LANES))
    upper = jnp.concatenate([high, low], axis=1)
    lower = jnp.concatenate([jnp.zeros_like(high), high], axis=1)
    return jnp.concatenate([upper, lower], axis=0)


def mm3(x, packed):
    both = jnp.dot(
        jnp.concatenate(parts(x), axis=1), packed, preferred_element_type=jnp.float32
    )
    return both[:, :LANES] + both[:, LANES:]


def damped(c):
    n = c.shape[0]
    i = lax.broadcasted_iota(jnp.int32, c.shape, 0)
    j = lax.broadcasted_iota(jnp.int32, c.shape, 1)
    eye = (i == j).astype(jnp.float32)
    trace = jnp.sum(jnp.sum(c * eye, axis=0, keepdims=True), axis=1, keepdims=True)
    low = 0.1 * trace / n
    a = c + low * eye
    high = jnp.max(jnp.sum(jnp.abs(a), axis=0, keepdims=True), axis=1, keepdims=True)
    return a, eye, low, jnp.minimum(high, trace + low)


def inverses(matrices):
    state = []
    for c in matrices:
        a, eye, low, high = damped(c)
        scale = 2.0 / (low + high)
        r = (high - low) / (high + low)
        state.append((a, eye, scale * a, scale * eye, scale, r))
    for step in range(NEWTON_STEPS):
        nxt = []
        for a, eye, m, x, scale, r in state:
            s = 2.0 / (2.0 - r * r)
            n = m.shape[0]
            if step == 0:
                mx = s * (2.0 * m - mm3(m, right(m)))
                xx = s * (2.0 * x - scale * m)
            else:
                both = mm3(jnp.concatenate([m, x], axis=0), right(m))
                mx = s * (2.0 * m - both[:n])
                xx = s * (2.0 * x - both[n:])
            nxt.append((a, eye, mx, xx, scale, r * r / (2.0 - r * r)))
        state = nxt
    result = []
    for a, eye, m, x, scale, r in state:
        n = a.shape[0]
        residual = eye - jnp.dot(
            a[:, :n], x, precision=HI, preferred_element_type=jnp.float32
        )
        result.append(x + mm3(x, right(residual)))
    return result


def side_kernel(fac_ref, gtr_ref, out_ref):
    ki = fac_ref.shape[1]
    half = ki // 2
    top = fac_ref[:half, :]
    low = fac_ref[half:ki, :]
    c_in = jnp.concatenate(
        [top, jnp.concatenate([top[:, half:].T, low[:, :half]], axis=1)], axis=0
    )
    count = fac_ref[ki : ki + 1, :1]
    inv_in, inv_out = inverses([c_in, wide(low[:, half:], half)])
    side = mm3(mm3(inv_in, right(gtr_ref[...])), right(inv_out)) * (count * count)
    out_ref[:, :half] = side[:half, :half]
    out_ref[:, half:] = side[half:, :half]


def scores_kernel(order, n_blk, side_ref, gte_ref, out_ref):
    z = lax.axis_index("dp")
    b = lax.axis_index("blk")
    lane = lax.broadcasted_iota(jnp.int32, out_ref.shape, 1)
    row = jnp.zeros(out_ref.shape, jnp.float32)
    side = side_ref[...]
    sums = [jnp.sum(side * gte_ref[p], axis=0, keepdims=True) for p in range(len(order))]
    values = jnp.sum(jnp.concatenate(sums, axis=0), axis=1, keepdims=True)
    for p, (dz, db) in enumerate(order):
        row = jnp.where(lane == (z ^ dz) * n_blk + (b ^ db), values[p : p + 1, :], row)
    out_ref[...] = row


def project(xs, w_in, w_out, n_groups, n_dp, n_blk):
    tokens, width = xs[0].shape
    rin, rout = w_in.shape[0], w_out.shape[0]
    ki, ko = rin * n_dp, rout * n_dp
    out_shape = jax.ShapeDtypeStruct((3 * tokens, ki), jnp.float32)
    if (n_groups, n_dp, n_blk) != (2, 4, 2):
        w_in = lax.all_gather(w_in, "dp", axis=0, tiled=True)
        w_out = lax.all_gather(w_out, "dp", axis=0, tiled=True)
        return call(project_kernel, out_shape, [vmem()] * 6, (*xs, w_in, w_out))

    part = width // 8
    shard = rin + rout
    q = lax.axis_index(PLANE)
    whole = jnp.concatenate([w_in, w_out], axis=0)
    mine = lax.dynamic_slice(whole, (0, q * 2 * part), (shard, 2 * part))
    opposite = lax.dynamic_slice(whole, (0, (q ^ 3) * 2 * part), (shard, 2 * part))
    operands = (*xs, w_in, w_out)
    *xs, w_in, w_out = call(
        functools.partial(load_kernel, 6),
        tuple(pltpu.VMEM(x.shape, x.dtype) for x in operands),
        [pl.BlockSpec(memory_space=pltpu.HBM)] * 6,
        [pltpu.with_memory_space_constraint(x, pltpu.HBM) for x in operands],
        flops=1 << 30,
        scratch_shapes=[pltpu.SemaphoreType.DMA((12,))],
    )
    halves = [mine[:, :part], mine[:, part:]]
    far = [swap(h, "dp", n_dp, 2) for h in halves]
    far_op = swap(opposite, "dp", n_dp, 2)
    both_a = stack((halves[0], far[0]), w_out)
    near_a = swap(both_a, "dp", n_dp, 1)
    both_b = stack((halves[1], far[1]))
    near_b = swap(both_b, "dp", n_dp, 1)
    za = stack((far[0], near_a))
    along_x, along_y = (0, 1), (1, 0)
    xa = mixed(za, PLANE, (n_groups, n_blk), along_x, along_y)
    ya = mixed(za, PLANE, (n_groups, n_blk), along_y, along_x)
    both_op = stack((opposite, far_op))
    near_op = swap(both_op, "dp", n_dp, 1)
    zb = stack((far[1], near_b))
    xb = mixed(zb, PLANE, (n_groups, n_blk), along_x, along_y)
    yb = mixed(zb, PLANE, (n_groups, n_blk), along_y, along_x)

    def accumulate(plan, pieces, acc):
        args = (*xs, w_in, w_out, *pieces) + (() if acc is None else (acc,))
        total = sum(width for _, _, width, _ in plan)
        return call(
            functools.partial(project_pieces_kernel, plan, acc is not None, len(pieces)),
            out_shape,
            [vmem()] * len(args),
            args,
            flops=1 << 28,
            scratch_shapes=[
                pltpu.VMEM((ki, total), jnp.bfloat16),
                pltpu.VMEM((ko, total), jnp.bfloat16),
            ],
        )

    def stacked(p):
        return tuple((p, i * shard, k) for i, k in enumerate((2, 1, 3)))

    acc = accumulate(
        ((0, 0, part, stacked(0)), (0, part, part, stacked(1))), (za, zb), None)
    acc = accumulate(
        ((1, 0, part, stacked(0)), (2, 0, part, stacked(1))), (xa, ya), acc)
    return accumulate(
        (
            (1, part, part, stacked(0)),
            (2, part, part, stacked(1)),
            (3, 0, 2 * part, ((2, 0, 2), (3, 0, 1), (3, shard, 3))),
        ),
        (xb, yb, far_op, near_op),
        acc,
    )


def per_device(
    n_groups, n_dp, n_blk, train_inputs, train_cotangents, train_lengths,
    test_inputs, test_cotangents, test_lengths, proj_in, proj_out,
):
    _, tokens, width = train_inputs.shape
    xs = [a.reshape(tokens, width) for a in (
        train_inputs, train_cotangents, test_inputs, test_cotangents)]
    part = project(xs, proj_in.T, proj_out.T, n_groups, n_dp, n_blk)
    ki = part.shape[1]
    ko = ki // 2
    other = swap(part, "mp", 2, 1)
    fac, gte, gtr = call(
        moments_kernel,
        (
            jax.ShapeDtypeStruct((ki + 8, ki), jnp.float32),
            jax.ShapeDtypeStruct((1, ki // 2, ki), jnp.float32),
            jax.ShapeDtypeStruct((ki, ko), jnp.float32),
        ),
        [smem(), smem(), vmem(), vmem()],
        (train_lengths, test_lengths, part, other),
    )
    order = [(0, 0)]
    for axis, count in (("dp", n_dp), ("blk", n_blk)):
        for k in bits(count):
            gte = jnp.concatenate([gte, swap(gte, axis, count, k)], axis=0)
            order += [(dz ^ k, db) if axis == "dp" else (dz, db ^ k) for dz, db in order]
    steps_z = [(k, 0) for k in bits(n_dp)]
    steps_x = [(0, k) for k in bits(n_blk)]
    first = steps_x + steps_z[::-1]
    second = steps_z[:1] + steps_x + steps_z[1:]
    for step0, step1 in zip(first, second):
        fac = fac + mixed(fac, ("dp", "blk"), (n_dp, n_blk), step0, step1)
    side = call(
        side_kernel,
        jax.ShapeDtypeStruct((ki // 2, ki), jnp.float32),
        [vmem()] * 2,
        (fac, gtr),
        flops=4 << 30,
    )
    return call(
        functools.partial(scores_kernel, order, n_blk),
        jax.ShapeDtypeStruct((1, n_dp * n_blk), jnp.float32),
        [vmem()] * 2,
        (side, gte),
    )


def solution(mesh):
    feature = P(("groups", "dp", "blk"), None, "mp")
    length = P(("groups", "dp", "blk"))
    weight = P("mp", "dp")
    shape = mesh.shape
    return jax.shard_map(
        functools.partial(per_device, shape["groups"], shape["dp"], shape["blk"]),
        mesh=mesh,
        in_specs=(feature, feature, length, feature, feature, length, weight, weight),
        out_specs=P(("groups", "dp", "blk"), None),
        check_vma=False,
    )
```

```python
import functools

import jax
import jax.numpy as jnp
from jax import lax
from jax.experimental import pallas as pl
from jax.experimental.pallas import tpu as pltpu
from jax.sharding import PartitionSpec as P

HI = lax.Precision.HIGHEST
NT = (((1,), (1,)), ((), ()))
TN = (((0,), (0,)), ((), ()))
NEWTON_STEPS = 7
PLANE = ("groups", "blk")
LANES = 128


def vmem():
    return pl.BlockSpec(memory_space=pltpu.VMEM)


def smem():
    return pl.BlockSpec(memory_space=pltpu.SMEM)


def call(kernel, out_shape, in_specs, args, flops=0, limit=16, **kw):
    return pl.pallas_call(
        kernel,
        out_shape=out_shape,
        in_specs=in_specs,
        out_specs=jax.tree.map(lambda _: vmem(), out_shape),
        compiler_params=pltpu.CompilerParams(vmem_limit_bytes=limit * 1024 * 1024),
        cost_estimate=pl.CostEstimate(flops=flops, bytes_accessed=1 << 16, transcendentals=0),
        **kw,
    )(*args)


def swap(x, axis, count, k):
    return lax.ppermute(x, axis, [(i, i ^ k) for i in range(count)])


def mixed(x, axes, counts, step0, step1):
    pairs = []
    for i in range(counts[0]):
        for j in range(counts[1]):
            for core, (di, dj) in enumerate((step0, step1)):
                pairs.append((
                    (i * counts[1] + j) * 2 + core,
                    ((i ^ di) * counts[1] + (j ^ dj)) * 2 + core,
                ))
    return lax.ppermute(x, (*axes, "mp"), pairs)


def bits(count):
    return [1 << s for s in reversed(range(count.bit_length() - 1))]


def load_kernel(n, *refs):
    srcs, dsts, sem = refs[:n], refs[n : 2 * n], refs[2 * n]
    copies = []
    for i, (src, dst) in enumerate(zip(srcs, dsts)):
        rows = src.shape[0] // 2
        for h in range(2):
            part = pl.ds(h * rows, rows)
            copies.append(pltpu.make_async_copy(src.at[part], dst.at[part], sem.at[2 * i + h]))
    for c in copies:
        c.start()
    for c in copies:
        c.wait()


def stack_kernel(n, *refs):
    at = 0
    for src in refs[:n]:
        refs[-1][at : at + src.shape[0], :] = src[...]
        at += src.shape[0]


def stack(parts, after=None):
    rows = sum(p.shape[0] for p in parts)
    extra = () if after is None else (after,)
    return call(
        functools.partial(stack_kernel, len(parts)),
        pltpu.VMEM((rows, parts[0].shape[1]), parts[0].dtype),
        [vmem()] * len(parts) + [pl.BlockSpec(memory_space=pl.ANY)] * len(extra),
        (*parts, *extra),
        limit=1,
    )


def store_products(x_parts, g_parts, acc_ref, out_ref):
    tokens = out_ref.shape[0] // 3
    ko = g_parts[0].shape[1]
    for n in range(2):
        rows = slice(n * tokens, (n + 1) * tokens)
        prior = 0.0 if acc_ref is None else acc_ref[rows, :]
        out_ref[rows, :] = prior + x_parts[n]
    rows = slice(2 * tokens, 3 * tokens)
    for n in range(2):
        cols = slice(n * ko, (n + 1) * ko)
        prior = 0.0 if acc_ref is None else acc_ref[rows, cols]
        out_ref[rows, cols] = prior + g_parts[n]


def nt(a, b):
    return lax.dot_general(a, b, NT, preferred_element_type=jnp.float32)


def project_kernel(*refs):
    x_refs, (w_in, w_out, out_ref) = refs[:4], refs[4:]
    xs = [nt(x_refs[n][...], w_in[...]) for n in (0, 2)]
    gs = [nt(x_refs[n][...], w_out[...]) for n in (1, 3)]
    store_products(xs, gs, None, out_ref)


def project_pieces_kernel(plan, with_acc, n_pieces, *refs):
    x_refs, (own_in, own_out) = refs[:4], refs[4:6]
    pieces = refs[6 : 6 + n_pieces]
    acc_ref = refs[6 + n_pieces] if with_acc else None
    out_ref, w_in, w_out = refs[6 + n_pieces + with_acc :]
    z = lax.axis_index("dp")
    q = lax.axis_index(PLANE)
    core = lax.axis_index("mp")
    rin, rout = own_in.shape[0], own_out.shape[0]
    quarter = own_in.shape[1] // 4
    xs, gs = [0.0, 0.0], [0.0, 0.0]
    at = 0
    for dq, col, width, rows in plan:
        other = q ^ (core * (3 ^ dq) + (1 - core) * dq) if dq in (1, 2) else q ^ dq
        start = pl.multiple_of(other * quarter + col, 128)
        cols = pl.ds(start, width)
        here = slice(at, at + width)
        at += width
        w_in[pl.ds(pl.multiple_of(z * rin, rin), rin), here] = own_in[:, cols]
        w_out[pl.ds(pl.multiple_of(z * rout, rout), rout), here] = own_out[:, cols]
        for p, row, k in rows:
            dst_in = pl.multiple_of((z ^ k) * rin, rin)
            dst_out = pl.multiple_of((z ^ k) * rout, rout)
            w_in[pl.ds(dst_in, rin), here] = pieces[p][row : row + rin, :]
            w_out[pl.ds(dst_out, rout), here] = pieces[p][row + rin : row + rin + rout, :]
        for m in range(2):
            xs[m] += nt(x_refs[2 * m][:, cols], w_in[:, here])
            gs[m] += nt(x_refs[2 * m + 1][:, cols], w_out[:, here])
    store_products(xs, gs, acc_ref, out_ref)


def moments_kernel(len_tr, len_te, mine, other, fac_ref, gte_ref, gtr_ref):
    tokens = mine.shape[0] // 3
    ki = mine.shape[1]
    ko = ki // 2
    total = mine[...] + other[...]
    rows = lax.broadcasted_iota(jnp.int32, (tokens, ki), 0)
    n_tr, n_te = len_tr[0], len_te[0]
    x_tr = jnp.where(rows < n_tr, total[:tokens], 0.0)
    x_te = jnp.where(rows < n_te, total[tokens : 2 * tokens], 0.0)
    g_both = total[2 * tokens :]
    g_tr = jnp.where(rows < n_tr, g_both, 0.0)[:, :ko]
    g_te = g_both[:, ko:]
    dot = functools.partial(
        lax.dot_general, dimension_numbers=TN, precision=HI,
        preferred_element_type=jnp.float32,
    )
    products = jnp.dot(
        x_tr.T, jnp.concatenate([x_tr, g_tr], axis=1), precision=HI,
        preferred_element_type=jnp.float32,
    )
    c_in = products[:, :ki]
    c_out = dot(g_tr, g_tr)
    half = ki // 2
    fac_ref[:half, :] = c_in[:half, :]
    fac_ref[half:ki, :half] = c_in[half:, half:]
    fac_ref[half:ki, half:] = c_out
    fac_ref[ki:, :] = jnp.full((8, ki), n_tr.astype(jnp.float32))
    grad_tr = products[:, ki:] / n_tr.astype(jnp.float32)
    grad_te = dot(x_te, g_te) / n_te.astype(jnp.float32)
    gtr_ref[...] = grad_tr
    gte_ref[0, :, :ko] = grad_te[:half]
    gte_ref[0, :, ko:] = grad_te[half:]


def wide(x, rows, cols=LANES):
    if x.shape[1] < cols:
        x = jnp.concatenate([x, jnp.zeros((x.shape[0], cols - x.shape[1]), x.dtype)], axis=1)
    if x.shape[0] < rows:
        x = jnp.concatenate([x, jnp.zeros((rows - x.shape[0], cols), x.dtype)], axis=0)
    return x


def parts(x):
    high = x.astype(jnp.bfloat16)
    return high, (x - high.astype(jnp.float32)).astype(jnp.bfloat16)


def right(x):
    high, low = parts(wide(x, LANES))
    upper = jnp.concatenate([high, low], axis=1)
    lower = jnp.concatenate([jnp.zeros_like(high), high], axis=1)
    return jnp.concatenate([upper, lower], axis=0)


def mm3(x, packed):
    both = jnp.dot(
        jnp.concatenate(parts(x), axis=1), packed, preferred_element_type=jnp.float32
    )
    return both[:, :LANES] + both[:, LANES:]


def damped(c):
    n = c.shape[0]
    i = lax.broadcasted_iota(jnp.int32, c.shape, 0)
    j = lax.broadcasted_iota(jnp.int32, c.shape, 1)
    eye = (i == j).astype(jnp.float32)
    trace = jnp.sum(jnp.sum(c * eye, axis=0, keepdims=True), axis=1, keepdims=True)
    low = 0.1 * trace / n
    a = c + low * eye
    high = jnp.max(jnp.sum(jnp.abs(a), axis=0, keepdims=True), axis=1, keepdims=True)
    return a, eye, low, jnp.minimum(high, trace + low)


def inverses(matrices):
    state = []
    for c in matrices:
        a, eye, low, high = damped(c)
        scale = 2.0 / (low + high)
        r = (high - low) / (high + low)
        state.append((a, eye, scale * a, scale * eye, scale, r))
    for step in range(NEWTON_STEPS):
        nxt = []
        for a, eye, m, x, scale, r in state:
            s = 2.0 / (2.0 - r * r)
            n = m.shape[0]
            if step == 0:
                mx = s * (2.0 * m - mm3(m, right(m)))
                xx = s * (2.0 * x - scale * m)
            else:
                both = mm3(jnp.concatenate([m, x], axis=0), right(m))
                mx = s * (2.0 * m - both[:n])
                xx = s * (2.0 * x - both[n:])
            nxt.append((a, eye, mx, xx, scale, r * r / (2.0 - r * r)))
        state = nxt
    result = []
    for a, eye, m, x, scale, r in state:
        n = a.shape[0]
        residual = eye - jnp.dot(
            a[:, :n], x, precision=HI, preferred_element_type=jnp.float32
        )
        result.append(x + mm3(x, right(residual)))
    return result


def side_kernel(fac_ref, other_ref, gtr_ref, out_ref):
    ki = fac_ref.shape[1]
    half = ki // 2
    total = jnp.where(lax.axis_index("mp") == 1, fac_ref[...], other_ref[...])
    top = total[:half]
    low = total[half:ki]
    c_in = jnp.concatenate(
        [top, jnp.concatenate([top[:, half:].T, low[:, :half]], axis=1)], axis=0
    )
    count = total[ki : ki + 1, :1]
    inv_in, inv_out = inverses([c_in, wide(low[:, half:], half)])
    side = mm3(mm3(inv_in, right(gtr_ref[...])), right(inv_out)) * (count * count)
    out_ref[:, :half] = side[:half, :half]
    out_ref[:, half:] = side[half:, :half]


def scores_kernel(order, n_blk, side_ref, gte_ref, other_ref, out_ref):
    z = lax.axis_index("dp")
    b = lax.axis_index("blk")
    lane = lax.broadcasted_iota(jnp.int32, out_ref.shape, 1)
    row = jnp.zeros(out_ref.shape, jnp.float32)
    side = side_ref[...]
    own = lax.axis_index("mp") == 0
    sums = [
        jnp.sum(side * jnp.where(own, gte_ref[p], other_ref[p]), axis=0, keepdims=True)
        for p in range(len(order))
    ]
    values = jnp.sum(jnp.concatenate(sums, axis=0), axis=1, keepdims=True)
    for p, (dz, db) in enumerate(order):
        row = jnp.where(lane == (z ^ dz) * n_blk + (b ^ db), values[p : p + 1, :], row)
    out_ref[...] = row


def project(xs, w_in, w_out, n_groups, n_dp, n_blk):
    tokens, width = xs[0].shape
    rin, rout = w_in.shape[0], w_out.shape[0]
    ki, ko = rin * n_dp, rout * n_dp
    out_shape = jax.ShapeDtypeStruct((3 * tokens, ki), jnp.float32)
    if (n_groups, n_dp, n_blk) != (2, 4, 2):
        w_in = lax.all_gather(w_in, "dp", axis=0, tiled=True)
        w_out = lax.all_gather(w_out, "dp", axis=0, tiled=True)
        return call(project_kernel, out_shape, [vmem()] * 6, (*xs, w_in, w_out))

    part = width // 8
    shard = rin + rout
    q = lax.axis_index(PLANE)
    whole = jnp.concatenate([w_in, w_out], axis=0)
    mine = lax.dynamic_slice(whole, (0, q * 2 * part), (shard, 2 * part))
    opposite = lax.dynamic_slice(whole, (0, (q ^ 3) * 2 * part), (shard, 2 * part))
    operands = (*xs, w_in, w_out)
    *xs, w_in, w_out = call(
        functools.partial(load_kernel, 6),
        tuple(pltpu.VMEM(x.shape, x.dtype) for x in operands),
        [pl.BlockSpec(memory_space=pltpu.HBM)] * 6,
        [pltpu.with_memory_space_constraint(x, pltpu.HBM) for x in operands],
        flops=1 << 30,
        scratch_shapes=[pltpu.SemaphoreType.DMA((12,))],
    )
    halves = [mine[:, :part], mine[:, part:]]
    far = [swap(h, "dp", n_dp, 2) for h in halves]
    far_op = swap(opposite, "dp", n_dp, 2)
    both_a = stack((halves[0], far[0]), w_out)
    near_a = swap(both_a, "dp", n_dp, 1)
    both_b = stack((halves[1], far[1]))
    near_b = swap(both_b, "dp", n_dp, 1)
    za = stack((far[0], near_a))
    along_x, along_y = (0, 1), (1, 0)
    xa = mixed(za, PLANE, (n_groups, n_blk), along_x, along_y)
    ya = mixed(za, PLANE, (n_groups, n_blk), along_y, along_x)
    both_op = stack((opposite, far_op))
    near_op = swap(both_op, "dp", n_dp, 1)
    zb = stack((far[1], near_b))
    xb = mixed(zb, PLANE, (n_groups, n_blk), along_x, along_y)
    yb = mixed(zb, PLANE, (n_groups, n_blk), along_y, along_x)

    def accumulate(plan, pieces, acc):
        args = (*xs, w_in, w_out, *pieces) + (() if acc is None else (acc,))
        total = sum(width for _, _, width, _ in plan)
        return call(
            functools.partial(project_pieces_kernel, plan, acc is not None, len(pieces)),
            out_shape,
            [vmem()] * len(args),
            args,
            flops=1 << 28,
            scratch_shapes=[
                pltpu.VMEM((ki, total), jnp.bfloat16),
                pltpu.VMEM((ko, total), jnp.bfloat16),
            ],
        )

    def stacked(p):
        return tuple((p, i * shard, k) for i, k in enumerate((2, 1, 3)))

    acc = accumulate(
        ((0, 0, part, stacked(0)), (0, part, part, stacked(1))), (za, zb), None)
    acc = accumulate(
        ((1, 0, part, stacked(0)), (2, 0, part, stacked(1))), (xa, ya), acc)
    return accumulate(
        (
            (1, part, part, stacked(0)),
            (2, part, part, stacked(1)),
            (3, 0, 2 * part, ((2, 0, 2), (3, 0, 1), (3, shard, 3))),
        ),
        (xb, yb, far_op, near_op),
        acc,
    )


def per_device(
    n_groups, n_dp, n_blk, train_inputs, train_cotangents, train_lengths,
    test_inputs, test_cotangents, test_lengths, proj_in, proj_out,
):
    _, tokens, width = train_inputs.shape
    xs = [a.reshape(tokens, width) for a in (
        train_inputs, train_cotangents, test_inputs, test_cotangents)]
    part = project(xs, proj_in.T, proj_out.T, n_groups, n_dp, n_blk)
    ki = part.shape[1]
    ko = ki // 2
    other = swap(part, "mp", 2, 1)
    fac, gte, gtr = call(
        moments_kernel,
        (
            jax.ShapeDtypeStruct((ki + 8, ki), jnp.float32),
            jax.ShapeDtypeStruct((1, ki // 2, ki), jnp.float32),
            jax.ShapeDtypeStruct((ki, ko), jnp.float32),
        ),
        [smem(), smem(), vmem(), vmem()],
        (train_lengths, test_lengths, part, other),
    )
    steps_z = [(k, 0) for k in bits(n_dp)]
    steps_x = [(0, k) for k in bits(n_blk)]
    axes, counts, stay = ("dp", "blk"), (n_dp, n_blk), (0, 0)
    order = [(0, 0)]
    for step in steps_z + steps_x:
        gte = jnp.concatenate([gte, mixed(gte, axes, counts, step, stay)], axis=0)
        order += [(dz ^ step[0], db ^ step[1]) for dz, db in order]
    for step in steps_x + steps_z:
        fac = fac + mixed(fac, axes, counts, stay, step)
    fac_other = swap(fac, "mp", 2, 1)
    gte_other = swap(gte, "mp", 2, 1)
    side = call(
        side_kernel,
        jax.ShapeDtypeStruct((ki // 2, ki), jnp.float32),
        [vmem()] * 3,
        (fac, fac_other, gtr),
        flops=4 << 30,
    )
    return call(
        functools.partial(scores_kernel, order, n_blk),
        jax.ShapeDtypeStruct((1, n_dp * n_blk), jnp.float32),
        [vmem()] * 3,
        (side, gte, gte_other),
    )


def solution(mesh):
    feature = P(("groups", "dp", "blk"), None, "mp")
    length = P(("groups", "dp", "blk"))
    weight = P("mp", "dp")
    shape = mesh.shape
    return jax.shard_map(
        functools.partial(per_device, shape["groups"], shape["dp"], shape["blk"]),
        mesh=mesh,
        in_specs=(feature, feature, length, feature, feature, length, weight, weight),
        out_specs=P(("groups", "dp", "blk"), None),
        check_vma=False,
    )
```

```python
import functools

import jax
import jax.numpy as jnp
from jax import lax
from jax.experimental import pallas as pl
from jax.experimental.pallas import tpu as pltpu
from jax.sharding import PartitionSpec as P

HI = lax.Precision.HIGHEST
NT = (((1,), (1,)), ((), ()))
TN = (((0,), (0,)), ((), ()))
NEWTON_STEPS = 7
PLANE = ("groups", "blk")
LANES = 128


def vmem():
    return pl.BlockSpec(memory_space=pltpu.VMEM)


def smem():
    return pl.BlockSpec(memory_space=pltpu.SMEM)


def call(kernel, out_shape, in_specs, args, flops=0, limit=16, **kw):
    return pl.pallas_call(
        kernel,
        out_shape=out_shape,
        in_specs=in_specs,
        out_specs=jax.tree.map(lambda _: vmem(), out_shape),
        compiler_params=pltpu.CompilerParams(vmem_limit_bytes=limit * 1024 * 1024),
        cost_estimate=pl.CostEstimate(flops=flops, bytes_accessed=1 << 16, transcendentals=0),
        **kw,
    )(*args)


def swap(x, axis, count, k):
    return lax.ppermute(x, axis, [(i, i ^ k) for i in range(count)])


def mixed(x, axes, counts, step0, step1):
    pairs = []
    for i in range(counts[0]):
        for j in range(counts[1]):
            for core, (di, dj) in enumerate((step0, step1)):
                pairs.append((
                    (i * counts[1] + j) * 2 + core,
                    ((i ^ di) * counts[1] + (j ^ dj)) * 2 + core,
                ))
    return lax.ppermute(x, (*axes, "mp"), pairs)


def bits(count):
    return [1 << s for s in reversed(range(count.bit_length() - 1))]


def load_kernel(n, *refs):
    srcs, dsts, sem = refs[:n], refs[n : 2 * n], refs[2 * n]
    copies = []
    for i, (src, dst) in enumerate(zip(srcs, dsts)):
        rows = src.shape[0] // 2
        for h in range(2):
            part = pl.ds(h * rows, rows)
            copies.append(pltpu.make_async_copy(src.at[part], dst.at[part], sem.at[2 * i + h]))
    for c in copies:
        c.start()
    for c in copies:
        c.wait()


def stack_kernel(n, *refs):
    at = 0
    for src in refs[:n]:
        refs[-1][at : at + src.shape[0], :] = src[...]
        at += src.shape[0]


def stack(parts, after=None):
    rows = sum(p.shape[0] for p in parts)
    extra = () if after is None else (after,)
    return call(
        functools.partial(stack_kernel, len(parts)),
        pltpu.VMEM((rows, parts[0].shape[1]), parts[0].dtype),
        [vmem()] * len(parts) + [pl.BlockSpec(memory_space=pl.ANY)] * len(extra),
        (*parts, *extra),
        limit=1,
    )


def store_products(x_parts, g_parts, acc_ref, out_ref):
    tokens = out_ref.shape[0] // 3
    ko = g_parts[0].shape[1]
    for n in range(2):
        rows = slice(n * tokens, (n + 1) * tokens)
        prior = 0.0 if acc_ref is None else acc_ref[rows, :]
        out_ref[rows, :] = prior + x_parts[n]
    rows = slice(2 * tokens, 3 * tokens)
    for n in range(2):
        cols = slice(n * ko, (n + 1) * ko)
        prior = 0.0 if acc_ref is None else acc_ref[rows, cols]
        out_ref[rows, cols] = prior + g_parts[n]


def nt(a, b):
    return lax.dot_general(a, b, NT, preferred_element_type=jnp.float32)


def project_kernel(*refs):
    x_refs, (w_in, w_out, out_ref) = refs[:4], refs[4:]
    xs = [nt(x_refs[n][...], w_in[...]) for n in (0, 2)]
    gs = [nt(x_refs[n][...], w_out[...]) for n in (1, 3)]
    store_products(xs, gs, None, out_ref)


def project_pieces_kernel(plan, with_acc, n_pieces, *refs):
    x_refs, (own_in, own_out) = refs[:4], refs[4:6]
    pieces = refs[6 : 6 + n_pieces]
    acc_ref = refs[6 + n_pieces] if with_acc else None
    out_ref, w_in, w_out = refs[6 + n_pieces + with_acc :]
    z = lax.axis_index("dp")
    q = lax.axis_index(PLANE)
    core = lax.axis_index("mp")
    rin, rout = own_in.shape[0], own_out.shape[0]
    quarter = own_in.shape[1] // 4
    xs, gs = [0.0, 0.0], [0.0, 0.0]
    at = 0
    for dq, col, width, rows in plan:
        other = q ^ (core * (3 ^ dq) + (1 - core) * dq) if dq in (1, 2) else q ^ dq
        start = pl.multiple_of(other * quarter + col, 128)
        cols = pl.ds(start, width)
        here = slice(at, at + width)
        at += width
        w_in[pl.ds(pl.multiple_of(z * rin, rin), rin), here] = own_in[:, cols]
        w_out[pl.ds(pl.multiple_of(z * rout, rout), rout), here] = own_out[:, cols]
        for p, row, k in rows:
            dst_in = pl.multiple_of((z ^ k) * rin, rin)
            dst_out = pl.multiple_of((z ^ k) * rout, rout)
            w_in[pl.ds(dst_in, rin), here] = pieces[p][row : row + rin, :]
            w_out[pl.ds(dst_out, rout), here] = pieces[p][row + rin : row + rin + rout, :]
        for m in range(2):
            xs[m] += nt(x_refs[2 * m][:, cols], w_in[:, here])
            gs[m] += nt(x_refs[2 * m + 1][:, cols], w_out[:, here])
    store_products(xs, gs, acc_ref, out_ref)


def moments_kernel(len_tr, len_te, mine, other, fac_ref, gte_ref, gtr_ref):
    tokens = mine.shape[0] // 3
    ki = mine.shape[1]
    ko = ki // 2
    total = mine[...] + other[...]
    rows = lax.broadcasted_iota(jnp.int32, (tokens, ki), 0)
    n_tr, n_te = len_tr[0], len_te[0]
    x_tr = jnp.where(rows < n_tr, total[:tokens], 0.0)
    x_te = jnp.where(rows < n_te, total[tokens : 2 * tokens], 0.0)
    g_both = total[2 * tokens :]
    g_tr = jnp.where(rows < n_tr, g_both, 0.0)[:, :ko]
    g_te = g_both[:, ko:]
    dot = functools.partial(
        lax.dot_general, dimension_numbers=TN, precision=HI,
        preferred_element_type=jnp.float32,
    )
    products = jnp.dot(
        x_tr.T, jnp.concatenate([x_tr, g_tr], axis=1), precision=HI,
        preferred_element_type=jnp.float32,
    )
    c_in = products[:, :ki]
    c_out = dot(g_tr, g_tr)
    half = ki // 2
    fac_ref[:half, :] = c_in[:half, :]
    fac_ref[half:ki, :half] = c_in[half:, half:]
    fac_ref[half:ki, half:] = c_out
    fac_ref[ki:, :] = jnp.full((8, ki), n_tr.astype(jnp.float32))
    grad_tr = products[:, ki:] / n_tr.astype(jnp.float32)
    grad_te = dot(x_te, g_te) / n_te.astype(jnp.float32)
    gtr_ref[...] = grad_tr
    gte_ref[0, :, :ko] = grad_te[:half]
    gte_ref[0, :, ko:] = grad_te[half:]


def wide(x, rows, cols=LANES):
    if x.shape[1] < cols:
        x = jnp.concatenate([x, jnp.zeros((x.shape[0], cols - x.shape[1]), x.dtype)], axis=1)
    if x.shape[0] < rows:
        x = jnp.concatenate([x, jnp.zeros((rows - x.shape[0], cols), x.dtype)], axis=0)
    return x


def parts(x):
    high = x.astype(jnp.bfloat16)
    return high, (x - high.astype(jnp.float32)).astype(jnp.bfloat16)


def right(x):
    high, low = parts(wide(x, LANES))
    upper = jnp.concatenate([high, low], axis=1)
    lower = jnp.concatenate([jnp.zeros_like(high), high], axis=1)
    return jnp.concatenate([upper, lower], axis=0)


def mm3(x, packed):
    both = jnp.dot(
        jnp.concatenate(parts(x), axis=1), packed, preferred_element_type=jnp.float32
    )
    return both[:, :LANES] + both[:, LANES:]


def damped(c):
    n = c.shape[0]
    i = lax.broadcasted_iota(jnp.int32, c.shape, 0)
    j = lax.broadcasted_iota(jnp.int32, c.shape, 1)
    eye = (i == j).astype(jnp.float32)
    trace = jnp.sum(jnp.sum(c * eye, axis=0, keepdims=True), axis=1, keepdims=True)
    low = 0.1 * trace / n
    a = c + low * eye
    high = jnp.max(jnp.sum(jnp.abs(a), axis=0, keepdims=True), axis=1, keepdims=True)
    return a, eye, low, jnp.minimum(high, trace + low)


def inverses(matrices):
    state = []
    for c in matrices:
        a, eye, low, high = damped(c)
        scale = 2.0 / (low + high)
        r = (high - low) / (high + low)
        state.append((a, eye, scale * a, scale * eye, scale, r))
    for step in range(NEWTON_STEPS):
        nxt = []
        for a, eye, m, x, scale, r in state:
            s = 2.0 / (2.0 - r * r)
            n = m.shape[0]
            if step == 0:
                mx = s * (2.0 * m - mm3(m, right(m)))
                xx = s * (2.0 * x - scale * m)
            else:
                both = mm3(jnp.concatenate([m, x], axis=0), right(m))
                mx = s * (2.0 * m - both[:n])
                xx = s * (2.0 * x - both[n:])
            nxt.append((a, eye, mx, xx, scale, r * r / (2.0 - r * r)))
        state = nxt
    result = []
    for a, eye, m, x, scale, r in state:
        n = a.shape[0]
        residual = eye - jnp.dot(
            a[:, :n], x, precision=HI, preferred_element_type=jnp.float32
        )
        result.append(x + mm3(x, right(residual)))
    return result


def side_kernel(fac_ref, gtr_ref, out_ref):
    ki = fac_ref.shape[1]
    half = ki // 2
    top = fac_ref[:half, :]
    low = fac_ref[half:ki, :]
    c_in = jnp.concatenate(
        [top, jnp.concatenate([top[:, half:].T, low[:, :half]], axis=1)], axis=0
    )
    count = fac_ref[ki : ki + 1, :1]
    inv_in, inv_out = inverses([c_in, wide(low[:, half:], half)])
    side = mm3(mm3(inv_in, right(gtr_ref[...])), right(inv_out)) * (count * count)
    out_ref[:, :half] = side[:half, :half]
    out_ref[:, half:] = side[half:, :half]


def scores_kernel(order, n_blk, side_ref, gte_ref, out_ref):
    z = lax.axis_index("dp")
    b = lax.axis_index("blk")
    lane = lax.broadcasted_iota(jnp.int32, out_ref.shape, 1)
    row = jnp.zeros(out_ref.shape, jnp.float32)
    side = side_ref[...]
    sums = [jnp.sum(side * gte_ref[p], axis=0, keepdims=True) for p in range(len(order))]
    values = jnp.sum(jnp.concatenate(sums, axis=0), axis=1, keepdims=True)
    for p, (dz, db) in enumerate(order):
        row = jnp.where(lane == (z ^ dz) * n_blk + (b ^ db), values[p : p + 1, :], row)
    out_ref[...] = row


def project(xs, w_in, w_out, n_groups, n_dp, n_blk):
    tokens, width = xs[0].shape
    rin, rout = w_in.shape[0], w_out.shape[0]
    ki, ko = rin * n_dp, rout * n_dp
    out_shape = jax.ShapeDtypeStruct((3 * tokens, ki), jnp.float32)
    if (n_groups, n_dp, n_blk) != (2, 4, 2):
        w_in = lax.all_gather(w_in, "dp", axis=0, tiled=True)
        w_out = lax.all_gather(w_out, "dp", axis=0, tiled=True)
        return call(project_kernel, out_shape, [vmem()] * 6, (*xs, w_in, w_out))

    part = width // 8
    shard = rin + rout
    q = lax.axis_index(PLANE)
    whole = jnp.concatenate([w_in, w_out], axis=0)
    mine = lax.dynamic_slice(whole, (0, q * 2 * part), (shard, 2 * part))
    opposite = lax.dynamic_slice(whole, (0, (q ^ 3) * 2 * part), (shard, 2 * part))
    operands = (*xs, w_in, w_out)
    *xs, w_in, w_out = call(
        functools.partial(load_kernel, 6),
        tuple(pltpu.VMEM(x.shape, x.dtype) for x in operands),
        [pl.BlockSpec(memory_space=pltpu.HBM)] * 6,
        [pltpu.with_memory_space_constraint(x, pltpu.HBM) for x in operands],
        flops=1 << 30,
        scratch_shapes=[pltpu.SemaphoreType.DMA((12,))],
    )
    halves = [mine[:, :part], mine[:, part:]]
    far = [swap(h, "dp", n_dp, 2) for h in halves]
    far_op = swap(opposite, "dp", n_dp, 2)
    both_a = stack((halves[0], far[0]), w_out)
    near_a = swap(both_a, "dp", n_dp, 1)
    both_b = stack((halves[1], far[1]))
    near_b = swap(both_b, "dp", n_dp, 1)
    za = stack((far[0], near_a), far_op)
    along_x, along_y = (0, 1), (1, 0)
    xa = mixed(za, PLANE, (n_groups, n_blk), along_x, along_y)
    ya = mixed(za, PLANE, (n_groups, n_blk), along_y, along_x)
    both_op = stack((opposite, far_op))
    near_op = swap(both_op, "dp", n_dp, 1)
    zb = stack((far[1], near_b))
    xb = mixed(zb, PLANE, (n_groups, n_blk), along_x, along_y)
    yb = mixed(zb, PLANE, (n_groups, n_blk), along_y, along_x)

    def accumulate(plan, pieces, acc):
        args = (*xs, w_in, w_out, *pieces) + (() if acc is None else (acc,))
        total = sum(width for _, _, width, _ in plan)
        return call(
            functools.partial(project_pieces_kernel, plan, acc is not None, len(pieces)),
            out_shape,
            [vmem()] * len(args),
            args,
            flops=1 << 30,
            scratch_shapes=[
                pltpu.VMEM((ki, total), jnp.bfloat16),
                pltpu.VMEM((ko, total), jnp.bfloat16),
            ],
        )

    def stacked(p):
        return tuple((p, i * shard, k) for i, k in enumerate((2, 1, 3)))

    acc = accumulate(
        ((0, 0, part, stacked(0)), (0, part, part, stacked(1))), (za, zb), None)
    acc = accumulate(
        ((1, 0, part, stacked(0)), (2, 0, part, stacked(1))), (xa, ya), acc)
    return accumulate(
        (
            (1, part, part, stacked(0)),
            (2, part, part, stacked(1)),
            (3, 0, 2 * part, ((2, 0, 2), (3, 0, 1), (3, shard, 3))),
        ),
        (xb, yb, far_op, near_op),
        acc,
    )


def per_device(
    n_groups, n_dp, n_blk, train_inputs, train_cotangents, train_lengths,
    test_inputs, test_cotangents, test_lengths, proj_in, proj_out,
):
    _, tokens, width = train_inputs.shape
    xs = [a.reshape(tokens, width) for a in (
        train_inputs, train_cotangents, test_inputs, test_cotangents)]
    part = project(xs, proj_in.T, proj_out.T, n_groups, n_dp, n_blk)
    ki = part.shape[1]
    ko = ki // 2
    other = swap(part, "mp", 2, 1)
    fac, gte, gtr = call(
        moments_kernel,
        (
            jax.ShapeDtypeStruct((ki + 8, ki), jnp.float32),
            jax.ShapeDtypeStruct((1, ki // 2, ki), jnp.float32),
            jax.ShapeDtypeStruct((ki, ko), jnp.float32),
        ),
        [smem(), smem(), vmem(), vmem()],
        (train_lengths, test_lengths, part, other),
    )
    order = [(0, 0)]
    for axis, count in (("dp", n_dp), ("blk", n_blk)):
        for k in bits(count):
            gte = jnp.concatenate([gte, swap(gte, axis, count, k)], axis=0)
            order += [(dz ^ k, db) if axis == "dp" else (dz, db ^ k) for dz, db in order]
    steps_z = [(k, 0) for k in bits(n_dp)]
    steps_x = [(0, k) for k in bits(n_blk)]
    first = steps_x + steps_z[::-1]
    second = steps_z[:1] + steps_x + steps_z[1:]
    for step0, step1 in zip(first, second):
        fac = fac + mixed(fac, ("dp", "blk"), (n_dp, n_blk), step0, step1)
    side = call(
        side_kernel,
        jax.ShapeDtypeStruct((ki // 2, ki), jnp.float32),
        [vmem()] * 2,
        (fac, gtr),
        flops=4 << 30,
    )
    return call(
        functools.partial(scores_kernel, order, n_blk),
        jax.ShapeDtypeStruct((1, n_dp * n_blk), jnp.float32),
        [vmem()] * 2,
        (side, gte),
    )


def solution(mesh):
    feature = P(("groups", "dp", "blk"), None, "mp")
    length = P(("groups", "dp", "blk"))
    weight = P("mp", "dp")
    shape = mesh.shape
    return jax.shard_map(
        functools.partial(per_device, shape["groups"], shape["dp"], shape["blk"]),
        mesh=mesh,
        in_specs=(feature, feature, length, feature, feature, length, weight, weight),
        out_specs=P(("groups", "dp", "blk"), None),
        check_vma=False,
    )
```

```python
import functools

import jax
import jax.numpy as jnp
from jax import lax
from jax.experimental import pallas as pl
from jax.experimental.pallas import tpu as pltpu
from jax.sharding import PartitionSpec as P

HI = lax.Precision.HIGHEST
NT = (((1,), (1,)), ((), ()))
TN = (((0,), (0,)), ((), ()))
NEWTON_STEPS = 7
PLANE = ("groups", "blk")
LANES = 128


def vmem():
    return pl.BlockSpec(memory_space=pltpu.VMEM)


def smem():
    return pl.BlockSpec(memory_space=pltpu.SMEM)


def call(kernel, out_shape, in_specs, args, flops=0, limit=16, **kw):
    return pl.pallas_call(
        kernel,
        out_shape=out_shape,
        in_specs=in_specs,
        out_specs=jax.tree.map(lambda _: vmem(), out_shape),
        compiler_params=pltpu.CompilerParams(vmem_limit_bytes=limit * 1024 * 1024),
        cost_estimate=pl.CostEstimate(flops=flops, bytes_accessed=1 << 16, transcendentals=0),
        **kw,
    )(*args)


def swap(x, axis, count, k):
    return lax.ppermute(x, axis, [(i, i ^ k) for i in range(count)])


def mixed(x, axes, counts, step0, step1):
    pairs = []
    for i in range(counts[0]):
        for j in range(counts[1]):
            for core, (di, dj) in enumerate((step0, step1)):
                pairs.append((
                    (i * counts[1] + j) * 2 + core,
                    ((i ^ di) * counts[1] + (j ^ dj)) * 2 + core,
                ))
    return lax.ppermute(x, (*axes, "mp"), pairs)


def bits(count):
    return [1 << s for s in reversed(range(count.bit_length() - 1))]


def load_kernel(n, *refs):
    srcs, dsts, sem = refs[:n], refs[n : 2 * n], refs[2 * n]
    copies = []
    for i, (src, dst) in enumerate(zip(srcs, dsts)):
        rows = src.shape[0] // 2
        for h in range(2):
            part = pl.ds(h * rows, rows)
            copies.append(pltpu.make_async_copy(src.at[part], dst.at[part], sem.at[2 * i + h]))
    for c in copies:
        c.start()
    for c in copies:
        c.wait()


def stack_kernel(n, *refs):
    at = 0
    for src in refs[:n]:
        refs[-1][at : at + src.shape[0], :] = src[...]
        at += src.shape[0]


def stack(parts, after=None):
    rows = sum(p.shape[0] for p in parts)
    extra = () if after is None else (after,)
    return call(
        functools.partial(stack_kernel, len(parts)),
        pltpu.VMEM((rows, parts[0].shape[1]), parts[0].dtype),
        [vmem()] * len(parts) + [pl.BlockSpec(memory_space=pl.ANY)] * len(extra),
        (*parts, *extra),
        limit=1,
    )


def store_products(x_parts, g_parts, acc_ref, out_ref):
    tokens = out_ref.shape[0] // 3
    ko = g_parts[0].shape[1]
    for n in range(2):
        rows = slice(n * tokens, (n + 1) * tokens)
        prior = 0.0 if acc_ref is None else acc_ref[rows, :]
        out_ref[rows, :] = prior + x_parts[n]
    rows = slice(2 * tokens, 3 * tokens)
    for n in range(2):
        cols = slice(n * ko, (n + 1) * ko)
        prior = 0.0 if acc_ref is None else acc_ref[rows, cols]
        out_ref[rows, cols] = prior + g_parts[n]


def nt(a, b):
    return lax.dot_general(a, b, NT, preferred_element_type=jnp.float32)


def project_kernel(*refs):
    x_refs, (w_in, w_out, out_ref) = refs[:4], refs[4:]
    xs = [nt(x_refs[n][...], w_in[...]) for n in (0, 2)]
    gs = [nt(x_refs[n][...], w_out[...]) for n in (1, 3)]
    store_products(xs, gs, None, out_ref)


def project_pieces_kernel(plan, with_acc, n_pieces, *refs):
    x_refs, (own_in, own_out) = refs[:4], refs[4:6]
    pieces = refs[6 : 6 + n_pieces]
    acc_ref = refs[6 + n_pieces] if with_acc else None
    out_ref, w_in, w_out = refs[6 + n_pieces + with_acc :]
    z = lax.axis_index("dp")
    q = lax.axis_index(PLANE)
    core = lax.axis_index("mp")
    rin, rout = own_in.shape[0], own_out.shape[0]
    quarter = own_in.shape[1] // 4
    xs, gs = [0.0, 0.0], [0.0, 0.0]
    at = 0
    for dq, col, width, rows in plan:
        other = q ^ (core * (3 ^ dq) + (1 - core) * dq) if dq in (1, 2) else q ^ dq
        start = pl.multiple_of(other * quarter + col, 128)
        cols = pl.ds(start, width)
        here = slice(at, at + width)
        at += width
        w_in[pl.ds(pl.multiple_of(z * rin, rin), rin), here] = own_in[:, cols]
        w_out[pl.ds(pl.multiple_of(z * rout, rout), rout), here] = own_out[:, cols]
        for p, row, k in rows:
            dst_in = pl.multiple_of((z ^ k) * rin, rin)
            dst_out = pl.multiple_of((z ^ k) * rout, rout)
            w_in[pl.ds(dst_in, rin), here] = pieces[p][row : row + rin, :]
            w_out[pl.ds(dst_out, rout), here] = pieces[p][row + rin : row + rin + rout, :]
        for m in range(2):
            xs[m] += nt(x_refs[2 * m][:, cols], w_in[:, here])
            gs[m] += nt(x_refs[2 * m + 1][:, cols], w_out[:, here])
    store_products(xs, gs, acc_ref, out_ref)


def moments_kernel(len_tr, len_te, mine, other, fac_ref, gte_ref, gtr_ref):
    tokens = mine.shape[0] // 3
    ki = mine.shape[1]
    ko = ki // 2
    total = mine[...] + other[...]
    rows = lax.broadcasted_iota(jnp.int32, (tokens, ki), 0)
    n_tr, n_te = len_tr[0], len_te[0]
    x_tr = jnp.where(rows < n_tr, total[:tokens], 0.0)
    x_te = jnp.where(rows < n_te, total[tokens : 2 * tokens], 0.0)
    g_both = total[2 * tokens :]
    g_tr = jnp.where(rows < n_tr, g_both, 0.0)[:, :ko]
    g_te = g_both[:, ko:]
    dot = functools.partial(
        lax.dot_general, dimension_numbers=TN, precision=HI,
        preferred_element_type=jnp.float32,
    )
    products = jnp.dot(
        x_tr.T, jnp.concatenate([x_tr, g_tr], axis=1), precision=HI,
        preferred_element_type=jnp.float32,
    )
    c_in = products[:, :ki]
    c_out = dot(g_tr, g_tr)
    half = ki // 2
    fac_ref[:half, :] = c_in[:half, :]
    fac_ref[half:ki, :half] = c_in[half:, half:]
    fac_ref[half:ki, half:] = c_out
    fac_ref[ki:, :] = jnp.full((8, ki), n_tr.astype(jnp.float32))
    grad_tr = products[:, ki:] / n_tr.astype(jnp.float32)
    grad_te = dot(x_te, g_te) / n_te.astype(jnp.float32)
    gtr_ref[...] = grad_tr
    gte_ref[0, :, :ko] = grad_te[:half]
    gte_ref[0, :, ko:] = grad_te[half:]


def wide(x, rows, cols=LANES):
    if x.shape[1] < cols:
        x = jnp.concatenate([x, jnp.zeros((x.shape[0], cols - x.shape[1]), x.dtype)], axis=1)
    if x.shape[0] < rows:
        x = jnp.concatenate([x, jnp.zeros((rows - x.shape[0], cols), x.dtype)], axis=0)
    return x


def parts(x):
    high = x.astype(jnp.bfloat16)
    return high, (x - high.astype(jnp.float32)).astype(jnp.bfloat16)


def right(x):
    high, low = parts(wide(x, LANES))
    upper = jnp.concatenate([high, low], axis=1)
    lower = jnp.concatenate([jnp.zeros_like(high), high], axis=1)
    return jnp.concatenate([upper, lower], axis=0)


def mm3(x, packed):
    both = jnp.dot(
        jnp.concatenate(parts(x), axis=1), packed, preferred_element_type=jnp.float32
    )
    return both[:, :LANES] + both[:, LANES:]


def damped(c):
    n = c.shape[0]
    i = lax.broadcasted_iota(jnp.int32, c.shape, 0)
    j = lax.broadcasted_iota(jnp.int32, c.shape, 1)
    eye = (i == j).astype(jnp.float32)
    trace = jnp.sum(jnp.sum(c * eye, axis=0, keepdims=True), axis=1, keepdims=True)
    low = 0.1 * trace / n
    a = c + low * eye
    high = jnp.max(jnp.sum(jnp.abs(a), axis=0, keepdims=True), axis=1, keepdims=True)
    return a, eye, low, jnp.minimum(high, trace + low)


def inverses(matrices):
    state = []
    for c in matrices:
        a, eye, low, high = damped(c)
        scale = 2.0 / (low + high)
        r = (high - low) / (high + low)
        state.append((a, eye, scale * a, scale * eye, scale, r))
    for step in range(NEWTON_STEPS):
        nxt = []
        for a, eye, m, x, scale, r in state:
            s = 2.0 / (2.0 - r * r)
            n = m.shape[0]
            if step == 0:
                mx = s * (2.0 * m - mm3(m, right(m)))
                xx = s * (2.0 * x - scale * m)
            else:
                both = mm3(jnp.concatenate([m, x], axis=0), right(m))
                mx = s * (2.0 * m - both[:n])
                xx = s * (2.0 * x - both[n:])
            nxt.append((a, eye, mx, xx, scale, r * r / (2.0 - r * r)))
        state = nxt
    result = []
    for a, eye, m, x, scale, r in state:
        n = a.shape[0]
        residual = eye - jnp.dot(
            a[:, :n], x, precision=HI, preferred_element_type=jnp.float32
        )
        result.append(x + mm3(x, right(residual)))
    return result


def side_kernel(fac_ref, gtr_ref, out_ref):
    ki = fac_ref.shape[1]
    half = ki // 2
    top = fac_ref[:half, :]
    low = fac_ref[half:ki, :]
    c_in = jnp.concatenate(
        [top, jnp.concatenate([top[:, half:].T, low[:, :half]], axis=1)], axis=0
    )
    count = fac_ref[ki : ki + 1, :1]
    inv_in, inv_out = inverses([c_in, wide(low[:, half:], half)])
    side = mm3(mm3(inv_in, right(gtr_ref[...])), right(inv_out)) * (count * count)
    out_ref[:, :half] = side[:half, :half]
    out_ref[:, half:] = side[half:, :half]


def scores_kernel(order, n_blk, side_ref, gte_ref, out_ref):
    z = lax.axis_index("dp")
    b = lax.axis_index("blk")
    lane = lax.broadcasted_iota(jnp.int32, out_ref.shape, 1)
    row = jnp.zeros(out_ref.shape, jnp.float32)
    side = side_ref[...]
    sums = [jnp.sum(side * gte_ref[p], axis=0, keepdims=True) for p in range(len(order))]
    values = jnp.sum(jnp.concatenate(sums, axis=0), axis=1, keepdims=True)
    for p, (dz, db) in enumerate(order):
        row = jnp.where(lane == (z ^ dz) * n_blk + (b ^ db), values[p : p + 1, :], row)
    out_ref[...] = row


def project(xs, w_in, w_out, n_groups, n_dp, n_blk):
    tokens, width = xs[0].shape
    rin, rout = w_in.shape[0], w_out.shape[0]
    ki, ko = rin * n_dp, rout * n_dp
    out_shape = jax.ShapeDtypeStruct((3 * tokens, ki), jnp.float32)
    if (n_groups, n_dp, n_blk) != (2, 4, 2):
        w_in = lax.all_gather(w_in, "dp", axis=0, tiled=True)
        w_out = lax.all_gather(w_out, "dp", axis=0, tiled=True)
        return call(project_kernel, out_shape, [vmem()] * 6, (*xs, w_in, w_out))

    part = width // 8
    shard = rin + rout
    q = lax.axis_index(PLANE)
    whole = jnp.concatenate([w_in, w_out], axis=0)
    mine = lax.dynamic_slice(whole, (0, q * 2 * part), (shard, 2 * part))
    opposite = lax.dynamic_slice(whole, (0, (q ^ 3) * 2 * part), (shard, 2 * part))
    operands = (*xs, w_in, w_out)
    *xs, w_in, w_out = call(
        functools.partial(load_kernel, 6),
        tuple(pltpu.VMEM(x.shape, x.dtype) for x in operands),
        [pl.BlockSpec(memory_space=pltpu.HBM)] * 6,
        [pltpu.with_memory_space_constraint(x, pltpu.HBM) for x in operands],
        flops=1 << 30,
        scratch_shapes=[pltpu.SemaphoreType.DMA((12,))],
    )
    halves = [mine[:, :part], mine[:, part:]]
    far = [swap(h, "dp", n_dp, 2) for h in halves]
    far_op = swap(opposite, "dp", n_dp, 2)
    both_a = stack((halves[0], far[0]))
    near_a = swap(both_a, "dp", n_dp, 1)
    both_b = stack((halves[1], far[1]))
    near_b = swap(both_b, "dp", n_dp, 1)
    za = stack((far[0], near_a))
    along_x, along_y = (0, 1), (1, 0)
    xa = mixed(za, PLANE, (n_groups, n_blk), along_x, along_y)
    ya = mixed(za, PLANE, (n_groups, n_blk), along_y, along_x)
    both_op = stack((opposite, far_op))
    near_op = swap(both_op, "dp", n_dp, 1)
    zb = stack((far[1], near_b))
    xb = mixed(zb, PLANE, (n_groups, n_blk), along_x, along_y)
    yb = mixed(zb, PLANE, (n_groups, n_blk), along_y, along_x)

    def accumulate(plan, pieces, acc):
        args = (*xs, w_in, w_out, *pieces) + (() if acc is None else (acc,))
        total = sum(width for _, _, width, _ in plan)
        return call(
            functools.partial(project_pieces_kernel, plan, acc is not None, len(pieces)),
            out_shape,
            [vmem()] * len(args),
            args,
            flops=1 << 28,
            scratch_shapes=[
                pltpu.VMEM((ki, total), jnp.bfloat16),
                pltpu.VMEM((ko, total), jnp.bfloat16),
            ],
        )

    def stacked(p):
        return tuple((p, i * shard, k) for i, k in enumerate((2, 1, 3)))

    acc = accumulate(
        ((0, 0, part, stacked(0)), (0, part, part, stacked(1))), (za, zb), None)
    acc = accumulate(
        ((1, 0, part, stacked(0)), (2, 0, part, stacked(1))), (xa, ya), acc)
    return accumulate(
        (
            (1, part, part, stacked(0)),
            (2, part, part, stacked(1)),
            (3, 0, 2 * part, ((2, 0, 2), (3, 0, 1), (3, shard, 3))),
        ),
        (xb, yb, far_op, near_op),
        acc,
    )


def per_device(
    n_groups, n_dp, n_blk, train_inputs, train_cotangents, train_lengths,
    test_inputs, test_cotangents, test_lengths, proj_in, proj_out,
):
    _, tokens, width = train_inputs.shape
    xs = [a.reshape(tokens, width) for a in (
        train_inputs, train_cotangents, test_inputs, test_cotangents)]
    part = project(xs, proj_in.T, proj_out.T, n_groups, n_dp, n_blk)
    ki = part.shape[1]
    ko = ki // 2
    other = swap(part, "mp", 2, 1)
    fac, gte, gtr = call(
        moments_kernel,
        (
            jax.ShapeDtypeStruct((ki + 8, ki), jnp.float32),
            jax.ShapeDtypeStruct((1, ki // 2, ki), jnp.float32),
            jax.ShapeDtypeStruct((ki, ko), jnp.float32),
        ),
        [smem(), smem(), vmem(), vmem()],
        (train_lengths, test_lengths, part, other),
    )
    order = [(0, 0)]
    for axis, count in (("dp", n_dp), ("blk", n_blk)):
        for k in bits(count):
            gte = jnp.concatenate([gte, swap(gte, axis, count, k)], axis=0)
            order += [(dz ^ k, db) if axis == "dp" else (dz, db ^ k) for dz, db in order]
    steps_z = [(k, 0) for k in bits(n_dp)]
    steps_x = [(0, k) for k in bits(n_blk)]
    first = steps_x + steps_z[::-1]
    second = steps_z[:1] + steps_x + steps_z[1:]
    for step0, step1 in zip(first, second):
        fac = fac + mixed(fac, ("dp", "blk"), (n_dp, n_blk), step0, step1)
    side = call(
        side_kernel,
        jax.ShapeDtypeStruct((ki // 2, ki), jnp.float32),
        [vmem()] * 2,
        (fac, gtr),
        flops=4 << 30,
    )
    return call(
        functools.partial(scores_kernel, order, n_blk),
        jax.ShapeDtypeStruct((1, n_dp * n_blk), jnp.float32),
        [vmem()] * 2,
        (side, gte),
    )


def solution(mesh):
    feature = P(("groups", "dp", "blk"), None, "mp")
    length = P(("groups", "dp", "blk"))
    weight = P("mp", "dp")
    shape = mesh.shape
    return jax.shard_map(
        functools.partial(per_device, shape["groups"], shape["dp"], shape["blk"]),
        mesh=mesh,
        in_specs=(feature, feature, length, feature, feature, length, weight, weight),
        out_specs=P(("groups", "dp", "blk"), None),
        check_vma=False,
    )
```

```python
import functools

import jax
import jax.numpy as jnp
from jax import lax
from jax.experimental import pallas as pl
from jax.experimental.pallas import tpu as pltpu
from jax.sharding import PartitionSpec as P

HI = lax.Precision.HIGHEST
NT = (((1,), (1,)), ((), ()))
TN = (((0,), (0,)), ((), ()))
NEWTON_STEPS = 7
PLANE = ("groups", "blk")
LANES = 128


def vmem():
    return pl.BlockSpec(memory_space=pltpu.VMEM)


def smem():
    return pl.BlockSpec(memory_space=pltpu.SMEM)


def call(kernel, out_shape, in_specs, args, flops=0, limit=16, **kw):
    return pl.pallas_call(
        kernel,
        out_shape=out_shape,
        in_specs=in_specs,
        out_specs=jax.tree.map(lambda _: vmem(), out_shape),
        compiler_params=pltpu.CompilerParams(vmem_limit_bytes=limit * 1024 * 1024),
        cost_estimate=pl.CostEstimate(flops=flops, bytes_accessed=1 << 16, transcendentals=0),
        **kw,
    )(*args)


def swap(x, axis, count, k):
    return lax.ppermute(x, axis, [(i, i ^ k) for i in range(count)])


def mixed(x, axes, counts, step0, step1):
    pairs = []
    for i in range(counts[0]):
        for j in range(counts[1]):
            for core, (di, dj) in enumerate((step0, step1)):
                pairs.append((
                    (i * counts[1] + j) * 2 + core,
                    ((i ^ di) * counts[1] + (j ^ dj)) * 2 + core,
                ))
    return lax.ppermute(x, (*axes, "mp"), pairs)


def bits(count):
    return [1 << s for s in reversed(range(count.bit_length() - 1))]


def load_kernel(n, *refs):
    srcs, dsts, sem = refs[:n], refs[n : 2 * n], refs[2 * n]
    copies = []
    for i, (src, dst) in enumerate(zip(srcs, dsts)):
        rows = src.shape[0] // 2
        for h in range(2):
            part = pl.ds(h * rows, rows)
            copies.append(pltpu.make_async_copy(src.at[part], dst.at[part], sem.at[2 * i + h]))
    for c in copies:
        c.start()
    for c in copies:
        c.wait()


def stack_kernel(n, *refs):
    at = 0
    for src in refs[:n]:
        refs[-1][at : at + src.shape[0], :] = src[...]
        at += src.shape[0]


def stack(parts, after=None):
    rows = sum(p.shape[0] for p in parts)
    extra = () if after is None else (after,)
    return call(
        functools.partial(stack_kernel, len(parts)),
        pltpu.VMEM((rows, parts[0].shape[1]), parts[0].dtype),
        [vmem()] * len(parts) + [pl.BlockSpec(memory_space=pl.ANY)] * len(extra),
        (*parts, *extra),
        limit=1,
    )


def store_products(x_parts, g_parts, acc_ref, out_ref):
    tokens = out_ref.shape[0] // 3
    ko = g_parts[0].shape[1]
    for n in range(2):
        rows = slice(n * tokens, (n + 1) * tokens)
        prior = 0.0 if acc_ref is None else acc_ref[rows, :]
        out_ref[rows, :] = prior + x_parts[n]
    rows = slice(2 * tokens, 3 * tokens)
    for n in range(2):
        cols = slice(n * ko, (n + 1) * ko)
        prior = 0.0 if acc_ref is None else acc_ref[rows, cols]
        out_ref[rows, cols] = prior + g_parts[n]


def nt(a, b):
    return lax.dot_general(a, b, NT, preferred_element_type=jnp.float32)


def project_kernel(*refs):
    x_refs, (w_in, w_out, out_ref) = refs[:4], refs[4:]
    xs = [nt(x_refs[n][...], w_in[...]) for n in (0, 2)]
    gs = [nt(x_refs[n][...], w_out[...]) for n in (1, 3)]
    store_products(xs, gs, None, out_ref)


def project_pieces_kernel(plan, with_acc, n_pieces, *refs):
    x_refs, (own_in, own_out) = refs[:4], refs[4:6]
    pieces = refs[6 : 6 + n_pieces]
    acc_ref = refs[6 + n_pieces] if with_acc else None
    out_ref, w_in, w_out = refs[6 + n_pieces + with_acc :]
    z = lax.axis_index("dp")
    q = lax.axis_index(PLANE)
    core = lax.axis_index("mp")
    rin, rout = own_in.shape[0], own_out.shape[0]
    quarter = own_in.shape[1] // 4
    xs, gs = [0.0, 0.0], [0.0, 0.0]
    at = 0
    for dq, col, width, rows in plan:
        other = q ^ (core * (3 ^ dq) + (1 - core) * dq) if dq in (1, 2) else q ^ dq
        start = pl.multiple_of(other * quarter + col, 128)
        cols = pl.ds(start, width)
        here = slice(at, at + width)
        at += width
        w_in[pl.ds(pl.multiple_of(z * rin, rin), rin), here] = own_in[:, cols]
        w_out[pl.ds(pl.multiple_of(z * rout, rout), rout), here] = own_out[:, cols]
        for p, row, k in rows:
            dst_in = pl.multiple_of((z ^ k) * rin, rin)
            dst_out = pl.multiple_of((z ^ k) * rout, rout)
            w_in[pl.ds(dst_in, rin), here] = pieces[p][row : row + rin, :]
            w_out[pl.ds(dst_out, rout), here] = pieces[p][row + rin : row + rin + rout, :]
        for m in range(2):
            xs[m] += nt(x_refs[2 * m][:, cols], w_in[:, here])
            gs[m] += nt(x_refs[2 * m + 1][:, cols], w_out[:, here])
    store_products(xs, gs, acc_ref, out_ref)


def with_corner(x, value):
    row = lax.broadcasted_iota(jnp.int32, x.shape, 0)
    col = lax.broadcasted_iota(jnp.int32, x.shape, 1)
    return jnp.where((row == 1) & (col == 0), value, x)


def moments_kernel(len_tr, len_te, mine, other, fac_ref, gte_ref, gtr_ref):
    tokens = mine.shape[0] // 3
    ki = mine.shape[1]
    ko = ki // 2
    total = mine[...] + other[...]
    rows = lax.broadcasted_iota(jnp.int32, (tokens, ki), 0)
    n_tr, n_te = len_tr[0], len_te[0]
    x_tr = jnp.where(rows < n_tr, total[:tokens], 0.0)
    x_te = jnp.where(rows < n_te, total[tokens : 2 * tokens], 0.0)
    g_both = total[2 * tokens :]
    g_tr = jnp.where(rows < n_tr, g_both, 0.0)[:, :ko]
    g_te = g_both[:, ko:]
    dot = functools.partial(
        lax.dot_general, dimension_numbers=TN, precision=HI,
        preferred_element_type=jnp.float32,
    )
    products = jnp.dot(
        x_tr.T, jnp.concatenate([x_tr, g_tr], axis=1), precision=HI,
        preferred_element_type=jnp.float32,
    )
    c_in = products[:, :ki]
    c_out = with_corner(dot(g_tr, g_tr), n_tr.astype(jnp.float32))
    half = ki // 2
    fac_ref[:half, :] = c_in[:half, :]
    fac_ref[half:ki, :half] = c_in[half:, half:]
    fac_ref[half:ki, half:] = c_out
    grad_tr = products[:, ki:] / n_tr.astype(jnp.float32)
    grad_te = dot(x_te, g_te) / n_te.astype(jnp.float32)
    gtr_ref[...] = grad_tr
    gte_ref[0, :, :ko] = grad_te[:half]
    gte_ref[0, :, ko:] = grad_te[half:]


def wide(x, rows, cols=LANES):
    if x.shape[1] < cols:
        x = jnp.concatenate([x, jnp.zeros((x.shape[0], cols - x.shape[1]), x.dtype)], axis=1)
    if x.shape[0] < rows:
        x = jnp.concatenate([x, jnp.zeros((rows - x.shape[0], cols), x.dtype)], axis=0)
    return x


def parts(x):
    high = x.astype(jnp.bfloat16)
    return high, (x - high.astype(jnp.float32)).astype(jnp.bfloat16)


def right(x):
    high, low = parts(wide(x, LANES))
    upper = jnp.concatenate([high, low], axis=1)
    lower = jnp.concatenate([jnp.zeros_like(high), high], axis=1)
    return jnp.concatenate([upper, lower], axis=0)


def mm3(x, packed):
    both = jnp.dot(
        jnp.concatenate(parts(x), axis=1), packed, preferred_element_type=jnp.float32
    )
    return both[:, :LANES] + both[:, LANES:]


def damped(c):
    n = c.shape[0]
    i = lax.broadcasted_iota(jnp.int32, c.shape, 0)
    j = lax.broadcasted_iota(jnp.int32, c.shape, 1)
    eye = (i == j).astype(jnp.float32)
    trace = jnp.sum(jnp.sum(c * eye, axis=0, keepdims=True), axis=1, keepdims=True)
    low = 0.1 * trace / n
    a = c + low * eye
    high = jnp.max(jnp.sum(jnp.abs(a), axis=0, keepdims=True), axis=1, keepdims=True)
    return a, eye, low, jnp.minimum(high, trace + low)


def inverses(matrices):
    state = []
    for c in matrices:
        a, eye, low, high = damped(c)
        scale = 2.0 / (low + high)
        r = (high - low) / (high + low)
        state.append((a, eye, scale * a, scale * eye, scale, r))
    for step in range(NEWTON_STEPS):
        nxt = []
        for a, eye, m, x, scale, r in state:
            s = 2.0 / (2.0 - r * r)
            n = m.shape[0]
            if step == 0:
                mx = s * (2.0 * m - mm3(m, right(m)))
                xx = s * (2.0 * x - scale * m)
            else:
                both = mm3(jnp.concatenate([m, x], axis=0), right(m))
                mx = s * (2.0 * m - both[:n])
                xx = s * (2.0 * x - both[n:])
            nxt.append((a, eye, mx, xx, scale, r * r / (2.0 - r * r)))
        state = nxt
    result = []
    for a, eye, m, x, scale, r in state:
        n = a.shape[0]
        residual = eye - jnp.dot(
            a[:, :n], x, precision=HI, preferred_element_type=jnp.float32
        )
        result.append(x + mm3(x, right(residual)))
    return result


def side_kernel(fac_ref, gtr_ref, out_ref):
    ki = fac_ref.shape[1]
    half = ki // 2
    top = fac_ref[:half, :]
    low = fac_ref[half:ki, :]
    c_in = jnp.concatenate(
        [top, jnp.concatenate([top[:, half:].T, low[:, :half]], axis=1)], axis=0
    )
    c_out = low[:, half:]
    count = c_out[1:2, :1]
    c_out = with_corner(c_out, c_out[:1, 1:2])
    inv_in, inv_out = inverses([c_in, wide(c_out, half)])
    side = mm3(mm3(inv_in, right(gtr_ref[...])), right(inv_out)) * (count * count)
    out_ref[:, :half] = side[:half, :half]
    out_ref[:, half:] = side[half:, :half]


def scores_kernel(order, n_blk, side_ref, gte_ref, out_ref):
    z = lax.axis_index("dp")
    b = lax.axis_index("blk")
    lane = lax.broadcasted_iota(jnp.int32, out_ref.shape, 1)
    row = jnp.zeros(out_ref.shape, jnp.float32)
    side = side_ref[...]
    sums = [jnp.sum(side * gte_ref[p], axis=0, keepdims=True) for p in range(len(order))]
    values = jnp.sum(jnp.concatenate(sums, axis=0), axis=1, keepdims=True)
    for p, (dz, db) in enumerate(order):
        row = jnp.where(lane == (z ^ dz) * n_blk + (b ^ db), values[p : p + 1, :], row)
    out_ref[...] = row


def project(xs, w_in, w_out, n_groups, n_dp, n_blk):
    tokens, width = xs[0].shape
    rin, rout = w_in.shape[0], w_out.shape[0]
    ki, ko = rin * n_dp, rout * n_dp
    out_shape = jax.ShapeDtypeStruct((3 * tokens, ki), jnp.float32)
    if (n_groups, n_dp, n_blk) != (2, 4, 2):
        w_in = lax.all_gather(w_in, "dp", axis=0, tiled=True)
        w_out = lax.all_gather(w_out, "dp", axis=0, tiled=True)
        return call(project_kernel, out_shape, [vmem()] * 6, (*xs, w_in, w_out))

    part = width // 8
    shard = rin + rout
    q = lax.axis_index(PLANE)
    whole = jnp.concatenate([w_in, w_out], axis=0)
    mine = lax.dynamic_slice(whole, (0, q * 2 * part), (shard, 2 * part))
    opposite = lax.dynamic_slice(whole, (0, (q ^ 3) * 2 * part), (shard, 2 * part))
    operands = (*xs, w_in, w_out)
    *xs, w_in, w_out = call(
        functools.partial(load_kernel, 6),
        tuple(pltpu.VMEM(x.shape, x.dtype) for x in operands),
        [pl.BlockSpec(memory_space=pltpu.HBM)] * 6,
        [pltpu.with_memory_space_constraint(x, pltpu.HBM) for x in operands],
        flops=1 << 30,
        scratch_shapes=[pltpu.SemaphoreType.DMA((12,))],
    )
    halves = [mine[:, :part], mine[:, part:]]
    far = [swap(h, "dp", n_dp, 2) for h in halves]
    far_op = swap(opposite, "dp", n_dp, 2)
    both_a = stack((halves[0], far[0]))
    near_a = swap(both_a, "dp", n_dp, 1)
    both_b = stack((halves[1], far[1]))
    near_b = swap(both_b, "dp", n_dp, 1)
    za = stack((far[0], near_a))
    along_x, along_y = (0, 1), (1, 0)
    xa = mixed(za, PLANE, (n_groups, n_blk), along_x, along_y)
    ya = mixed(za, PLANE, (n_groups, n_blk), along_y, along_x)
    both_op = stack((opposite, far_op))
    near_op = swap(both_op, "dp", n_dp, 1)
    zb = stack((far[1], near_b))
    xb = mixed(zb, PLANE, (n_groups, n_blk), along_x, along_y)
    yb = mixed(zb, PLANE, (n_groups, n_blk), along_y, along_x)

    def accumulate(plan, pieces, acc):
        args = (*xs, w_in, w_out, *pieces) + (() if acc is None else (acc,))
        total = sum(width for _, _, width, _ in plan)
        return call(
            functools.partial(project_pieces_kernel, plan, acc is not None, len(pieces)),
            out_shape,
            [vmem()] * len(args),
            args,
            flops=1 << 28,
            scratch_shapes=[
                pltpu.VMEM((ki, total), jnp.bfloat16),
                pltpu.VMEM((ko, total), jnp.bfloat16),
            ],
        )

    def stacked(p):
        return tuple((p, i * shard, k) for i, k in enumerate((2, 1, 3)))

    acc = accumulate(
        ((0, 0, part, stacked(0)), (0, part, part, stacked(1))), (za, zb), None)
    acc = accumulate(
        ((1, 0, part, stacked(0)), (2, 0, part, stacked(1))), (xa, ya), acc)
    return accumulate(
        (
            (1, part, part, stacked(0)),
            (2, part, part, stacked(1)),
            (3, 0, 2 * part, ((2, 0, 2), (3, 0, 1), (3, shard, 3))),
        ),
        (xb, yb, far_op, near_op),
        acc,
    )


def per_device(
    n_groups, n_dp, n_blk, train_inputs, train_cotangents, train_lengths,
    test_inputs, test_cotangents, test_lengths, proj_in, proj_out,
):
    _, tokens, width = train_inputs.shape
    xs = [a.reshape(tokens, width) for a in (
        train_inputs, train_cotangents, test_inputs, test_cotangents)]
    part = project(xs, proj_in.T, proj_out.T, n_groups, n_dp, n_blk)
    ki = part.shape[1]
    ko = ki // 2
    other = swap(part, "mp", 2, 1)
    fac, gte, gtr = call(
        moments_kernel,
        (
            jax.ShapeDtypeStruct((ki, ki), jnp.float32),
            jax.ShapeDtypeStruct((1, ki // 2, ki), jnp.float32),
            jax.ShapeDtypeStruct((ki, ko), jnp.float32),
        ),
        [smem(), smem(), vmem(), vmem()],
        (train_lengths, test_lengths, part, other),
    )
    order = [(0, 0)]
    for axis, count in (("dp", n_dp), ("blk", n_blk)):
        for k in bits(count):
            gte = jnp.concatenate([gte, swap(gte, axis, count, k)], axis=0)
            order += [(dz ^ k, db) if axis == "dp" else (dz, db ^ k) for dz, db in order]
    steps_z = [(k, 0) for k in bits(n_dp)]
    steps_x = [(0, k) for k in bits(n_blk)]
    first = steps_x + steps_z[::-1]
    second = steps_z[:1] + steps_x + steps_z[1:]
    for step0, step1 in zip(first, second):
        fac = fac + mixed(fac, ("dp", "blk"), (n_dp, n_blk), step0, step1)
    side = call(
        side_kernel,
        jax.ShapeDtypeStruct((ki // 2, ki), jnp.float32),
        [vmem()] * 2,
        (fac, gtr),
        flops=4 << 30,
    )
    return call(
        functools.partial(scores_kernel, order, n_blk),
        jax.ShapeDtypeStruct((1, n_dp * n_blk), jnp.float32),
        [vmem()] * 2,
        (side, gte),
    )


def solution(mesh):
    feature = P(("groups", "dp", "blk"), None, "mp")
    length = P(("groups", "dp", "blk"))
    weight = P("mp", "dp")
    shape = mesh.shape
    return jax.shard_map(
        functools.partial(per_device, shape["groups"], shape["dp"], shape["blk"]),
        mesh=mesh,
        in_specs=(feature, feature, length, feature, feature, length, weight, weight),
        out_specs=P(("groups", "dp", "blk"), None),
        check_vma=False,
    )
```

```python
import functools

import jax
import jax.numpy as jnp
from jax import lax
from jax.experimental import pallas as pl
from jax.experimental.pallas import tpu as pltpu
from jax.sharding import PartitionSpec as P

HI = lax.Precision.HIGHEST
NT = (((1,), (1,)), ((), ()))
TN = (((0,), (0,)), ((), ()))
NEWTON_STEPS = 7
PLANE = ("groups", "blk")
LANES = 128


def vmem():
    return pl.BlockSpec(memory_space=pltpu.VMEM)


def smem():
    return pl.BlockSpec(memory_space=pltpu.SMEM)


def call(kernel, out_shape, in_specs, args, flops=0, limit=16, **kw):
    return pl.pallas_call(
        kernel,
        out_shape=out_shape,
        in_specs=in_specs,
        out_specs=jax.tree.map(lambda _: vmem(), out_shape),
        compiler_params=pltpu.CompilerParams(vmem_limit_bytes=limit * 1024 * 1024),
        cost_estimate=pl.CostEstimate(flops=flops, bytes_accessed=1 << 16, transcendentals=0),
        **kw,
    )(*args)


def swap(x, axis, count, k):
    return lax.ppermute(x, axis, [(i, i ^ k) for i in range(count)])


def mixed(x, axes, counts, step0, step1):
    pairs = []
    for i in range(counts[0]):
        for j in range(counts[1]):
            for core, (di, dj) in enumerate((step0, step1)):
                pairs.append((
                    (i * counts[1] + j) * 2 + core,
                    ((i ^ di) * counts[1] + (j ^ dj)) * 2 + core,
                ))
    return lax.ppermute(x, (*axes, "mp"), pairs)


def bits(count):
    return [1 << s for s in reversed(range(count.bit_length() - 1))]


def load_kernel(n, *refs):
    srcs, dsts, sem = refs[:n], refs[n : 2 * n], refs[2 * n]
    copies = []
    for i, (src, dst) in enumerate(zip(srcs, dsts)):
        rows = src.shape[0] // 2
        for h in range(2):
            part = pl.ds(h * rows, rows)
            copies.append(pltpu.make_async_copy(src.at[part], dst.at[part], sem.at[2 * i + h]))
    for c in copies:
        c.start()
    for c in copies:
        c.wait()


def stack_kernel(n, *refs):
    at = 0
    for src in refs[:n]:
        refs[-1][at : at + src.shape[0], :] = src[...]
        at += src.shape[0]


def stack(parts, after=None):
    rows = sum(p.shape[0] for p in parts)
    extra = () if after is None else (after,)
    return call(
        functools.partial(stack_kernel, len(parts)),
        pltpu.VMEM((rows, parts[0].shape[1]), parts[0].dtype),
        [vmem()] * len(parts) + [pl.BlockSpec(memory_space=pl.ANY)] * len(extra),
        (*parts, *extra),
        limit=1,
    )


def store_products(x_parts, g_parts, acc_ref, out_ref):
    tokens = out_ref.shape[0] // 3
    ko = g_parts[0].shape[1]
    for n in range(2):
        rows = slice(n * tokens, (n + 1) * tokens)
        prior = 0.0 if acc_ref is None else acc_ref[rows, :]
        out_ref[rows, :] = prior + x_parts[n]
    rows = slice(2 * tokens, 3 * tokens)
    for n in range(2):
        cols = slice(n * ko, (n + 1) * ko)
        prior = 0.0 if acc_ref is None else acc_ref[rows, cols]
        out_ref[rows, cols] = prior + g_parts[n]


def nt(a, b):
    return lax.dot_general(a, b, NT, preferred_element_type=jnp.float32)


def project_kernel(*refs):
    x_refs, (w_in, w_out, out_ref) = refs[:4], refs[4:]
    xs = [nt(x_refs[n][...], w_in[...]) for n in (0, 2)]
    gs = [nt(x_refs[n][...], w_out[...]) for n in (1, 3)]
    store_products(xs, gs, None, out_ref)


def project_pieces_kernel(plan, with_acc, n_pieces, *refs):
    x_refs, (own_in, own_out) = refs[:4], refs[4:6]
    pieces = refs[6 : 6 + n_pieces]
    acc_ref = refs[6 + n_pieces] if with_acc else None
    out_ref, w_in, w_out = refs[6 + n_pieces + with_acc :]
    z = lax.axis_index("dp")
    q = lax.axis_index(PLANE)
    core = lax.axis_index("mp")
    rin, rout = own_in.shape[0], own_out.shape[0]
    quarter = own_in.shape[1] // 4
    xs, gs = [0.0, 0.0], [0.0, 0.0]
    at = 0
    for dq, col, width, rows in plan:
        other = q ^ (core * (3 ^ dq) + (1 - core) * dq) if dq in (1, 2) else q ^ dq
        start = pl.multiple_of(other * quarter + col, 128)
        cols = pl.ds(start, width)
        here = slice(at, at + width)
        at += width
        w_in[pl.ds(pl.multiple_of(z * rin, rin), rin), here] = own_in[:, cols]
        w_out[pl.ds(pl.multiple_of(z * rout, rout), rout), here] = own_out[:, cols]
        for p, row, k in rows:
            dst_in = pl.multiple_of((z ^ k) * rin, rin)
            dst_out = pl.multiple_of((z ^ k) * rout, rout)
            w_in[pl.ds(dst_in, rin), here] = pieces[p][row : row + rin, :]
            w_out[pl.ds(dst_out, rout), here] = pieces[p][row + rin : row + rin + rout, :]
        for m in range(2):
            xs[m] += nt(x_refs[2 * m][:, cols], w_in[:, here])
            gs[m] += nt(x_refs[2 * m + 1][:, cols], w_out[:, here])
    store_products(xs, gs, acc_ref, out_ref)


def with_corner(x, value):
    row = lax.broadcasted_iota(jnp.int32, x.shape, 0)
    col = lax.broadcasted_iota(jnp.int32, x.shape, 1)
    return jnp.where((row == 1) & (col == 0), value, x)


def moments_kernel(len_tr, len_te, mine, other, fac_ref, gte_ref, gtr_ref):
    tokens = mine.shape[0] // 3
    ki = mine.shape[1]
    ko = ki // 2
    total = mine[...] + other[...]
    rows = lax.broadcasted_iota(jnp.int32, (tokens, ki), 0)
    n_tr, n_te = len_tr[0], len_te[0]
    x_tr = jnp.where(rows < n_tr, total[:tokens], 0.0)
    x_te = jnp.where(rows < n_te, total[tokens : 2 * tokens], 0.0)
    g_both = total[2 * tokens :]
    g_tr = jnp.where(rows < n_tr, g_both, 0.0)[:, :ko]
    g_te = g_both[:, ko:]
    dot = functools.partial(
        lax.dot_general, dimension_numbers=TN, precision=HI,
        preferred_element_type=jnp.float32,
    )
    products = jnp.dot(
        x_tr.T, jnp.concatenate([x_tr, g_tr], axis=1), precision=HI,
        preferred_element_type=jnp.float32,
    )
    c_in = products[:, :ki]
    c_out = with_corner(dot(g_tr, g_tr), n_tr.astype(jnp.float32))
    half = ki // 2
    fac_ref[:half, :] = c_in[:half, :]
    fac_ref[half:ki, :half] = c_in[half:, half:]
    fac_ref[half:ki, half:] = c_out
    grad_tr = products[:, ki:] / n_tr.astype(jnp.float32)
    grad_te = dot(x_te, g_te) / n_te.astype(jnp.float32)
    gtr_ref[...] = grad_tr
    gte_ref[0, :, :ko] = grad_te[:half]
    gte_ref[0, :, ko:] = grad_te[half:]


def wide(x, rows, cols=LANES):
    if x.shape[1] < cols:
        x = jnp.concatenate([x, jnp.zeros((x.shape[0], cols - x.shape[1]), x.dtype)], axis=1)
    if x.shape[0] < rows:
        x = jnp.concatenate([x, jnp.zeros((rows - x.shape[0], cols), x.dtype)], axis=0)
    return x


def parts(x):
    high = x.astype(jnp.bfloat16)
    return high, (x - high.astype(jnp.float32)).astype(jnp.bfloat16)


def right(x):
    high, low = parts(wide(x, LANES))
    upper = jnp.concatenate([high, low], axis=1)
    lower = jnp.concatenate([jnp.zeros_like(high), high], axis=1)
    return jnp.concatenate([upper, lower], axis=0)


def mm3(x, packed):
    both = jnp.dot(
        jnp.concatenate(parts(x), axis=1), packed, preferred_element_type=jnp.float32
    )
    return both[:, :LANES] + both[:, LANES:]


def damped(c):
    n = c.shape[0]
    i = lax.broadcasted_iota(jnp.int32, c.shape, 0)
    j = lax.broadcasted_iota(jnp.int32, c.shape, 1)
    eye = (i == j).astype(jnp.float32)
    trace = jnp.sum(jnp.sum(c * eye, axis=0, keepdims=True), axis=1, keepdims=True)
    low = 0.1 * trace / n
    a = c + low * eye
    high = jnp.max(jnp.sum(jnp.abs(a), axis=0, keepdims=True), axis=1, keepdims=True)
    return a, eye, low, jnp.minimum(high, trace + low)


def inverses(matrices):
    state = []
    for c in matrices:
        a, eye, low, high = damped(c)
        scale = 2.0 / (low + high)
        r = (high - low) / (high + low)
        state.append((a, eye, scale * a, scale * eye, scale, r))
    for step in range(NEWTON_STEPS):
        nxt = []
        for a, eye, m, x, scale, r in state:
            s = 2.0 / (2.0 - r * r)
            n = m.shape[0]
            if step == 0:
                mx = s * (2.0 * m - mm3(m, right(m)))
                xx = s * (2.0 * x - scale * m)
            else:
                both = mm3(jnp.concatenate([m, x], axis=0), right(m))
                mx = s * (2.0 * m - both[:n])
                xx = s * (2.0 * x - both[n:])
            nxt.append((a, eye, mx, xx, scale, r * r / (2.0 - r * r)))
        state = nxt
    result = []
    for a, eye, m, x, scale, r in state:
        n = a.shape[0]
        residual = eye - jnp.dot(
            a[:, :n], x, precision=HI, preferred_element_type=jnp.float32
        )
        result.append(x + mm3(x, right(residual)))
    return result


def side_kernel(fac_ref, gtr_ref, out_ref):
    ki = fac_ref.shape[1]
    half = ki // 2
    top = fac_ref[:half, :]
    low = fac_ref[half:ki, :]
    c_in = jnp.concatenate(
        [top, jnp.concatenate([top[:, half:].T, low[:, :half]], axis=1)], axis=0
    )
    c_out = low[:, half:]
    count = c_out[1:2, :1]
    c_out = with_corner(c_out, c_out[:1, 1:2])
    inv_in, inv_out = inverses([c_in, wide(c_out, half)])
    side = mm3(mm3(inv_in, right(gtr_ref[...])), right(inv_out)) * (count * count)
    out_ref[:, :half] = side[:half, :half]
    out_ref[:, half:] = side[half:, :half]


def scores_kernel(order, n_blk, side_ref, gte_ref, out_ref):
    z = lax.axis_index("dp")
    b = lax.axis_index("blk")
    lane = lax.broadcasted_iota(jnp.int32, out_ref.shape, 1)
    row = jnp.zeros(out_ref.shape, jnp.float32)
    side = side_ref[...]
    sums = [jnp.sum(side * gte_ref[p], axis=0, keepdims=True) for p in range(len(order))]
    values = jnp.sum(jnp.concatenate(sums, axis=0), axis=1, keepdims=True)
    for p, (dz, db) in enumerate(order):
        row = jnp.where(lane == (z ^ dz) * n_blk + (b ^ db), values[p : p + 1, :], row)
    out_ref[...] = row


def project(xs, w_in, w_out, n_groups, n_dp, n_blk):
    tokens, width = xs[0].shape
    rin, rout = w_in.shape[0], w_out.shape[0]
    ki, ko = rin * n_dp, rout * n_dp
    out_shape = jax.ShapeDtypeStruct((3 * tokens, ki), jnp.float32)
    if (n_groups, n_dp, n_blk) != (2, 4, 2):
        w_in = lax.all_gather(w_in, "dp", axis=0, tiled=True)
        w_out = lax.all_gather(w_out, "dp", axis=0, tiled=True)
        return call(project_kernel, out_shape, [vmem()] * 6, (*xs, w_in, w_out))

    part = width // 8
    shard = rin + rout
    q = lax.axis_index(PLANE)
    whole = jnp.concatenate([w_in, w_out], axis=0)
    mine = lax.dynamic_slice(whole, (0, q * 2 * part), (shard, 2 * part))
    opposite = lax.dynamic_slice(whole, (0, (q ^ 3) * 2 * part), (shard, 2 * part))
    operands = (*xs, w_in, w_out)
    *xs, w_in, w_out = call(
        functools.partial(load_kernel, 6),
        tuple(pltpu.VMEM(x.shape, x.dtype) for x in operands),
        [pl.BlockSpec(memory_space=pltpu.HBM)] * 6,
        [pltpu.with_memory_space_constraint(x, pltpu.HBM) for x in operands],
        flops=1 << 30,
        scratch_shapes=[pltpu.SemaphoreType.DMA((12,))],
    )
    halves = [mine[:, :part], mine[:, part:]]
    far = [swap(h, "dp", n_dp, 2) for h in halves]
    far_op = swap(opposite, "dp", n_dp, 2)
    both_a = stack((halves[0], far[0]))
    near_a = swap(both_a, "dp", n_dp, 1)
    both_b = stack((halves[1], far[1]))
    near_b = swap(both_b, "dp", n_dp, 1)
    za = stack((far[0], near_a))
    along_x, along_y = (0, 1), (1, 0)
    xa = mixed(za, PLANE, (n_groups, n_blk), along_x, along_y)
    ya = mixed(za, PLANE, (n_groups, n_blk), along_y, along_x)
    both_op = stack((opposite, far_op))
    near_op = swap(both_op, "dp", n_dp, 1)
    zb = stack((far[1], near_b))
    xb = mixed(zb, PLANE, (n_groups, n_blk), along_x, along_y)
    yb = mixed(zb, PLANE, (n_groups, n_blk), along_y, along_x)

    def accumulate(plan, pieces, acc):
        args = (*xs, w_in, w_out, *pieces) + (() if acc is None else (acc,))
        total = sum(width for _, _, width, _ in plan)
        return call(
            functools.partial(project_pieces_kernel, plan, acc is not None, len(pieces)),
            out_shape,
            [vmem()] * len(args),
            args,
            flops=1 << 28,
            scratch_shapes=[
                pltpu.VMEM((ki, total), jnp.bfloat16),
                pltpu.VMEM((ko, total), jnp.bfloat16),
            ],
        )

    def stacked(p):
        return tuple((p, i * shard, k) for i, k in enumerate((2, 1, 3)))

    acc = accumulate(
        (
            (0, 0, part, stacked(0)),
            (0, part, part, stacked(1)),
            (1, 0, part, stacked(2)),
            (2, 0, part, stacked(3)),
        ),
        (za, zb, xa, ya),
        None,
    )
    return accumulate(
        (
            (1, part, part, stacked(0)),
            (2, part, part, stacked(1)),
            (3, 0, 2 * part, ((2, 0, 2), (3, 0, 1), (3, shard, 3))),
        ),
        (xb, yb, far_op, near_op),
        acc,
    )


def per_device(
    n_groups, n_dp, n_blk, train_inputs, train_cotangents, train_lengths,
    test_inputs, test_cotangents, test_lengths, proj_in, proj_out,
):
    _, tokens, width = train_inputs.shape
    xs = [a.reshape(tokens, width) for a in (
        train_inputs, train_cotangents, test_inputs, test_cotangents)]
    part = project(xs, proj_in.T, proj_out.T, n_groups, n_dp, n_blk)
    ki = part.shape[1]
    ko = ki // 2
    other = swap(part, "mp", 2, 1)
    fac, gte, gtr = call(
        moments_kernel,
        (
            jax.ShapeDtypeStruct((ki, ki), jnp.float32),
            jax.ShapeDtypeStruct((1, ki // 2, ki), jnp.float32),
            jax.ShapeDtypeStruct((ki, ko), jnp.float32),
        ),
        [smem(), smem(), vmem(), vmem()],
        (train_lengths, test_lengths, part, other),
    )
    order = [(0, 0)]
    for axis, count in (("dp", n_dp), ("blk", n_blk)):
        for k in bits(count):
            gte = jnp.concatenate([gte, swap(gte, axis, count, k)], axis=0)
            order += [(dz ^ k, db) if axis == "dp" else (dz, db ^ k) for dz, db in order]
    steps_z = [(k, 0) for k in bits(n_dp)]
    steps_x = [(0, k) for k in bits(n_blk)]
    first = steps_x + steps_z[::-1]
    second = steps_z[:1] + steps_x + steps_z[1:]
    for step0, step1 in zip(first, second):
        fac = fac + mixed(fac, ("dp", "blk"), (n_dp, n_blk), step0, step1)
    side = call(
        side_kernel,
        jax.ShapeDtypeStruct((ki // 2, ki), jnp.float32),
        [vmem()] * 2,
        (fac, gtr),
        flops=4 << 30,
    )
    return call(
        functools.partial(scores_kernel, order, n_blk),
        jax.ShapeDtypeStruct((1, n_dp * n_blk), jnp.float32),
        [vmem()] * 2,
        (side, gte),
    )


def solution(mesh):
    feature = P(("groups", "dp", "blk"), None, "mp")
    length = P(("groups", "dp", "blk"))
    weight = P("mp", "dp")
    shape = mesh.shape
    return jax.shard_map(
        functools.partial(per_device, shape["groups"], shape["dp"], shape["blk"]),
        mesh=mesh,
        in_specs=(feature, feature, length, feature, feature, length, weight, weight),
        out_specs=P(("groups", "dp", "blk"), None),
        check_vma=False,
    )
```
